32 devices in a mesh: dp: 2 (over y), seq: 16 (over z, x, core).
Axes of the slice: x: 2, y: 2, z: 4, core: 2. Of those that a mesh axis runs over, the one named last changes fastest.
Arguments:
- queries: bfloat16 [2, 2048, 1536], P('dp', 'seq'), may hold values from -6 to 6
- keys: bfloat16 [2, 2048, 1536], P('dp', 'seq'), may hold values from -6 to 6
- values: bfloat16 [2, 2048, 1536], P('dp', 'seq'), may hold values from -6 to 6
- segment_ids: int32 [2, 2048], P('dp'), may hold values from 0 to 31, never falling along the last dimension, each value on 1 to 128 neighbouring positions
- norm_gain: float32 [1536], replicated, may hold values from 0.25 to 1.75
- conv_kernel: float32 [31, 1536], replicated, may hold values from -1 to 1
- conv_bias: float32 [1536], replicated, may hold values from -3 to 3
- cotangent: bfloat16 [2, 2048, 1536], P('dp', 'seq'), may hold values from -6 to 6
Outputs:
- conv_out: bfloat16 [2, 2048, 1536], P('dp', 'seq')
- query_grad: bfloat16 [2, 2048, 1536], P('dp', 'seq')
- key_grad: bfloat16 [2, 2048, 1536], P('dp', 'seq')
- value_grad: bfloat16 [2, 2048, 1536], P('dp', 'seq')
- gain_grad: float32 [1536], replicated
- kernel_grad: float32 [31, 1536], replicated
- bias_grad: float32 [1536], replicated
The draws below stay inside these ranges and needn't reach their ends.
Inputs may be any that keep to these rules, and one draw needn't show every extreme that they name: `segment_ids`: within each row, utterance numbers never fall; each utterance holds 1 to 128 frames, and some utterance exactly 128.
All inputs are finite; a program needn't handle non-finite values.
Results may differ from the reference program's by a relative error of at most 0.023.
Values may be sent and summed in bfloat16 or wider, within the bound.
No kernel may reach another device: no remote copies, remote signals or barrier semaphores. Data moves between devices by JAX's collectives and lax.ppermute only.
A program may use at most 64 MiB of HBM per device.

```python
import math
import jax
import jax.numpy as jnp
import numpy as np
from jax import lax

HEADS = 24
HEAD_DIM = 64
D = 1536
KERNEL = 31
FRAMES_DEV = 128
MAX_LEN = 128
BATCH = 2
SEQLEN = 2048
SEGMENTS = 32


def paired_fields(key):
    base = jax.random.fold_in(key, 9173)
    first, second = jax.random.split(base, 2)
    shape = (BATCH, SEQLEN, HEADS, HEAD_DIM)
    query_part = jnp.clip(jax.random.normal(first, shape, jnp.float32), -6.0, 6.0)
    key_part = jnp.clip(jax.random.normal(second, shape, jnp.float32), -6.0, 6.0)
    return (query_part.reshape(BATCH, SEQLEN, HEADS * HEAD_DIM), key_part.reshape(BATCH, SEQLEN, HEADS * HEAD_DIM))


def draw_queries(key, part):
    return paired_fields(key)[0].astype(jnp.bfloat16)


def draw_keys(key, part):
    return paired_fields(key)[1].astype(jnp.bfloat16)


def steps_of(own_key, extent, pieces, smallest, high):
    def one(dim, parts):
        draws = jax.random.uniform(jax.random.fold_in(jax.random.fold_in(own_key, 6), dim), (parts,), jnp.float32, smallest / len(pieces), high / len(pieces))
        return jnp.repeat(jnp.exp(draws), extent[dim] // parts).reshape((-1,) + (1,) * (len(extent) - dim - 1))

    level = one(*pieces[0])
    for cut in pieces[1:]:
        level = level * one(*cut)
    return level


def length_profile(number_of, total, bound, skew):
    loads = [(1 << 20) // math.isqrt(rank ** skew) + 1 for rank in range(2, number_of + 1)]
    rest, counts = total - bound - (number_of - 1), [1] * (number_of - 1)
    while rest > 0:
        free = [i for i in range(number_of - 1) if counts[i] < bound]
        whole, budget = sum([loads[i] for i in free]), rest
        for i in free:
            extra = min(bound - counts[i], max(1, budget * loads[i] // whole), rest)
            counts[i] = counts[i] + extra
            rest = rest - extra
    return np.array([bound] + counts)


def ragged_sizes(own_key, amount, total, most, skew):
    if amount == 2:
        one = jax.random.randint(own_key, (), max(1, total - most), min(most, total - 1) + 1)
        return jnp.stack([one, total - one])
    sizes = jnp.asarray(length_profile(amount, total, most, skew), jnp.int32)
    couples = (amount - 1) // 2
    donor, taker = sizes[1:1 + 2 * couples:2], sizes[2:2 + 2 * couples:2]
    room = jnp.minimum(donor - 1, most - taker)
    moved = jax.random.randint(jax.random.fold_in(own_key, 1), (couples,), 0, 1 << 20) % (room + 1)
    sizes = sizes.at[1:1 + 2 * couples:2].set(donor - moved).at[2:2 + 2 * couples:2].set(taker + moved)
    return sizes[jax.random.permutation(jax.random.fold_in(own_key, 2), amount)]


def scatter_about(rng, extent, scale, most, shards=(), kind=jnp.bfloat16):
    drawn = scale * jax.random.normal(rng, extent, jnp.float32)
    if shards:
        drawn = drawn * steps_of(rng, extent, shards, -0.22, 0.18)
    return jnp.clip(drawn, -most, most).astype(kind)


def setup_inputs(seed: int = 0) -> dict:
    key_list = jax.random.split(jax.random.key(seed), 9)
    return {
        "queries": draw_queries(jax.random.fold_in(key_list[8], 71), 0),
        "keys": draw_keys(jax.random.fold_in(key_list[8], 71), 0),
        "values": scatter_about(key_list[2], (BATCH, SEQLEN, D), 1.0, 6.0, ((0, 2), (1, 16))),
        "segment_ids": jax.vmap(lambda own: jnp.searchsorted(jnp.cumsum(ragged_sizes(own, SEGMENTS, SEQLEN, MAX_LEN, 1)), jnp.arange(SEQLEN), side="right"))(jax.random.split(key_list[3], BATCH)).reshape((BATCH, SEQLEN)).astype(jnp.int32),
        "norm_gain": jnp.clip(1.0 + 0.15 * jax.random.normal(key_list[4], (D,), jnp.float32), 0.25, 1.75),
        "conv_kernel": scatter_about(key_list[5], (KERNEL, D), KERNEL ** -0.5, 1.0, (), jnp.float32),
        "conv_bias": scatter_about(key_list[6], (D,), 0.5, 3.0, (), jnp.float32),
        "cotangent": scatter_about(key_list[7], (BATCH, SEQLEN, D), 1.0, 6.0, ((0, 2), (1, 16))),
    }


EPS = 1e-05
NEG = -1e+30

def masked_logits(query_rows, key_rows, same_seg):
    factor = query_rows.shape[-1] ** (-0.5)
    logits = jnp.einsum('qhe,khe->hqk', query_rows.astype(jnp.float32), key_rows.astype(jnp.float32)) * factor
    return jnp.where(same_seg[None], logits, NEG)

def forward_block(query_rows, key_rows, value_rows, same_seg):
    logits = masked_logits(query_rows, key_rows, same_seg)
    row_top = lax.optimization_barrier(jnp.max(logits, -1, keepdims=True))
    exponent = jnp.exp(logits - row_top)
    row_total = lax.optimization_barrier(jnp.sum(exponent, -1, keepdims=True))
    attn_weights = (exponent / row_total).astype(jnp.bfloat16)
    context = jnp.einsum('hqk,khe->qhe', attn_weights.astype(jnp.float32), value_rows.astype(jnp.float32))
    return (context, (row_top + jnp.log(row_total))[..., 0])

def back_terms(query_rows, key_rows, value_rows, grad_rows, log_total, row_delta, same_seg):
    factor = query_rows.shape[-1] ** (-0.5)
    logits = masked_logits(query_rows, key_rows, same_seg)
    prob_back = jnp.exp(logits - log_total[:, :, None])
    grad_prob = jnp.einsum('qhe,khe->hqk', grad_rows.astype(jnp.float32), value_rows.astype(jnp.float32))
    grad_logit = (prob_back * (grad_prob - row_delta[:, :, None]) * factor).astype(jnp.bfloat16)
    return (prob_back.astype(jnp.bfloat16), grad_logit)

def row_pass(operands, norm_gain, conv_kernel, conv_bias):
    query_row, key_row, value_row, seg_row, cot_row = operands
    length = query_row.shape[0]
    width = query_row.shape[1]
    reach_rows = MAX_LEN
    frame_count = FRAMES_DEV
    half_taps = KERNEL // 2
    block_count = length // frame_count
    seg_row = seg_row.astype(jnp.int32)
    query_heads = query_row.reshape(length, HEADS, HEAD_DIM)
    key_heads = key_row.reshape(length, HEADS, HEAD_DIM)
    value_heads = value_row.reshape(length, HEADS, HEAD_DIM)
    edge_fill = jnp.full((reach_rows,), -1, jnp.int32)
    seg_padded = jnp.concatenate([edge_fill, seg_row, edge_fill])

    def pad_rows(tensor):
        return jnp.pad(tensor, ((reach_rows, reach_rows), (0, 0), (0, 0)))
    key_padded = pad_rows(key_heads)
    value_padded = pad_rows(value_heads)
    starts = jnp.arange(block_count, dtype=jnp.int32) * frame_count
    wide_count = frame_count + 2 * reach_rows

    def forward_one(start_row):
        own_seg = lax.dynamic_slice_in_dim(seg_row, start_row, frame_count)
        wide_seg = lax.dynamic_slice_in_dim(seg_padded, start_row, wide_count)
        return forward_block(lax.dynamic_slice_in_dim(query_heads, start_row, frame_count), lax.dynamic_slice_in_dim(key_padded, start_row, wide_count), lax.dynamic_slice_in_dim(value_padded, start_row, wide_count), own_seg[:, None] == wide_seg[None, :])
    context_blocks, total_blocks = lax.map(forward_one, starts)
    context = context_blocks.reshape(length, width).astype(jnp.bfloat16)
    total_rows = total_blocks.transpose(1, 0, 2).reshape(HEADS, length)
    context_f = context.astype(jnp.float32)
    row_mean = lax.optimization_barrier(jnp.mean(context_f, -1, keepdims=True))
    centred = context_f - row_mean
    inv_std = lax.rsqrt(lax.optimization_barrier(jnp.mean(centred * centred, -1, keepdims=True)) + EPS)
    normed = centred * inv_std
    conv_in = (normed * norm_gain).astype(jnp.bfloat16)
    conv_wide = jnp.pad(conv_in.astype(jnp.float32), ((half_taps, half_taps), (0, 0)))
    conv_seg = seg_padded[reach_rows - half_taps:reach_rows + length + half_taps]
    same_taps = [(conv_seg[tap_index:tap_index + length] == seg_row)[:, None] for tap_index in range(KERNEL)]
    pre_act = jnp.broadcast_to(conv_bias, (length, width))
    for tap_index in range(KERNEL):
        pre_act = pre_act + conv_kernel[tap_index] * jnp.where(same_taps[tap_index], conv_wide[tap_index:tap_index + length], 0.0)
    gate_sig = jax.nn.sigmoid(pre_act)
    conv_out = (pre_act * gate_sig).astype(jnp.bfloat16)
    grad_pre = (cot_row.astype(jnp.float32) * gate_sig * (1.0 + pre_act * (1.0 - gate_sig))).astype(jnp.bfloat16)
    grad_pre_f = grad_pre.astype(jnp.float32)
    bias_part = lax.optimization_barrier(jnp.sum(grad_pre_f, 0))
    kernel_rows = []
    for tap_index in range(KERNEL):
        kernel_rows.append(lax.optimization_barrier(jnp.sum(jnp.where(same_taps[tap_index], conv_wide[tap_index:tap_index + length] * grad_pre_f, 0.0), 0)))
    kernel_part = jnp.stack(kernel_rows, 0)
    grad_wide = jnp.pad(grad_pre_f, ((half_taps, half_taps), (0, 0)))
    grad_in = jnp.zeros((length, width), jnp.float32)
    for tap_index in range(KERNEL):
        mirror = 2 * half_taps - tap_index
        grad_in = grad_in + conv_kernel[tap_index] * jnp.where(same_taps[mirror], grad_wide[mirror:mirror + length], 0.0)
    gain_part = lax.optimization_barrier(jnp.sum(grad_in * normed, 0))
    grad_norm = grad_in * norm_gain
    grad_context = ((grad_norm - lax.optimization_barrier(jnp.mean(grad_norm, -1, keepdims=True)) - normed * lax.optimization_barrier(jnp.mean(grad_norm * normed, -1, keepdims=True))) * inv_std).astype(jnp.bfloat16)
    row_delta = lax.optimization_barrier(jnp.sum((grad_context.astype(jnp.float32) * context_f).reshape(length, HEADS, HEAD_DIM), -1)).T
    grad_heads = grad_context.reshape(length, HEADS, HEAD_DIM)

    def query_one(start_row):
        own_seg = lax.dynamic_slice_in_dim(seg_row, start_row, frame_count)
        wide_seg = lax.dynamic_slice_in_dim(seg_padded, start_row, wide_count)
        key_rows = lax.dynamic_slice_in_dim(key_padded, start_row, wide_count)
        prob_low, grad_logit = back_terms(lax.dynamic_slice_in_dim(query_heads, start_row, frame_count), key_rows, lax.dynamic_slice_in_dim(value_padded, start_row, wide_count), lax.dynamic_slice_in_dim(grad_heads, start_row, frame_count), lax.dynamic_slice_in_dim(total_rows, start_row, frame_count, 1), lax.dynamic_slice_in_dim(row_delta, start_row, frame_count, 1), own_seg[:, None] == wide_seg[None, :])
        return jnp.einsum('hqk,khe->qhe', grad_logit.astype(jnp.float32), key_rows.astype(jnp.float32))
    query_grad = lax.map(query_one, starts).reshape(length, width).astype(jnp.bfloat16)
    query_padded = pad_rows(query_heads)
    grad_padded = pad_rows(grad_heads)
    total_padded = jnp.pad(total_rows, ((0, 0), (reach_rows, reach_rows)))
    delta_padded = jnp.pad(row_delta, ((0, 0), (reach_rows, reach_rows)))

    def key_one(start_row):
        own_seg = lax.dynamic_slice_in_dim(seg_row, start_row, frame_count)
        wide_seg = lax.dynamic_slice_in_dim(seg_padded, start_row, wide_count)
        query_rows = lax.dynamic_slice_in_dim(query_padded, start_row, wide_count)
        grad_rows = lax.dynamic_slice_in_dim(grad_padded, start_row, wide_count)
        prob_low, grad_logit = back_terms(query_rows, lax.dynamic_slice_in_dim(key_heads, start_row, frame_count), lax.dynamic_slice_in_dim(value_heads, start_row, frame_count), grad_rows, lax.dynamic_slice_in_dim(total_padded, start_row, wide_count, 1), lax.dynamic_slice_in_dim(delta_padded, start_row, wide_count, 1), wide_seg[:, None] == own_seg[None, :])
        key_part = jnp.einsum('hqk,qhe->khe', grad_logit.astype(jnp.float32), query_rows.astype(jnp.float32))
        value_part = jnp.einsum('hqk,qhe->khe', prob_low.astype(jnp.float32), grad_rows.astype(jnp.float32))
        return (key_part, value_part)
    key_blocks, value_blocks = lax.map(key_one, starts)
    key_grad = key_blocks.reshape(length, width).astype(jnp.bfloat16)
    value_grad = value_blocks.reshape(length, width).astype(jnp.bfloat16)
    return (conv_out, query_grad, key_grad, value_grad, gain_part, kernel_part, bias_part)

def reference(queries, keys, values, segment_ids, norm_gain, conv_kernel, conv_bias, cotangent):

    def one_row(operands):
        return row_pass(operands, norm_gain, conv_kernel, conv_bias)
    results = lax.map(one_row, (queries, keys, values, segment_ids, cotangent))
    conv_out, query_grad, key_grad, value_grad, gain_rows, kernel_rows, bias_rows = results
    norm_factor = (BATCH * SEQLEN) ** (-0.5)
    return (conv_out, query_grad, key_grad, value_grad, lax.optimization_barrier(jnp.sum(gain_rows, 0)) * norm_factor, lax.optimization_barrier(jnp.sum(kernel_rows, 0)) * norm_factor, lax.optimization_barrier(jnp.sum(bias_rows, 0)) * norm_factor)
```

```python
import functools

import jax
import jax.numpy as jnp
from jax import lax
from jax.experimental import pallas as pl
from jax.experimental.pallas import tpu as pltpu
from jax.sharding import PartitionSpec as P

HEAD_DIM = 64
EPS = 1e-05
NEG = -1e30
LANES = 128
PAD = 16
GROUPS = 3
VMEM = pl.BlockSpec(memory_space=pltpu.VMEM)
F32 = jnp.float32
BF16 = jnp.bfloat16


def dot(a, b, dims):
    return lax.dot_general(a, b, (dims, ((), ())), preferred_element_type=F32)


NN = ((1,), (0,))
NT = ((1,), (1,))
TN = ((0,), (0,))


def lanes_of(index):
    return pl.ds(pl.multiple_of(index * LANES, LANES), LANES)


def block_ids(seg_ref, frames):
    me = lax.axis_index("seq")
    count = seg_ref.shape[1] // frames
    own = seg_ref[0:1, pl.ds(pl.multiple_of(me * frames, frames), frames)].astype(F32)
    before = jnp.maximum(me - 1, 0)
    after = jnp.minimum(me + 1, count - 1)
    prev = seg_ref[0:1, pl.ds(pl.multiple_of(before * frames, frames), frames)].astype(F32)
    following = seg_ref[0:1, pl.ds(pl.multiple_of(after * frames, frames), frames)].astype(F32)
    prev_last = jnp.where(me > 0, prev[:, frames - 1 :], -1.0)
    following = jnp.where(me < count - 1, following, -1.0)
    return own, following, prev_last, following[:, 0:1]


def crossing(seg_ref, frames):
    own, following, _, edge = block_ids(seg_ref, frames)
    left = jnp.sum(jnp.where((own == edge) & (edge >= 0.0), 1.0, 0.0), 1, keepdims=True)
    right = jnp.sum(jnp.where(following == edge, 1.0, 0.0), 1, keepdims=True)
    length = jnp.where(left > 0.0, left + right, 0.0)
    return frames - left, length


def iota(shape, axis):
    return lax.broadcasted_iota(jnp.int32, shape, axis).astype(F32)


def gather_matrix(first, length, frames):
    shape = (frames, 2 * frames)
    row = iota(shape, 0)
    return jnp.where((iota(shape, 1) == row + first) & (row < length), 1.0, 0.0).astype(BF16)


def scatter_matrix(first, length, frames):
    shape = (2 * frames, frames)
    col = iota(shape, 1)
    return jnp.where((iota(shape, 0) == col + first) & (col < length), 1.0, 0.0).astype(BF16)


def pair_masks(rows):
    low = lax.broadcasted_iota(jnp.int32, (rows, LANES), 1) < HEAD_DIM
    return low


def stack_pair(pair, low):
    zero = jnp.zeros_like(pair)
    return jnp.concatenate([jnp.where(low, pair, zero), jnp.where(low, zero, pair)], 0)


def attend(query, key, value, bias, keep, low):
    frames = query.shape[0]
    logits = dot(query * jnp.asarray(HEAD_DIM**-0.5, BF16), stack_pair(key, low), NT)
    halves = []
    for half in range(2):
        part = logits[:, half * frames : (half + 1) * frames] + bias
        top = jnp.max(part, 1, keepdims=True)
        power = jnp.exp(part - top)
        total = jnp.sum(power, 1, keepdims=True)
        halves.append((power * (1.0 / total)).astype(BF16))
    prob = jnp.concatenate(halves, 1)
    context = dot(prob, stack_pair(value, low), NN)
    return prob, (context * keep).astype(BF16)


def attend_back(query, key, value, prob, context, grad, low):
    frames = query.shape[0]
    scale = HEAD_DIM**-0.5
    grad_prob = dot(grad, stack_pair(value, low), NT)
    product = grad.astype(F32) * context.astype(F32)
    zero = jnp.zeros_like(product)
    deltas = (
        jnp.sum(jnp.where(low, product, zero), 1, keepdims=True),
        jnp.sum(jnp.where(low, zero, product), 1, keepdims=True),
    )
    parts = []
    for half in range(2):
        cols = slice(half * frames, (half + 1) * frames)
        parts.append(
            (prob[:, cols].astype(F32) * (grad_prob[:, cols] - deltas[half]) * scale).astype(BF16)
        )
    query_grad = dot(jnp.concatenate(parts, 1), stack_pair(key, low), NN)
    key_grad = dot(jnp.concatenate(parts, 0), stack_pair(query, low), TN)
    prob_rows = jnp.concatenate([prob[:, :frames], prob[:, frames:]], 0)
    value_grad = dot(prob_rows, stack_pair(grad, low), TN)
    return query_grad, key_grad, value_grad


def normalize(context):
    context = context.astype(F32)
    centred = context - jnp.mean(context, -1, keepdims=True)
    inv_std = lax.rsqrt(jnp.mean(centred * centred, -1, keepdims=True) + EPS)
    return centred * inv_std, inv_std


CHUNK = 32


def chunks(frames):
    return [pl.ds(start, CHUNK) for start in range(0, frames, CHUNK)]


def clear_edges(pad_ref, frames):
    zero = jnp.zeros((PAD, pad_ref.shape[1]), F32)
    pad_ref[0:PAD, :] = zero
    pad_ref[PAD + frames : 2 * PAD + frames, :] = zero


def shifts(frames, taps):
    base = PAD - taps // 2
    for turn in range(8):
        for start in range(0, 2 * PAD + 1, 8):
            tap = start + turn - base
            if 0 <= tap < taps:
                yield turn, start, tap


def turned(block, turn):
    rows = block.shape[0]
    return block if turn == 0 else pltpu.roll(block, rows - turn, 0)


def conv_forward(pad_ref, kernel_ref, bias_ref, mask_ref, frames, lanes):
    taps = kernel_ref.shape[0]
    block = pad_ref[:, lanes]
    total = jnp.broadcast_to(bias_ref[0:1, lanes], (frames, LANES))
    at, view = None, None
    for turn, start, tap in shifts(frames, taps):
        if turn != at:
            at, view = turn, turned(block, turn)
        term = view[start : start + frames]
        if mask_ref is not None:
            term = term * mask_ref[tap * frames : (tap + 1) * frames, :]
        total = total + kernel_ref[tap : tap + 1, lanes] * term
    return total


def conv_backward(pad_ref, conv_in, kernel_ref, mask_ref, frames, lanes, store):
    taps = kernel_ref.shape[0]
    block = pad_ref[:, lanes]
    total = jnp.zeros((frames, LANES), F32)
    at, view = None, None
    for turn, start, mirror in shifts(frames, taps):
        if turn != at:
            at, view = turn, turned(block, turn)
        tap = taps - 1 - mirror
        term = view[start : start + frames]
        if mask_ref is not None:
            term = term * mask_ref[mirror * frames : (mirror + 1) * frames, :]
        total = total + kernel_ref[tap : tap + 1, lanes] * term
        store(tap, jnp.sum(conv_in * term, 0, keepdims=True))
    return total


def gate(pre_act):
    return 1.0 / (1.0 + jnp.exp(-pre_act))


def gate_grad(cotangent, pre_act, sig):
    return (cotangent * sig * (1.0 + pre_act * (1.0 - sig))).astype(BF16).astype(F32)


def norm_backward(context_ref, grad_ref, gain_ref, keep, out_ref, frames):
    for rows in chunks(frames):
        normed, inv_std = normalize(context_ref[rows, :])
        grad = grad_ref[rows, :] * gain_ref[0:1, :]
        centre = jnp.mean(grad, -1, keepdims=True)
        slope = jnp.mean(grad * normed, -1, keepdims=True)
        result = (grad - centre - normed * slope) * inv_std
        out_ref[rows, :] = jnp.where(keep[rows.start : rows.start + CHUNK, 0:1] > 0.0, result, 0.0).astype(BF16)


def own_kernel(
    q_ref, k_ref, v_ref, cot_ref, seg_ref, gain_ref, kernel_ref, bias_ref,
    out_ref, grad_ref, prob_ref, context_ref, sums_ref,
    pad_ref, normed_ref, pre_ref, mask_ref, keep_ref,
):
    frames, width = q_ref.shape
    taps = kernel_ref.shape[0]
    tiles = width // LANES
    own, _, prev_last, next_first = block_ids(seg_ref, frames)
    ids = jnp.where((own == prev_last) | (own == next_first), -5.0, own)
    ids_row = jnp.broadcast_to(ids, (frames, frames))
    ids_col = jnp.transpose(ids_row)
    bias = jnp.where(ids_row == ids_col, 0.0, NEG)
    keep = jnp.where(ids_col >= 0.0, 1.0, 0.0)
    keep_ref[...] = keep
    pad_ref[0:PAD, 0:LANES] = jnp.full((PAD, LANES), -9.0, F32)
    pad_ref[PAD + frames :, 0:LANES] = jnp.full((PAD, LANES), -9.0, F32)
    pad_ref[PAD : PAD + frames, 0:LANES] = ids_col
    ids_pad = pad_ref[:, 0:LANES]
    at, view = None, None
    for turn, start, tap in shifts(frames, taps):
        if turn != at:
            at, view = turn, turned(ids_pad, turn)
        mask_ref[tap * frames : (tap + 1) * frames, :] = jnp.where(
            view[start : start + frames] == ids_col, 1.0, 0.0
        )
    clear_edges(pad_ref, frames)
    low = pair_masks(frames)

    @pl.loop(0, tiles)
    def _(index):
        lanes = lanes_of(index)
        prob, context = attend(q_ref[:, lanes], k_ref[:, lanes], v_ref[:, lanes], bias, keep, low)
        prob_ref[index] = prob
        context_ref[:, lanes] = context

    for rows in chunks(frames):
        normed, _ = normalize(context_ref[rows, :])
        normed = jnp.where(keep[rows.start : rows.start + CHUNK, 0:1] > 0.0, normed, 0.0)
        normed_ref[rows, :] = normed
        pad_ref[pl.ds(PAD + rows.start, CHUNK), :] = (
            (normed * gain_ref[0:1, :]).astype(BF16).astype(F32)
        )

    @pl.loop(0, tiles)
    def _(index):
        lanes = lanes_of(index)
        pre_ref[:, lanes] = conv_forward(pad_ref, kernel_ref, bias_ref, mask_ref, frames, lanes)

    @pl.loop(0, tiles)
    def _(index):
        lanes = lanes_of(index)
        pre_act = pre_ref[:, lanes]
        sig = gate(pre_act)
        out_ref[:, lanes] = (pre_act * sig * keep_ref[...]).astype(BF16)
        grad_pre = gate_grad(cot_ref[:, lanes].astype(F32) * keep_ref[...], pre_act, sig)
        conv_in = pad_ref[PAD : PAD + frames, lanes]
        pad_ref[PAD : PAD + frames, lanes] = grad_pre
        sums_ref[taps : taps + 1, lanes] = jnp.sum(grad_pre, 0, keepdims=True)

        def store(tap, value):
            sums_ref[tap : tap + 1, lanes] = value

        grad_in = conv_backward(pad_ref, conv_in, kernel_ref, mask_ref, frames, lanes, store)
        sums_ref[taps + 1 : taps + 2, lanes] = jnp.sum(grad_in * normed_ref[:, lanes], 0, keepdims=True)
        pre_ref[:, lanes] = grad_in

    norm_backward(context_ref, pre_ref, gain_ref, keep, grad_ref, frames)


def cross_forward_kernel(
    q_ref, k_ref, v_ref, qn_ref, kn_ref, vn_ref, seg_ref, gain_ref, kernel_ref, bias_ref,
    own_ref, next_ref, qg_ref, kg_ref, vg_ref, prob_ref, context_ref, pre_ref,
    pad_ref,
):
    frames, width = q_ref.shape
    tiles = width // LANES
    first, length = crossing(seg_ref, frames)
    pick = gather_matrix(first, length, frames)
    place = scatter_matrix(first, length, frames)
    shape = (frames, frames)
    bias = jnp.where(iota(shape, 1) < length, 0.0, NEG)
    keep = jnp.where(iota(shape, 0) < length, 1.0, 0.0)
    low = pair_masks(frames)
    clear_edges(pad_ref, frames)

    @pl.loop(0, tiles)
    def _(index):
        lanes = lanes_of(index)

        def picked(own, other):
            both = jnp.concatenate([own[:, lanes], other[:, lanes]], 0)
            return dot(pick, both, NN).astype(BF16)

        query, key, value = picked(q_ref, qn_ref), picked(k_ref, kn_ref), picked(v_ref, vn_ref)
        qg_ref[:, lanes] = query
        kg_ref[:, lanes] = key
        vg_ref[:, lanes] = value
        prob, context = attend(query, key, value, bias, keep, low)
        prob_ref[index] = prob
        context_ref[:, lanes] = context

    for rows in chunks(frames):
        normed, _ = normalize(context_ref[rows, :])
        normed = jnp.where(keep[rows.start : rows.start + CHUNK, 0:1] > 0.0, normed, 0.0)
        pad_ref[pl.ds(PAD + rows.start, CHUNK), :] = (
            (normed * gain_ref[0:1, :]).astype(BF16).astype(F32)
        )

    @pl.loop(0, tiles)
    def _(index):
        lanes = lanes_of(index)
        pre_act = conv_forward(pad_ref, kernel_ref, bias_ref, None, frames, lanes)
        pre_ref[:, lanes] = pre_act
        placed = dot(place, (pre_act * gate(pre_act)).astype(BF16), NN).astype(BF16)
        own_ref[:, lanes] = placed[:frames]
        next_ref[:, lanes] = placed[frames:]


def cross_conv_kernel(
    cot_ref, cotn_ref, seg_ref, gain_ref, kernel_ref, context_ref, pre_ref, part_ref,
    grad_ref, sums_ref,
    pad_ref, in_ref, normed_ref, back_ref,
):
    frames, width = cot_ref.shape
    taps = kernel_ref.shape[0]
    tiles = width // LANES
    first, length = crossing(seg_ref, frames)
    pick = gather_matrix(first, length, frames)
    keep = jnp.where(iota((frames, frames), 0) < length, 1.0, 0.0)
    clear_edges(pad_ref, frames)
    for rows in chunks(frames):
        normed, _ = normalize(context_ref[rows, :])
        normed = jnp.where(keep[rows.start : rows.start + CHUNK, 0:1] > 0.0, normed, 0.0)
        normed_ref[rows, :] = normed
        in_ref[rows, :] = (normed * gain_ref[0:1, :]).astype(BF16).astype(F32)

    @pl.loop(0, tiles)
    def _(index):
        lanes = lanes_of(index)
        cotangent = dot(pick, jnp.concatenate([cot_ref[:, lanes], cotn_ref[:, lanes]], 0), NN)
        pre_act = pre_ref[:, lanes]
        grad_pre = gate_grad(cotangent, pre_act, gate(pre_act))
        pad_ref[PAD : PAD + frames, lanes] = grad_pre

        def store(row, value):
            sums_ref[row : row + 1, lanes] = part_ref[row : row + 1, lanes] + value

        store(taps, jnp.sum(grad_pre, 0, keepdims=True))
        grad_in = conv_backward(pad_ref, in_ref[:, lanes], kernel_ref, None, frames, lanes, store)
        store(taps + 1, jnp.sum(grad_in * normed_ref[:, lanes], 0, keepdims=True))
        back_ref[:, lanes] = grad_in

    norm_backward(context_ref, back_ref, gain_ref, keep, grad_ref, frames)


def cross_back_kernel(
    group, tiles, q_ref, k_ref, v_ref, prob_ref, context_ref, grad_ref, seg_ref, own_ref, next_ref
):
    frames = q_ref.shape[0]
    place = scatter_matrix(*crossing(seg_ref, frames), frames)
    low = pair_masks(frames)

    @pl.loop(0, tiles)
    def _(step):
        index = group * tiles + step
        lanes, dest = lanes_of(index), lanes_of(step)
        results = attend_back(
            q_ref[:, lanes], k_ref[:, lanes], v_ref[:, lanes], prob_ref[index],
            context_ref[:, lanes], grad_ref[:, lanes], low,
        )
        for which, result in enumerate(results):
            placed = dot(place, result.astype(BF16), NN).astype(BF16)
            own_ref[which, :, dest] = placed[:frames]
            next_ref[which, :, dest] = placed[frames:]


def own_back_kernel(q_ref, k_ref, v_ref, prob_ref, context_ref, grad_ref, *refs):
    cross, (out_ref,) = refs[:-1], refs[-1:]
    frames, width = q_ref.shape
    low = pair_masks(frames)
    tiles = width // LANES // len(cross)
    for group, cross_ref in enumerate(cross):

        @pl.loop(0, tiles)
        def _(step):
            index = group * tiles + step
            lanes, dest = lanes_of(index), lanes_of(step)
            results = attend_back(
                q_ref[:, lanes], k_ref[:, lanes], v_ref[:, lanes], prob_ref[index],
                context_ref[:, lanes], grad_ref[:, lanes], low,
            )
            for which, result in enumerate(results):
                out_ref[which, :, lanes] = result.astype(BF16) + cross_ref[which, :, dest]


def call(kernel, outs, scratch, flops, *args):
    size = sum(a.size * a.dtype.itemsize for a in args) + sum(o.size * o.dtype.itemsize for o in outs)
    return pl.pallas_call(
        kernel,
        out_shape=outs,
        in_specs=[VMEM] * len(args),
        out_specs=[VMEM] * len(outs),
        scratch_shapes=scratch,
        compiler_params=pltpu.CompilerParams(vmem_limit_bytes=40 * 1024 * 1024),
        cost_estimate=pl.CostEstimate(flops=flops, bytes_accessed=size, transcendentals=0),
    )(*args)


def total_over_devices(part, axes):
    total = part
    for axis in axes:
        count = lax.axis_size(axis)
        step = 1
        while step < count:
            sent = total.astype(BF16)
            came = lax.ppermute(sent, axis, [(i, i ^ step) for i in range(count)])
            total = sent.astype(F32) + came.astype(F32)
            step *= 2
    return total


def per_device(queries, keys, values, segment_ids, norm_gain, conv_kernel, conv_bias, cotangent):
    q, k, v, cot = queries[0], keys[0], values[0], cotangent[0]
    frames, width = q.shape
    taps = conv_kernel.shape[0]
    tiles = width // LANES
    count = lax.axis_size("seq")
    gain, bias = norm_gain[None], conv_bias[None]
    seg = segment_ids
    to_left = [(i + 1, i) for i in range(count - 1)]
    to_right = [(i, i + 1) for i in range(count - 1)]
    qn, kn, vn, cotn = (lax.ppermute(a, "seq", to_left) for a in (q, k, v, cot))

    def sds(shape, dtype):
        return jax.ShapeDtypeStruct(shape, dtype)

    rows16 = sds((frames, width), BF16)
    rows32 = sds((frames, width), F32)
    probs = sds((tiles, frames, 2 * frames), BF16)
    sums = sds((taps + 2, width), F32)
    padded = pltpu.VMEM((frames + 2 * PAD, width), F32)
    plain = pltpu.VMEM((frames, width), F32)

    out_own, grad_own, prob_own, context_own, sums_own = call(
        own_kernel,
        [rows16, rows16, probs, rows16, sums],
        [padded, plain, plain, pltpu.VMEM((taps * frames, LANES), F32), pltpu.VMEM((frames, LANES), F32)],
        10**10,
        q, k, v, cot, seg, gain, conv_kernel, bias,
    )
    out_cross, out_next, qg, kg, vg, prob_cross, context_cross, pre_cross = call(
        cross_forward_kernel,
        [rows16, rows16, rows16, rows16, rows16, probs, rows16, rows32],
        [padded],
        4 * 10**9,
        q, k, v, qn, kn, vn, seg, gain, conv_kernel, bias,
    )
    out_came = lax.ppermute(out_next, "seq", to_right)
    grad_cross, sums_both = call(
        cross_conv_kernel,
        [rows16, sums],
        [padded, plain, plain, plain],
        4 * 10**9,
        cot, cotn, seg, gain, conv_kernel, context_cross, pre_cross, sums_own,
    )
    per_group = tiles // GROUPS
    piece = sds((3, frames, per_group * LANES), BF16)
    own_parts, came_parts = [], []
    for group in range(GROUPS):
        own_part, next_part = call(
            functools.partial(cross_back_kernel, group, per_group),
            [piece, piece],
            [],
            10**9,
            qg, kg, vg, prob_cross, context_cross, grad_cross, seg,
        )
        own_parts.append(own_part)
        came_parts.append(lax.ppermute(next_part, "seq", to_right))
    (grads_own,) = call(
        own_back_kernel,
        [sds((3, frames, width), BF16)],
        [],
        3 * 10**9,
        q, k, v, prob_own, context_own, grad_own, *own_parts,
    )
    conv_out = out_own + out_cross + out_came
    grads = grads_own + jnp.concatenate(came_parts, 2)
    total = total_over_devices(sums_both, ("seq", "dp"))
    total = total * (lax.axis_size("dp") * count * frames) ** (-0.5)
    return (
        conv_out[None],
        grads[0][None],
        grads[1][None],
        grads[2][None],
        total[taps + 1],
        total[:taps],
        total[taps],
    )


def solution(mesh):
    rows = P("dp", "seq", None)
    return jax.shard_map(
        per_device,
        mesh=mesh,
        in_specs=(rows, rows, rows, P("dp", None), P(), P(), P(), rows),
        out_specs=(rows, rows, rows, rows, P(), P(), P()),
        check_vma=False,
    )
```

```python
import functools

import jax
import jax.numpy as jnp
from jax import lax
from jax.experimental import pallas as pl
from jax.experimental.pallas import tpu as pltpu
from jax.sharding import PartitionSpec as P

HEAD_DIM = 64
EPS = 1e-05
NEG = -1e30
LANES = 128
PAD = 16
GROUPS = 2
WIDE = 512
VMEM = pl.BlockSpec(memory_space=pltpu.VMEM)
F32 = jnp.float32
BF16 = jnp.bfloat16


def dot(a, b, dims):
    return lax.dot_general(a, b, (dims, ((), ())), preferred_element_type=F32)


NN = ((1,), (0,))
NT = ((1,), (1,))
TN = ((0,), (0,))


def lanes_of(index):
    return pl.ds(pl.multiple_of(index * LANES, LANES), LANES)


def block_ids(seg_ref, frames):
    me = lax.axis_index("seq")
    count = seg_ref.shape[1] // frames
    own = seg_ref[0:1, pl.ds(pl.multiple_of(me * frames, frames), frames)].astype(F32)
    before = jnp.maximum(me - 1, 0)
    after = jnp.minimum(me + 1, count - 1)
    prev = seg_ref[0:1, pl.ds(pl.multiple_of(before * frames, frames), frames)].astype(F32)
    following = seg_ref[0:1, pl.ds(pl.multiple_of(after * frames, frames), frames)].astype(F32)
    prev_last = jnp.where(me > 0, prev[:, frames - 1 :], -1.0)
    following = jnp.where(me < count - 1, following, -1.0)
    return own, following, prev_last, following[:, 0:1]


def crossing(seg_ref, frames):
    own, following, _, edge = block_ids(seg_ref, frames)
    left = jnp.sum(jnp.where((own == edge) & (edge >= 0.0), 1.0, 0.0), 1, keepdims=True)
    right = jnp.sum(jnp.where(following == edge, 1.0, 0.0), 1, keepdims=True)
    length = jnp.where(left > 0.0, left + right, 0.0)
    return frames - left, length


def iota(shape, axis):
    return lax.broadcasted_iota(jnp.int32, shape, axis).astype(F32)


def gather_matrix(first, length, frames):
    shape = (frames, 2 * frames)
    row = iota(shape, 0)
    return jnp.where((iota(shape, 1) == row + first) & (row < length), 1.0, 0.0).astype(BF16)


def scatter_matrix(first, length, frames):
    shape = (2 * frames, frames)
    col = iota(shape, 1)
    return jnp.where((iota(shape, 0) == col + first) & (col < length), 1.0, 0.0).astype(BF16)


def pair_masks(rows):
    low = lax.broadcasted_iota(jnp.int32, (rows, LANES), 1) < HEAD_DIM
    return low


def stack_pair(pair, low):
    zero = jnp.zeros_like(pair)
    return jnp.concatenate([jnp.where(low, pair, zero), jnp.where(low, zero, pair)], 0)


def attend(query, key, value, bias, keep, low):
    frames = query.shape[0]
    logits = dot(query * jnp.asarray(HEAD_DIM**-0.5, BF16), stack_pair(key, low), NT)
    halves = []
    for half in range(2):
        part = logits[:, half * frames : (half + 1) * frames] + bias
        top = jnp.max(part, 1, keepdims=True)
        power = jnp.exp(part - top)
        total = jnp.sum(power, 1, keepdims=True)
        halves.append((power * (1.0 / total)).astype(BF16))
    prob = jnp.concatenate(halves, 1)
    context = dot(prob, stack_pair(value, low), NN)
    return prob, (context * keep).astype(BF16)


def attend_back(query, key, value, prob, context, grad, low):
    frames = query.shape[0]
    scale = HEAD_DIM**-0.5
    grad_prob = dot(grad, stack_pair(value, low), NT)
    product = grad.astype(F32) * context.astype(F32)
    zero = jnp.zeros_like(product)
    deltas = (
        jnp.sum(jnp.where(low, product, zero), 1, keepdims=True),
        jnp.sum(jnp.where(low, zero, product), 1, keepdims=True),
    )
    parts = []
    for half in range(2):
        cols = slice(half * frames, (half + 1) * frames)
        parts.append(
            (prob[:, cols].astype(F32) * (grad_prob[:, cols] - deltas[half]) * scale).astype(BF16)
        )
    query_grad = dot(jnp.concatenate(parts, 1), stack_pair(key, low), NN)
    key_grad = dot(jnp.concatenate(parts, 0), stack_pair(query, low), TN)
    prob_rows = jnp.concatenate([prob[:, :frames], prob[:, frames:]], 0)
    value_grad = dot(prob_rows, stack_pair(grad, low), TN)
    return query_grad, key_grad, value_grad


def normalize(context):
    context = context.astype(F32)
    centred = context - jnp.mean(context, -1, keepdims=True)
    inv_std = lax.rsqrt(jnp.mean(centred * centred, -1, keepdims=True) + EPS)
    return centred * inv_std, inv_std


CHUNK = 32


def chunks(frames):
    return [pl.ds(start, CHUNK) for start in range(0, frames, CHUNK)]


def clear_edges(pad_ref, frames):
    zero = jnp.zeros((PAD, pad_ref.shape[1]), F32)
    pad_ref[0:PAD, :] = zero
    pad_ref[PAD + frames : 2 * PAD + frames, :] = zero


def shifts(frames, taps):
    base = PAD - taps // 2
    for turn in range(8):
        for start in range(0, 2 * PAD + 1, 8):
            tap = start + turn - base
            if 0 <= tap < taps:
                yield turn, start, tap


def turned(block, turn):
    rows = block.shape[0]
    return block if turn == 0 else pltpu.roll(block, rows - turn, 0)


def conv_forward(pad_ref, kernel_ref, bias_ref, mask_ref, frames, lanes):
    taps = kernel_ref.shape[0]
    block = pad_ref[:, lanes]
    total = jnp.broadcast_to(bias_ref[0:1, lanes], (frames, LANES))
    at, view = None, None
    for turn, start, tap in shifts(frames, taps):
        if turn != at:
            at, view = turn, turned(block, turn)
        term = view[start : start + frames]
        if mask_ref is not None:
            term = term * mask_ref[tap * frames : (tap + 1) * frames, :]
        total = total + kernel_ref[tap : tap + 1, lanes] * term
    return total


def conv_backward(pad_ref, conv_in, kernel_ref, mask_ref, frames, lanes, store):
    taps = kernel_ref.shape[0]
    block = pad_ref[:, lanes]
    total = jnp.zeros((frames, LANES), F32)
    at, view = None, None
    for turn, start, mirror in shifts(frames, taps):
        if turn != at:
            at, view = turn, turned(block, turn)
        tap = taps - 1 - mirror
        term = view[start : start + frames]
        if mask_ref is not None:
            term = term * mask_ref[mirror * frames : (mirror + 1) * frames, :]
        total = total + kernel_ref[tap : tap + 1, lanes] * term
        store(tap, jnp.sum(conv_in * term, 0, keepdims=True))
    return total


def gate(pre_act):
    return 1.0 / (1.0 + jnp.exp(-pre_act))


def gate_grad(cotangent, pre_act, sig):
    return (cotangent * sig * (1.0 + pre_act * (1.0 - sig))).astype(BF16).astype(F32)


def norm_backward(context_ref, grad_ref, gain_ref, keep, out_ref, frames):
    for rows in chunks(frames):
        normed, inv_std = normalize(context_ref[rows, :])
        grad = grad_ref[rows, :] * gain_ref[0:1, :]
        centre = jnp.mean(grad, -1, keepdims=True)
        slope = jnp.mean(grad * normed, -1, keepdims=True)
        result = (grad - centre - normed * slope) * inv_std
        out_ref[rows, :] = jnp.where(keep[rows.start : rows.start + CHUNK, 0:1] > 0.0, result, 0.0).astype(BF16)


def wide(width):
    return [slice(start, start + WIDE) for start in range(0, width, WIDE)]


def forward_all(q_ref, k_ref, v_ref, prob_ref, context_ref, bias, keep, low):
    for index in range(q_ref.shape[1] // LANES):
        lanes = slice(index * LANES, (index + 1) * LANES)
        prob, context = attend(q_ref[:, lanes], k_ref[:, lanes], v_ref[:, lanes], bias, keep, low)
        prob_ref[index] = prob
        context_ref[:, lanes] = context


def normalize_all(context_ref, gain_ref, keep, normed_ref, in_ref, offset, frames):
    for rows in chunks(frames):
        normed, _ = normalize(context_ref[rows, :])
        normed = jnp.where(keep[rows.start : rows.start + CHUNK, 0:1] > 0.0, normed, 0.0)
        if normed_ref is not None:
            normed_ref[rows, :] = normed
        in_ref[pl.ds(offset + rows.start, CHUNK), :] = (
            (normed * gain_ref[0:1, :]).astype(BF16).astype(F32)
        )


def mask_kernel(taps, seg_ref, bias_ref, keep_ref, mask_ref, pad_ref):
    frames = bias_ref.shape[0]
    own, _, prev_last, next_first = block_ids(seg_ref, frames)
    ids = jnp.where((own == prev_last) | (own == next_first), -5.0, own)
    ids_row = jnp.broadcast_to(ids, (frames, frames))
    ids_col = jnp.transpose(ids_row)
    bias_ref[...] = jnp.where(ids_row == ids_col, 0.0, NEG)
    keep_ref[...] = jnp.where(ids_col >= 0.0, 1.0, 0.0)
    pad_ref[...] = jnp.full(pad_ref.shape, -9.0, F32)
    pad_ref[PAD : PAD + frames, :] = ids_col
    ids_pad = pad_ref[...]
    at, view = None, None
    for turn, start, tap in shifts(frames, taps):
        if turn != at:
            at, view = turn, turned(ids_pad, turn)
        mask_ref[tap * frames : (tap + 1) * frames, :] = jnp.where(
            view[start : start + frames] == ids_col, 1.0, 0.0
        )


def own_kernel(
    q_ref, k_ref, v_ref, cot_ref, gain_row, kernel_ref, bias_row, same_ref, keep_ref, mask_ref,
    out_ref, grad_ref, prob_ref, context_ref, sums_ref, gain_ref, bias_ref,
    pad_ref, normed_ref, pre_ref,
):
    frames, width = q_ref.shape
    taps = kernel_ref.shape[0]
    tiles = width // LANES
    clear_edges(pad_ref, frames)
    low = pair_masks(frames)
    gain_ref[...] = gain_row[...].reshape(1, width)
    bias_ref[...] = bias_row[...].reshape(1, width)
    bias, keep = same_ref[...], keep_ref[...]
    forward_all(q_ref, k_ref, v_ref, prob_ref, context_ref, bias, keep, low)
    normalize_all(context_ref, gain_ref, keep, normed_ref, pad_ref, PAD, frames)

    @pl.loop(0, tiles)
    def _(index):
        lanes = lanes_of(index)
        pre_ref[:, lanes] = conv_forward(pad_ref, kernel_ref, bias_ref, mask_ref, frames, lanes)

    @pl.loop(0, tiles)
    def _(index):
        lanes = lanes_of(index)
        pre_act = pre_ref[:, lanes]
        sig = gate(pre_act)
        out_ref[:, lanes] = (pre_act * sig * keep_ref[...]).astype(BF16)
        grad_pre = gate_grad(cot_ref[:, lanes].astype(F32) * keep_ref[...], pre_act, sig)
        conv_in = pad_ref[PAD : PAD + frames, lanes]
        pad_ref[PAD : PAD + frames, lanes] = grad_pre
        sums_ref[taps : taps + 1, lanes] = jnp.sum(grad_pre, 0, keepdims=True)

        def store(tap, value):
            sums_ref[tap : tap + 1, lanes] = value

        grad_in = conv_backward(pad_ref, conv_in, kernel_ref, mask_ref, frames, lanes, store)
        sums_ref[taps + 1 : taps + 2, lanes] = jnp.sum(grad_in * normed_ref[:, lanes], 0, keepdims=True)
        pre_ref[:, lanes] = grad_in

    norm_backward(context_ref, pre_ref, gain_ref, keep, grad_ref, frames)


def cross_forward_kernel(
    q_ref, k_ref, v_ref, qn_ref, kn_ref, vn_ref, seg_ref, gain_ref, kernel_ref, bias_ref, add_ref,
    own_ref, next_ref, qg_ref, kg_ref, vg_ref, prob_ref, context_ref, pre_ref,
    pad_ref, out_ref,
):
    frames, width = q_ref.shape
    tiles = width // LANES
    first, length = crossing(seg_ref, frames)
    pick = gather_matrix(first, length, frames)
    place = scatter_matrix(first, length, frames)
    shape = (frames, frames)
    bias = jnp.where(iota(shape, 1) < length, 0.0, NEG)
    keep = jnp.where(iota(shape, 0) < length, 1.0, 0.0)
    low = pair_masks(frames)
    clear_edges(pad_ref, frames)
    for own, other, got in ((q_ref, qn_ref, qg_ref), (k_ref, kn_ref, kg_ref), (v_ref, vn_ref, vg_ref)):
        for cols in wide(width):
            both = jnp.concatenate([own[:, cols], other[:, cols]], 0)
            got[:, cols] = dot(pick, both, NN).astype(BF16)
    forward_all(qg_ref, kg_ref, vg_ref, prob_ref, context_ref, bias, keep, low)
    normalize_all(context_ref, gain_ref, keep, None, pad_ref, PAD, frames)

    @pl.loop(0, tiles)
    def _(index):
        lanes = lanes_of(index)
        pre_act = conv_forward(pad_ref, kernel_ref, bias_ref, None, frames, lanes)
        pre_ref[:, lanes] = pre_act
        out_ref[:, lanes] = (pre_act * gate(pre_act)).astype(BF16)

    for cols in wide(width):
        placed = dot(place, out_ref[:, cols], NN).astype(BF16)
        own_ref[:, cols] = placed[:frames] + add_ref[:, cols]
        next_ref[:, cols] = placed[frames:]


def cross_conv_kernel(
    cot_ref, cotn_ref, seg_ref, gain_ref, kernel_ref, context_ref, pre_ref, part_ref,
    back_ref, sums_ref, sent_ref,
    pad_ref, in_ref, normed_ref,
):
    frames, width = cot_ref.shape
    taps = kernel_ref.shape[0]
    tiles = width // LANES
    first, length = crossing(seg_ref, frames)
    pick = gather_matrix(first, length, frames)
    keep = jnp.where(iota((frames, frames), 0) < length, 1.0, 0.0)
    clear_edges(pad_ref, frames)
    for cols in wide(width):
        cotangent = dot(pick, jnp.concatenate([cot_ref[:, cols], cotn_ref[:, cols]], 0), NN)
        pre_act = pre_ref[:, cols]
        pad_ref[PAD : PAD + frames, cols] = gate_grad(cotangent, pre_act, gate(pre_act))
    normalize_all(context_ref, gain_ref, keep, normed_ref, in_ref, 0, frames)

    @pl.loop(0, tiles)
    def _(index):
        lanes = lanes_of(index)

        def store(row, value):
            sums_ref[row : row + 1, lanes] = part_ref[row : row + 1, lanes] + value

        store(taps, jnp.sum(pad_ref[PAD : PAD + frames, lanes], 0, keepdims=True))
        grad_in = conv_backward(pad_ref, in_ref[:, lanes], kernel_ref, None, frames, lanes, store)
        store(taps + 1, jnp.sum(grad_in * normed_ref[:, lanes], 0, keepdims=True))
        back_ref[:, lanes] = grad_in

    sent_ref[...] = sums_ref[...].astype(BF16)


def cross_back_kernel(
    group, tiles, q_ref, k_ref, v_ref, prob_ref, context_ref, back_ref, gain_ref, seg_ref,
    own_ref, next_ref, grad_ref=None,
):
    frames = q_ref.shape[0]
    first, length = crossing(seg_ref, frames)
    place = scatter_matrix(first, length, frames)
    low = pair_masks(frames)
    if group == 0:
        keep = jnp.where(iota((frames, frames), 0) < length, 1.0, 0.0)
        norm_backward(context_ref, back_ref, gain_ref, keep, grad_ref, frames)
    else:
        grad_ref = back_ref
    for step in range(tiles):
        index = group * tiles + step
        lanes = slice(index * LANES, (index + 1) * LANES)
        dest = slice(step * LANES, (step + 1) * LANES)
        results = attend_back(
            q_ref[:, lanes], k_ref[:, lanes], v_ref[:, lanes], prob_ref[index],
            context_ref[:, lanes], grad_ref[:, lanes], low,
        )
        joined = jnp.concatenate([result.astype(BF16) for result in results], 1)
        placed = dot(place, joined, NN).astype(BF16)
        for which in range(3):
            cols = slice(which * LANES, (which + 1) * LANES)
            own_ref[which, :, dest] = placed[:frames, cols]
            next_ref[which, :, dest] = placed[frames:, cols]


def own_back_kernel(q_ref, k_ref, v_ref, prob_ref, context_ref, grad_ref, *refs):
    cross, (out_ref,) = refs[:-1], refs[-1:]
    frames, width = q_ref.shape
    low = pair_masks(frames)
    tiles = width // LANES // len(cross)
    for group, cross_ref in enumerate(cross):
        for step in range(tiles):
            index = group * tiles + step
            lanes = slice(index * LANES, (index + 1) * LANES)
            dest = slice(step * LANES, (step + 1) * LANES)
            results = attend_back(
                q_ref[:, lanes], k_ref[:, lanes], v_ref[:, lanes], prob_ref[index],
                context_ref[:, lanes], grad_ref[:, lanes], low,
            )
            for which, result in enumerate(results):
                out_ref[which, :, lanes] = result.astype(BF16) + cross_ref[which, :, dest]


def finish_kernel(scale, sent_ref, came_ref, gain_ref, kernel_ref, bias_ref):
    taps, width = kernel_ref.shape
    total = (sent_ref[...].astype(F32) + came_ref[...].astype(F32)) * scale
    kernel_ref[...] = total[:taps]
    bias_ref[...] = total[taps : taps + 1].reshape(width)
    gain_ref[...] = total[taps + 1 : taps + 2].reshape(width)


def call(kernel, outs, scratch, flops, *args):
    size = sum(a.size * a.dtype.itemsize for a in args) + sum(o.size * o.dtype.itemsize for o in outs)
    return pl.pallas_call(
        kernel,
        out_shape=outs,
        in_specs=[VMEM] * len(args),
        out_specs=[VMEM] * len(outs),
        scratch_shapes=scratch,
        compiler_params=pltpu.CompilerParams(vmem_limit_bytes=24 * 1024 * 1024),
        cost_estimate=pl.CostEstimate(flops=flops, bytes_accessed=size, transcendentals=0),
    )(*args)


def after(value, *others):
    return lax.optimization_barrier((value,) + others)[0]


def sum_steps(axes):
    steps = []
    for axis in axes:
        step = 1
        while step < lax.axis_size(axis):
            steps.append((axis, step))
            step *= 2
    return steps


def exchange(sent, axis, step):
    return lax.ppermute(sent, axis, [(i, i ^ step) for i in range(lax.axis_size(axis))])


def added(sent, came):
    return (sent.astype(F32) + came.astype(F32)).astype(BF16)


def per_device(queries, keys, values, segment_ids, norm_gain, conv_kernel, conv_bias, cotangent):
    q, k, v, cot = queries[0], keys[0], values[0], cotangent[0]
    frames, width = q.shape
    taps = conv_kernel.shape[0]
    tiles = width // LANES
    count = lax.axis_size("seq")
    to_left = [(i + 1, i) for i in range(count - 1)]
    to_right = [(i, i + 1) for i in range(count - 1)]
    qn, kn, vn, cotn = (lax.ppermute(a, "seq", to_left) for a in (q, k, v, cot))

    def sds(shape, dtype):
        return jax.ShapeDtypeStruct(shape, dtype)

    rows16 = sds((frames, width), BF16)
    rows32 = sds((frames, width), F32)
    probs = sds((tiles, frames, 2 * frames), BF16)
    sums = sds((taps + 2, width), F32)
    row = sds((1, width), F32)
    padded = pltpu.VMEM((frames + 2 * PAD, width), F32)
    plain = pltpu.VMEM((frames, width), F32)

    square = sds((frames, frames), F32)
    same, keep, masks = call(
        functools.partial(mask_kernel, taps),
        [square, square, sds((taps * frames, LANES), F32)],
        [pltpu.VMEM((frames + 2 * PAD, LANES), F32)],
        10**10,
        segment_ids,
    )
    out_own, grad_own, prob_own, context_own, sums_own, gain, bias = call(
        own_kernel,
        [rows16, rows16, probs, rows16, sums, row, row],
        [padded, plain, plain],
        10**10,
        q, k, v, cot, norm_gain, conv_kernel, conv_bias, same, keep, masks,
    )
    out_both, out_next, qg, kg, vg, prob_cross, context_cross, pre_cross = call(
        cross_forward_kernel,
        [rows16, rows16, rows16, rows16, rows16, probs, rows16, rows32],
        [padded, pltpu.VMEM((frames, width), BF16)],
        4 * 10**9,
        q, k, v, qn, kn, vn, segment_ids, gain, conv_kernel, bias, out_own,
    )
    out_came = lax.ppermute(out_next, "seq", to_right)
    back_cross, _, sent = call(
        cross_conv_kernel,
        [rows32, sums, sds(sums.shape, BF16)],
        [padded, plain, plain],
        4 * 10**9,
        cot, cotn, segment_ids, gain, conv_kernel, context_cross, pre_cross, sums_own,
    )
    steps = sum_steps(("seq", "dp"))
    came = exchange(sent, *steps[0])
    per_group = tiles // GROUPS
    piece = sds((3, frames, per_group * LANES), BF16)
    own_parts, came_parts = [], []
    grad_cross = back_cross
    for group in range(GROUPS):
        own_part, next_part, *rest = call(
            functools.partial(cross_back_kernel, group, per_group),
            [piece, piece] + [rows16] * (group == 0),
            [],
            2 * 10**9,
            qg, kg, vg, prob_cross, context_cross, grad_cross, gain, segment_ids,
        )
        if group == 0:
            (grad_cross,) = rest
        own_parts.append(own_part)
        came_parts.append(lax.ppermute(next_part, "seq", to_right))
        if group == 0:
            conv_out = out_both + after(out_came, own_part)
            sent = added(sent, after(came, own_part, conv_out))
        else:
            sent = added(sent, after(came, own_part, came_parts[0]))
        came = exchange(sent, *steps[group + 1])
    (grads_own,) = call(
        own_back_kernel,
        [sds((3, frames, width), BF16)],
        [],
        4 * 10**9,
        q, k, v, prob_own, context_own, grad_own, *own_parts,
    )
    came = after(came, grads_own, *came_parts)
    for step in steps[GROUPS + 1 :]:
        sent = added(sent, came)
        came = exchange(sent, *step)
    grads = grads_own + jnp.concatenate(came_parts, 2)
    scale = (lax.axis_size("dp") * count * frames) ** (-0.5)
    gain_grad, kernel_grad, bias_grad = call(
        functools.partial(finish_kernel, scale),
        [sds((width,), F32), sds(conv_kernel.shape, F32), sds((width,), F32)],
        [],
        10**6,
        sent, came,
    )
    return (
        conv_out[None],
        grads[0][None],
        grads[1][None],
        grads[2][None],
        gain_grad,
        kernel_grad,
        bias_grad,
    )


def solution(mesh):
    rows = P("dp", "seq", None)
    return jax.shard_map(
        per_device,
        mesh=mesh,
        in_specs=(rows, rows, rows, P("dp", None), P(), P(), P(), rows),
        out_specs=(rows, rows, rows, rows, P(), P(), P()),
        check_vma=False,
    )
```

```python
import functools

import jax
import jax.numpy as jnp
from jax import lax
from jax.experimental import pallas as pl
from jax.experimental.pallas import tpu as pltpu
from jax.sharding import PartitionSpec as P

HEAD_DIM = 64
EPS = 1e-05
NEG = -1e30
LANES = 128
PAD = 16
GROUPS = 2
WIDE = 512
VMEM = pl.BlockSpec(memory_space=pltpu.VMEM)
F32 = jnp.float32
BF16 = jnp.bfloat16


def dot(a, b, dims):
    return lax.dot_general(a, b, (dims, ((), ())), preferred_element_type=F32)


NN = ((1,), (0,))
NT = ((1,), (1,))
TN = ((0,), (0,))


def lanes_of(index):
    return pl.ds(pl.multiple_of(index * LANES, LANES), LANES)


def block_ids(seg_ref, frames):
    me = lax.axis_index("seq")
    count = seg_ref.shape[1] // frames
    own = seg_ref[0:1, pl.ds(pl.multiple_of(me * frames, frames), frames)].astype(F32)
    before = jnp.maximum(me - 1, 0)
    after = jnp.minimum(me + 1, count - 1)
    prev = seg_ref[0:1, pl.ds(pl.multiple_of(before * frames, frames), frames)].astype(F32)
    following = seg_ref[0:1, pl.ds(pl.multiple_of(after * frames, frames), frames)].astype(F32)
    prev_last = jnp.where(me > 0, prev[:, frames - 1 :], -1.0)
    following = jnp.where(me < count - 1, following, -1.0)
    return own, following, prev_last, following[:, 0:1]


def crossing(seg_ref, frames):
    own, following, _, edge = block_ids(seg_ref, frames)
    left = jnp.sum(jnp.where((own == edge) & (edge >= 0.0), 1.0, 0.0), 1, keepdims=True)
    right = jnp.sum(jnp.where(following == edge, 1.0, 0.0), 1, keepdims=True)
    length = jnp.where(left > 0.0, left + right, 0.0)
    return frames - left, length


def iota(shape, axis):
    return lax.broadcasted_iota(jnp.int32, shape, axis).astype(F32)


def gather_matrix(first, length, frames):
    shape = (frames, 2 * frames)
    row = iota(shape, 0)
    return jnp.where((iota(shape, 1) == row + first) & (row < length), 1.0, 0.0).astype(BF16)


def scatter_matrix(first, length, frames):
    shape = (2 * frames, frames)
    col = iota(shape, 1)
    return jnp.where((iota(shape, 0) == col + first) & (col < length), 1.0, 0.0).astype(BF16)


def pair_masks(rows):
    low = lax.broadcasted_iota(jnp.int32, (rows, LANES), 1) < HEAD_DIM
    return low


def stack_pair(pair, low):
    zero = jnp.zeros_like(pair)
    return jnp.concatenate([jnp.where(low, pair, zero), jnp.where(low, zero, pair)], 0)


def attend(query, key, value, bias, keep, low):
    frames = query.shape[0]
    logits = dot(query * jnp.asarray(HEAD_DIM**-0.5, BF16), stack_pair(key, low), NT)
    halves = []
    for half in range(2):
        part = logits[:, half * frames : (half + 1) * frames] + bias
        top = jnp.max(part, 1, keepdims=True)
        power = jnp.exp(part - top)
        total = jnp.sum(power, 1, keepdims=True)
        halves.append((power * (1.0 / total)).astype(BF16))
    prob = jnp.concatenate(halves, 1)
    context = dot(prob, stack_pair(value, low), NN)
    return prob, (context * keep).astype(BF16)


def attend_back(query, key, value, prob, context, grad, low):
    frames = query.shape[0]
    scale = HEAD_DIM**-0.5
    grad_prob = dot(grad, stack_pair(value, low), NT)
    product = grad.astype(F32) * context.astype(F32)
    zero = jnp.zeros_like(product)
    deltas = (
        jnp.sum(jnp.where(low, product, zero), 1, keepdims=True),
        jnp.sum(jnp.where(low, zero, product), 1, keepdims=True),
    )
    parts = []
    for half in range(2):
        cols = slice(half * frames, (half + 1) * frames)
        parts.append(
            (prob[:, cols].astype(F32) * (grad_prob[:, cols] - deltas[half]) * scale).astype(BF16)
        )
    query_grad = dot(jnp.concatenate(parts, 1), stack_pair(key, low), NN)
    key_grad = dot(jnp.concatenate(parts, 0), stack_pair(query, low), TN)
    prob_rows = jnp.concatenate([prob[:, :frames], prob[:, frames:]], 0)
    value_grad = dot(prob_rows, stack_pair(grad, low), TN)
    return query_grad, key_grad, value_grad


def normalize(context):
    context = context.astype(F32)
    centred = context - jnp.mean(context, -1, keepdims=True)
    inv_std = lax.rsqrt(jnp.mean(centred * centred, -1, keepdims=True) + EPS)
    return centred * inv_std, inv_std


CHUNK = 32


def chunks(frames):
    return [pl.ds(start, CHUNK) for start in range(0, frames, CHUNK)]


def clear_edges(pad_ref, frames):
    zero = jnp.zeros((PAD, pad_ref.shape[1]), F32)
    pad_ref[0:PAD, :] = zero
    pad_ref[PAD + frames : 2 * PAD + frames, :] = zero


def shifts(frames, taps):
    base = PAD - taps // 2
    for turn in range(8):
        for start in range(0, 2 * PAD + 1, 8):
            tap = start + turn - base
            if 0 <= tap < taps:
                yield turn, start, tap


def turned(block, turn):
    rows = block.shape[0]
    return block if turn == 0 else pltpu.roll(block, rows - turn, 0)


def conv_forward(pad_ref, kernel_ref, bias_ref, mask_ref, frames, lanes):
    taps = kernel_ref.shape[0]
    block = pad_ref[:, lanes]
    total = jnp.broadcast_to(bias_ref[0:1, lanes], (frames, LANES))
    at, view = None, None
    for turn, start, tap in shifts(frames, taps):
        if turn != at:
            at, view = turn, turned(block, turn)
        term = view[start : start + frames]
        if mask_ref is not None:
            term = term * mask_ref[tap * frames : (tap + 1) * frames, :]
        total = total + kernel_ref[tap : tap + 1, lanes] * term
    return total


def conv_backward(pad_ref, conv_in, kernel_ref, mask_ref, frames, lanes, store):
    taps = kernel_ref.shape[0]
    block = pad_ref[:, lanes]
    total = jnp.zeros((frames, LANES), F32)
    at, view = None, None
    for turn, start, mirror in shifts(frames, taps):
        if turn != at:
            at, view = turn, turned(block, turn)
        tap = taps - 1 - mirror
        term = view[start : start + frames]
        if mask_ref is not None:
            term = term * mask_ref[mirror * frames : (mirror + 1) * frames, :]
        total = total + kernel_ref[tap : tap + 1, lanes] * term
        store(tap, jnp.sum(conv_in * term, 0, keepdims=True))
    return total


def gate(pre_act):
    return 1.0 / (1.0 + jnp.exp(-pre_act))


def gate_grad(cotangent, pre_act, sig):
    return (cotangent * sig * (1.0 + pre_act * (1.0 - sig))).astype(BF16).astype(F32)


def norm_backward(context_ref, grad_ref, gain_ref, keep, out_ref, frames):
    for rows in chunks(frames):
        normed, inv_std = normalize(context_ref[rows, :])
        grad = grad_ref[rows, :] * gain_ref[0:1, :]
        centre = jnp.mean(grad, -1, keepdims=True)
        slope = jnp.mean(grad * normed, -1, keepdims=True)
        result = (grad - centre - normed * slope) * inv_std
        out_ref[rows, :] = jnp.where(keep[rows.start : rows.start + CHUNK, 0:1] > 0.0, result, 0.0).astype(BF16)


def wide(width):
    return [slice(start, start + WIDE) for start in range(0, width, WIDE)]


def forward_all(q_ref, k_ref, v_ref, prob_ref, context_ref, bias, keep, low):
    for index in range(q_ref.shape[1] // LANES):
        lanes = slice(index * LANES, (index + 1) * LANES)
        prob, context = attend(q_ref[:, lanes], k_ref[:, lanes], v_ref[:, lanes], bias, keep, low)
        prob_ref[index] = prob
        context_ref[:, lanes] = context


def normalize_all(context_ref, gain_ref, keep, normed_ref, in_ref, offset, frames):
    for rows in chunks(frames):
        normed, _ = normalize(context_ref[rows, :])
        normed = jnp.where(keep[rows.start : rows.start + CHUNK, 0:1] > 0.0, normed, 0.0)
        if normed_ref is not None:
            normed_ref[rows, :] = normed
        in_ref[pl.ds(offset + rows.start, CHUNK), :] = (
            (normed * gain_ref[0:1, :]).astype(BF16).astype(F32)
        )


def mask_kernel(taps, seg_ref, bias_ref, keep_ref, mask_ref, pad_ref):
    frames = bias_ref.shape[0]
    own, _, prev_last, next_first = block_ids(seg_ref, frames)
    ids = jnp.where((own == prev_last) | (own == next_first), -5.0, own)
    ids_row = jnp.broadcast_to(ids, (frames, frames))
    ids_col = jnp.transpose(ids_row)
    bias_ref[...] = jnp.where(ids_row == ids_col, 0.0, NEG)
    keep_ref[...] = jnp.where(ids_col >= 0.0, 1.0, 0.0)
    pad_ref[...] = jnp.full(pad_ref.shape, -9.0, F32)
    pad_ref[PAD : PAD + frames, :] = ids_col
    ids_pad = pad_ref[...]
    at, view = None, None
    for turn, start, tap in shifts(frames, taps):
        if turn != at:
            at, view = turn, turned(ids_pad, turn)
        mask_ref[tap * frames : (tap + 1) * frames, :] = jnp.where(
            view[start : start + frames] == ids_col, 1.0, 0.0
        )


def stack_kernel(q_ref, k_ref, v_ref, out_ref, sems):
    copies = [
        pltpu.make_async_copy(ref, out_ref.at[i], sems.at[i]) for i, ref in enumerate((q_ref, k_ref, v_ref))
    ]
    for copy in copies:
        copy.start()
    for copy in copies:
        copy.wait()


def own_kernel(
    qkv_ref, cot_ref, gain_row, kernel_ref, bias_row, same_ref, keep_ref, mask_ref,
    out_ref, back_ref, prob_ref, context_ref, sums_ref, gain_ref, bias_ref,
    pad_ref, normed_ref,
):
    q_ref, k_ref, v_ref = (qkv_ref.at[i] for i in range(3))
    frames, width = q_ref.shape
    taps = kernel_ref.shape[0]
    tiles = width // LANES
    clear_edges(pad_ref, frames)
    low = pair_masks(frames)
    gain_ref[...] = gain_row[...].reshape(1, width)
    bias_ref[...] = bias_row[...].reshape(1, width)
    bias, keep = same_ref[...], keep_ref[...]
    forward_all(q_ref, k_ref, v_ref, prob_ref, context_ref, bias, keep, low)
    normalize_all(context_ref, gain_ref, keep, normed_ref, pad_ref, PAD, frames)

    @pl.loop(0, tiles)
    def _(index):
        lanes = lanes_of(index)
        back_ref[:, lanes] = conv_forward(pad_ref, kernel_ref, bias_ref, mask_ref, frames, lanes)

    @pl.loop(0, tiles)
    def _(index):
        lanes = lanes_of(index)
        pre_act = back_ref[:, lanes]
        sig = gate(pre_act)
        out_ref[:, lanes] = (pre_act * sig * keep_ref[...]).astype(BF16)
        grad_pre = gate_grad(cot_ref[:, lanes].astype(F32) * keep_ref[...], pre_act, sig)
        conv_in = pad_ref[PAD : PAD + frames, lanes]
        pad_ref[PAD : PAD + frames, lanes] = grad_pre
        sums_ref[taps : taps + 1, lanes] = jnp.sum(grad_pre, 0, keepdims=True)

        def store(tap, value):
            sums_ref[tap : tap + 1, lanes] = value

        grad_in = conv_backward(pad_ref, conv_in, kernel_ref, mask_ref, frames, lanes, store)
        sums_ref[taps + 1 : taps + 2, lanes] = jnp.sum(grad_in * normed_ref[:, lanes], 0, keepdims=True)
        back_ref[:, lanes] = grad_in


def cross_forward_kernel(
    qkv_ref, other_ref, seg_ref, gain_ref, kernel_ref, bias_ref, add_ref,
    own_ref, next_ref, got_ref, prob_ref, context_ref, pre_ref,
    pad_ref, out_ref,
):
    frames, width = qkv_ref.shape[1:]
    tiles = width // LANES
    first, length = crossing(seg_ref, frames)
    pick = gather_matrix(first, length, frames)
    place = scatter_matrix(first, length, frames)
    shape = (frames, frames)
    bias = jnp.where(iota(shape, 1) < length, 0.0, NEG)
    keep = jnp.where(iota(shape, 0) < length, 1.0, 0.0)
    low = pair_masks(frames)
    clear_edges(pad_ref, frames)
    for which in range(3):
        for cols in wide(width):
            both = jnp.concatenate([qkv_ref[which, :, cols], other_ref[which, :, cols]], 0)
            got_ref[which, :, cols] = dot(pick, both, NN).astype(BF16)
    forward_all(*(got_ref.at[i] for i in range(3)), prob_ref, context_ref, bias, keep, low)
    normalize_all(context_ref, gain_ref, keep, None, pad_ref, PAD, frames)

    @pl.loop(0, tiles)
    def _(index):
        lanes = lanes_of(index)
        pre_act = conv_forward(pad_ref, kernel_ref, bias_ref, None, frames, lanes)
        pre_ref[:, lanes] = pre_act
        out_ref[:, lanes] = (pre_act * gate(pre_act)).astype(BF16)

    for cols in wide(width):
        placed = dot(place, out_ref[:, cols], NN).astype(BF16)
        own_ref[:, cols] = placed[:frames] + add_ref[:, cols]
        next_ref[:, cols] = placed[frames:]


def cross_conv_kernel(
    cot_ref, cotn_ref, seg_ref, gain_ref, kernel_ref, context_ref, pre_ref, part_ref,
    back_ref, mine_ref, other_ref,
    pad_ref, in_ref, normed_ref, sums_ref,
):
    frames, width = cot_ref.shape
    taps = kernel_ref.shape[0]
    tiles = width // LANES
    first, length = crossing(seg_ref, frames)
    pick = gather_matrix(first, length, frames)
    keep = jnp.where(iota((frames, frames), 0) < length, 1.0, 0.0)
    clear_edges(pad_ref, frames)
    for cols in wide(width):
        cotangent = dot(pick, jnp.concatenate([cot_ref[:, cols], cotn_ref[:, cols]], 0), NN)
        pre_act = pre_ref[:, cols]
        pad_ref[PAD : PAD + frames, cols] = gate_grad(cotangent, pre_act, gate(pre_act))
    normalize_all(context_ref, gain_ref, keep, normed_ref, in_ref, 0, frames)

    @pl.loop(0, tiles)
    def _(index):
        lanes = lanes_of(index)

        def store(row, value):
            sums_ref[row : row + 1, lanes] = part_ref[row : row + 1, lanes] + value

        store(taps, jnp.sum(pad_ref[PAD : PAD + frames, lanes], 0, keepdims=True))
        grad_in = conv_backward(pad_ref, in_ref[:, lanes], kernel_ref, None, frames, lanes, store)
        store(taps + 1, jnp.sum(grad_in * normed_ref[:, lanes], 0, keepdims=True))
        back_ref[:, lanes] = grad_in

    half = width // 2
    mine = lax.rem(lax.axis_index("seq"), 2)
    mine_ref[...] = sums_ref[:, pl.ds(pl.multiple_of(mine * half, LANES), half)].astype(BF16)
    other_ref[...] = sums_ref[:, pl.ds(pl.multiple_of((1 - mine) * half, LANES), half)].astype(BF16)


def cross_back_kernel(
    group, tiles, qkv_ref, prob_ref, context_ref, back_ref, gain_ref, seg_ref,
    own_ref, next_ref, grad_ref=None,
):
    q_ref, k_ref, v_ref = (qkv_ref.at[i] for i in range(3))
    frames = q_ref.shape[0]
    first, length = crossing(seg_ref, frames)
    place = scatter_matrix(first, length, frames)
    low = pair_masks(frames)
    if group == 0:
        keep = jnp.where(iota((frames, frames), 0) < length, 1.0, 0.0)
        norm_backward(context_ref, back_ref, gain_ref, keep, grad_ref, frames)
    else:
        grad_ref = back_ref
    for step in range(tiles):
        index = group * tiles + step
        lanes = slice(index * LANES, (index + 1) * LANES)
        dest = slice(step * LANES, (step + 1) * LANES)
        results = attend_back(
            q_ref[:, lanes], k_ref[:, lanes], v_ref[:, lanes], prob_ref[index],
            context_ref[:, lanes], grad_ref[:, lanes], low,
        )
        joined = jnp.concatenate([result.astype(BF16) for result in results], 1)
        placed = dot(place, joined, NN).astype(BF16)
        for which in range(3):
            cols = slice(which * LANES, (which + 1) * LANES)
            own_ref[which, :, dest] = placed[:frames, cols]
            next_ref[which, :, dest] = placed[frames:, cols]


def own_back_kernel(first, *refs):
    if first:
        qkv_ref, prob_ref, context_ref, back_ref, gain_ref, keep_ref, cross_ref, out_ref, grad_ref = refs
        frames = keep_ref.shape[0]
        norm_backward(context_ref, back_ref, gain_ref, keep_ref[...], grad_ref, frames)
    else:
        qkv_ref, prob_ref, context_ref, grad_ref, cross_ref, out_ref = refs
    frames, part = out_ref.shape[1:]
    low = pair_masks(frames)
    tiles = part // LANES
    for step in range(tiles):
        index = step if first else step + prob_ref.shape[0] - tiles
        lanes = slice(index * LANES, (index + 1) * LANES)
        dest = slice(step * LANES, (step + 1) * LANES)
        results = attend_back(
            *(qkv_ref[i, :, lanes] for i in range(3)), prob_ref[index],
            context_ref[:, lanes], grad_ref[:, lanes], low,
        )
        for which, result in enumerate(results):
            out_ref[which, :, dest] = result.astype(BF16) + cross_ref[which, :, dest]


def merge_kernel(*refs):
    ins, outs = refs[:-6], refs[-4:-1]
    out_both_ref, out_came_ref, conv_ref = refs[-6], refs[-5], refs[-1]
    conv_ref[...] = out_both_ref[...] + out_came_ref[...]
    half = len(ins) // 2
    start = 0
    for own_ref, came_ref in zip(ins[:half], ins[half:]):
        part = own_ref.shape[2]
        for which, out_ref in enumerate(outs):
            out_ref[:, start : start + part] = own_ref[which] + came_ref[which]
        start += part


def finish_kernel(scale, mine_ref, came_ref, gain_ref, kernel_ref, bias_ref):
    taps, width = kernel_ref.shape
    even = lax.rem(lax.axis_index("seq"), 2) == 0
    mine, came = mine_ref[...].astype(F32) * scale, came_ref[...].astype(F32) * scale
    total = jnp.concatenate([jnp.where(even, mine, came), jnp.where(even, came, mine)], 1)
    kernel_ref[...] = total[:taps]
    bias_ref[...] = total[taps : taps + 1].reshape(width)
    gain_ref[...] = total[taps + 1 : taps + 2].reshape(width)


def call(kernel, outs, scratch, flops, *args, space=pltpu.VMEM, limit=24):
    size = sum(a.size * a.dtype.itemsize for a in args) + sum(o.size * o.dtype.itemsize for o in outs)
    return pl.pallas_call(
        kernel,
        out_shape=outs,
        in_specs=[pl.BlockSpec(memory_space=space)] * len(args),
        out_specs=[pl.BlockSpec(memory_space=space)] * len(outs),
        scratch_shapes=scratch,
        compiler_params=pltpu.CompilerParams(vmem_limit_bytes=limit * 1024 * 1024),
        cost_estimate=pl.CostEstimate(flops=flops, bytes_accessed=size, transcendentals=0),
    )(*args)


def after(value, *others):
    return lax.optimization_barrier((value,) + others)[0]


def sum_steps():
    steps = {"seq": [], "dp": []}
    for axis, distances in steps.items():
        step = 1
        while step < lax.axis_size(axis):
            distances.append((axis, step))
            step *= 2
    return steps["seq"][:-1] + steps["dp"] + steps["seq"][-1:]


def exchange(sent, axis, step):
    return lax.ppermute(sent, axis, [(i, i ^ step) for i in range(lax.axis_size(axis))])


def added(sent, came):
    return (sent.astype(F32) + came.astype(F32)).astype(BF16)


def per_device(queries, keys, values, segment_ids, norm_gain, conv_kernel, conv_bias, cotangent):
    frames, width = queries.shape[1:]
    cot = cotangent[0]
    taps = conv_kernel.shape[0]
    tiles = width // LANES
    count = lax.axis_size("seq")
    to_left = [(i + 1, i) for i in range(count - 1)]
    to_right = [(i, i + 1) for i in range(count - 1)]
    (qkv,) = call(
        stack_kernel,
        [jax.ShapeDtypeStruct((3, frames, width), BF16)],
        [pltpu.SemaphoreType.DMA((3,))],
        10**6,
        queries[0], keys[0], values[0],
        space=pl.ANY,
        limit=60,
    )
    qkv_next = lax.ppermute(qkv, "seq", to_left)
    cot_next = lax.ppermute(cot, "seq", to_left)

    def sds(shape, dtype):
        return jax.ShapeDtypeStruct(shape, dtype)

    rows16 = sds((frames, width), BF16)
    rows32 = sds((frames, width), F32)
    three = sds((3, frames, width), BF16)
    probs = sds((tiles, frames, 2 * frames), BF16)
    half_sums = sds((taps + 2, width // 2), BF16)
    row = sds((1, width), F32)
    square = sds((frames, frames), F32)
    padded = pltpu.VMEM((frames + 2 * PAD, width), F32)
    plain = pltpu.VMEM((frames, width), F32)

    same, keep, masks = call(
        functools.partial(mask_kernel, taps),
        [square, square, sds((taps * frames, LANES), F32)],
        [pltpu.VMEM((frames + 2 * PAD, LANES), F32)],
        10**10,
        segment_ids,
    )
    out_own, back_own, prob_own, context_own, sums_own, gain, bias = call(
        own_kernel,
        [rows16, rows32, probs, rows16, sds((taps + 2, width), F32), row, row],
        [padded, plain],
        10**10,
        qkv, cot, norm_gain, conv_kernel, conv_bias, same, keep, masks,
    )
    out_both, out_next, got, prob_cross, context_cross, pre_cross = call(
        cross_forward_kernel,
        [rows16, rows16, three, probs, rows16, rows32],
        [padded, pltpu.VMEM((frames, width), BF16)],
        4 * 10**9,
        qkv, qkv_next, segment_ids, gain, conv_kernel, bias, out_own,
    )
    back_cross, mine, other = call(
        cross_conv_kernel,
        [rows32, half_sums, half_sums],
        [padded, plain, plain, pltpu.VMEM((taps + 2, width), F32)],
        4 * 10**9,
        cot, cot_next, segment_ids, gain, conv_kernel, context_cross, pre_cross, sums_own,
    )
    steps = sum_steps()
    came = exchange(other, *steps[0])
    out_came = lax.ppermute(after(out_next, mine), "seq", to_right)
    per_group = tiles // GROUPS
    piece = sds((3, frames, per_group * LANES), BF16)
    grad_cross = back_cross
    own_parts, came_parts, sent = [], [], mine
    for group in range(GROUPS):
        own_part, next_part, *rest = call(
            functools.partial(cross_back_kernel, group, per_group),
            [piece, piece] + [rows16] * (group == 0),
            [],
            2 * 10**9,
            got, prob_cross, context_cross, grad_cross, gain, segment_ids,
        )
        if group == 0:
            (grad_cross,) = rest
        own_parts.append(own_part)
        sent = added(sent, after(came, own_part))
        if group == 1:
            sent = after(sent, out_came)
        came = exchange(sent, *steps[group + 1])
        came_parts.append(lax.ppermute(after(next_part, sent), "seq", to_right))
    grads = []
    grad_own = back_own
    for group in range(GROUPS):
        extra = [gain, keep] if group == 0 else []
        part, *rest = call(
            functools.partial(own_back_kernel, group == 0),
            [piece] + [rows16] * (group == 0),
            [],
            3 * 10**9,
            qkv, prob_own, context_own, grad_own, *extra, own_parts[group],
        )
        if group == 0:
            (grad_own,) = rest
        grads.append(part)
        sent = added(sent, after(came, part, *came_parts[: group + 1]))
        came = exchange(sent, *steps[group + GROUPS + 1])
    for step in steps[2 * GROUPS + 1 :]:
        sent = added(sent, came)
        came = exchange(sent, *step)
    query_grad, key_grad, value_grad, conv_out = call(
        merge_kernel, [rows16] * 4, [], 10**9, *grads, *came_parts, out_both, out_came,
    )
    sent = added(sent, after(came, query_grad))
    came = exchange(sent, *steps[0])
    scale = (lax.axis_size("dp") * count * frames) ** (-0.5)
    gain_grad, kernel_grad, bias_grad = call(
        functools.partial(finish_kernel, scale),
        [sds((width,), F32), sds(conv_kernel.shape, F32), sds((width,), F32)],
        [],
        10**6,
        sent, came,
    )
    return (
        conv_out[None],
        query_grad[None],
        key_grad[None],
        value_grad[None],
        gain_grad,
        kernel_grad,
        bias_grad,
    )


def solution(mesh):
    rows = P("dp", "seq", None)
    return jax.shard_map(
        per_device,
        mesh=mesh,
        in_specs=(rows, rows, rows, P("dp", None), P(), P(), P(), rows),
        out_specs=(rows, rows, rows, rows, P(), P(), P()),
        check_vma=False,
    )
```

```python
import functools

import jax
import jax.numpy as jnp
from jax import lax
from jax.experimental import pallas as pl
from jax.experimental.pallas import tpu as pltpu
from jax.sharding import PartitionSpec as P

HEAD_DIM = 64
EPS = 1e-05
NEG = -1e30
LANES = 128
PAD = 16
GROUPS = 2
WIDE = 512
VMEM = pl.BlockSpec(memory_space=pltpu.VMEM)
F32 = jnp.float32
BF16 = jnp.bfloat16


def dot(a, b, dims):
    return lax.dot_general(a, b, (dims, ((), ())), preferred_element_type=F32)


NN = ((1,), (0,))
NT = ((1,), (1,))
TN = ((0,), (0,))


def lanes_of(index):
    return pl.ds(pl.multiple_of(index * LANES, LANES), LANES)


def block_ids(seg_ref, frames):
    me = lax.axis_index("seq")
    count = seg_ref.shape[1] // frames
    own = seg_ref[0:1, pl.ds(pl.multiple_of(me * frames, frames), frames)].astype(F32)
    before = jnp.maximum(me - 1, 0)
    after = jnp.minimum(me + 1, count - 1)
    prev = seg_ref[0:1, pl.ds(pl.multiple_of(before * frames, frames), frames)].astype(F32)
    following = seg_ref[0:1, pl.ds(pl.multiple_of(after * frames, frames), frames)].astype(F32)
    prev_last = jnp.where(me > 0, prev[:, frames - 1 :], -1.0)
    following = jnp.where(me < count - 1, following, -1.0)
    return own, following, prev_last, following[:, 0:1]


def crossing(seg_ref, frames):
    own, following, _, edge = block_ids(seg_ref, frames)
    left = jnp.sum(jnp.where((own == edge) & (edge >= 0.0), 1.0, 0.0), 1, keepdims=True)
    right = jnp.sum(jnp.where(following == edge, 1.0, 0.0), 1, keepdims=True)
    length = jnp.where(left > 0.0, left + right, 0.0)
    return frames - left, length


def iota(shape, axis):
    return lax.broadcasted_iota(jnp.int32, shape, axis).astype(F32)


def frame_of(shape, axis):
    place = lax.broadcasted_iota(jnp.int32, shape, axis)
    tiles = shape[axis] // 8
    return (lax.rem(place, 8) * tiles + lax.div(place, 8)).astype(F32)


def gather_matrix(first, length, frames):
    shape = (frames, 2 * frames)
    row = frame_of(shape, 0)
    return jnp.where((iota(shape, 1) == row + first) & (row < length), 1.0, 0.0).astype(BF16)


def scatter_matrix(first, length, frames):
    shape = (2 * frames, frames)
    col = frame_of(shape, 1)
    return jnp.where((iota(shape, 0) == col + first) & (col < length), 1.0, 0.0).astype(BF16)


def pair_masks(rows):
    low = lax.broadcasted_iota(jnp.int32, (rows, LANES), 1) < HEAD_DIM
    return low


def stack_pair(pair, low):
    zero = jnp.zeros_like(pair)
    return jnp.concatenate([jnp.where(low, pair, zero), jnp.where(low, zero, pair)], 0)


def attend(query, key, value, bias, keep, low):
    frames = query.shape[0]
    logits = dot(query * jnp.asarray(HEAD_DIM**-0.5, BF16), stack_pair(key, low), NT)
    halves = []
    for half in range(2):
        part = logits[:, half * frames : (half + 1) * frames] + bias
        top = jnp.max(part, 1, keepdims=True)
        power = jnp.exp(part - top)
        total = jnp.sum(power, 1, keepdims=True)
        halves.append((power * (1.0 / total)).astype(BF16))
    prob = jnp.concatenate(halves, 1)
    context = dot(prob, stack_pair(value, low), NN)
    return prob, (context * keep).astype(BF16)


def attend_back(query, key, value, prob, context, grad, low):
    frames = query.shape[0]
    scale = HEAD_DIM**-0.5
    grad_prob = dot(grad, stack_pair(value, low), NT)
    product = grad.astype(F32) * context.astype(F32)
    zero = jnp.zeros_like(product)
    deltas = (
        jnp.sum(jnp.where(low, product, zero), 1, keepdims=True),
        jnp.sum(jnp.where(low, zero, product), 1, keepdims=True),
    )
    parts = []
    for half in range(2):
        cols = slice(half * frames, (half + 1) * frames)
        parts.append(
            (prob[:, cols].astype(F32) * (grad_prob[:, cols] - deltas[half]) * scale).astype(BF16)
        )
    query_grad = dot(jnp.concatenate(parts, 1), stack_pair(key, low), NN)
    key_grad = dot(jnp.concatenate(parts, 0), stack_pair(query, low), TN)
    prob_rows = jnp.concatenate([prob[:, :frames], prob[:, frames:]], 0)
    value_grad = dot(prob_rows, stack_pair(grad, low), TN)
    return query_grad, key_grad, value_grad


def normalize(context):
    context = context.astype(F32)
    centred = context - jnp.mean(context, -1, keepdims=True)
    inv_std = lax.rsqrt(jnp.mean(centred * centred, -1, keepdims=True) + EPS)
    return centred * inv_std, inv_std


CHUNK = 32


def chunks(frames):
    return [pl.ds(start, CHUNK) for start in range(0, frames, CHUNK)]


def clear_edges(pad_ref, frames):
    zero = jnp.zeros((PAD, pad_ref.shape[1]), F32)
    pad_ref[0:PAD, :] = zero
    pad_ref[PAD + frames : 2 * PAD + frames, :] = zero


def shifts(frames, taps):
    base = PAD - taps // 2
    for turn in range(8):
        for start in range(0, 2 * PAD + 1, 8):
            tap = start + turn - base
            if 0 <= tap < taps:
                yield turn, start, tap


def turned(block, turn):
    rows = block.shape[0]
    return block if turn == 0 else pltpu.roll(block, rows - turn, 0)


def conv_forward(pad_ref, kernel_ref, bias_ref, mask_ref, frames, lanes):
    taps = kernel_ref.shape[0]
    block = pad_ref[:, lanes]
    total = jnp.broadcast_to(bias_ref[0:1, lanes], (frames, LANES))
    at, view = None, None
    for turn, start, tap in shifts(frames, taps):
        if turn != at:
            at, view = turn, turned(block, turn)
        term = view[start : start + frames]
        if mask_ref is not None:
            term = term * mask_ref[tap * frames : (tap + 1) * frames, :]
        total = total + kernel_ref[tap : tap + 1, lanes] * term
    return total


def conv_backward(pad_ref, conv_in, kernel_ref, mask_ref, frames, lanes, store):
    taps = kernel_ref.shape[0]
    block = pad_ref[:, lanes]
    total = jnp.zeros((frames, LANES), F32)
    at, view = None, None
    for turn, start, mirror in shifts(frames, taps):
        if turn != at:
            at, view = turn, turned(block, turn)
        tap = taps - 1 - mirror
        term = view[start : start + frames]
        if mask_ref is not None:
            term = term * mask_ref[mirror * frames : (mirror + 1) * frames, :]
        total = total + kernel_ref[tap : tap + 1, lanes] * term
        store(tap, jnp.sum(conv_in * term, 0, keepdims=True))
    return total


def phase_views(block, half_taps):
    tiles = block.shape[0] // 8
    row = lax.broadcasted_iota(jnp.int32, (8, LANES), 0)
    views = {}
    for j in range(tiles):
        tile = block[8 * j : 8 * j + 8]
        views[j] = tile
        if j - tiles >= -half_taps:
            views[j - tiles] = jnp.where(row >= 1, pltpu.roll(tile, 1, 0), 0.0)
        if j < half_taps:
            views[j + tiles] = jnp.where(row < 7, pltpu.roll(tile, 7, 0), 0.0)
    return views


def half_rate(views, taps, tiles):
    reach = tiles // 2 + (taps + 1) // 2 - 1
    low = -(taps // 2)
    middle = [views[low + 2 * n + 1] if low + 2 * n + 1 in views else None for n in range(reach)]
    before = [views[low + 2 * n] for n in range(reach)]
    after_ = [views.get(low + 2 * n + 2) for n in range(reach)]
    return middle, before, after_


def minus(a, b):
    if b is None:
        return a
    return -b if a is None else a - b


def phase_conv(block, weight, taps, start):
    tiles = block.shape[0] // 8
    middle, before, behind = half_rate(phase_views(block, taps // 2), taps, tiles)
    pairs = tiles // 2

    def run(values, weights, total):
        for s, w in enumerate(weights):
            for a in range(pairs):
                if values[a + s] is not None:
                    term = w * values[a + s]
                    total[a] = term if total[a] is None else total[a] + term
        return total

    even = [weight(t) for t in range(0, taps, 2)]
    odd = [weight(t) for t in range(1, taps, 2)]
    both = [e + o for e, o in zip(even, odd)] + even[len(odd) :]
    shared = run(middle, both, [start] * pairs)
    first = run([minus(b, m) for b, m in zip(before, middle)], even, list(shared))
    second = run([minus(b, m) for b, m in zip(behind, middle)], odd, list(shared))
    return jnp.concatenate([tile for pair in zip(first, second) for tile in pair], 0)


def phase_products(block, rows, taps, store):
    tiles = block.shape[0] // 8
    middle, before, behind = half_rate(phase_views(block, taps // 2), taps, tiles)
    pairs = tiles // 2
    even = [rows[16 * a : 16 * a + 8] for a in range(pairs)]
    odd = [rows[16 * a + 8 : 16 * a + 16] for a in range(pairs)]
    both = [e + o for e, o in zip(even, odd)]
    first = [minus(b, m) for b, m in zip(before, middle)]
    second = [minus(b, m) for b, m in zip(behind, middle)]

    def run(values, tiles_of, s):
        total = None
        for a in range(pairs):
            if values[a + s] is not None:
                term = tiles_of[a] * values[a + s]
                total = term if total is None else total + term
        return total

    for s in range((taps + 1) // 2):
        shared = run(middle, both, s)
        store(2 * s, jnp.sum(shared + run(first, even, s), 0, keepdims=True))
        if 2 * s + 1 < taps:
            store(2 * s + 1, jnp.sum(shared + run(second, odd, s), 0, keepdims=True))


def gate(pre_act):
    return 1.0 / (1.0 + jnp.exp(-pre_act))


def gate_grad(cotangent, pre_act, sig):
    return (cotangent * sig * (1.0 + pre_act * (1.0 - sig))).astype(BF16).astype(F32)


def norm_backward(context_ref, grad_ref, gain_ref, keep, out_ref, frames):
    for rows in chunks(frames):
        normed, inv_std = normalize(context_ref[rows, :])
        grad = grad_ref[rows, :] * gain_ref[0:1, :]
        centre = jnp.mean(grad, -1, keepdims=True)
        slope = jnp.mean(grad * normed, -1, keepdims=True)
        result = (grad - centre - normed * slope) * inv_std
        out_ref[rows, :] = jnp.where(keep[rows.start : rows.start + CHUNK, 0:1] > 0.0, result, 0.0).astype(BF16)


def wide(width):
    return [slice(start, start + WIDE) for start in range(0, width, WIDE)]


def forward_all(q_ref, k_ref, v_ref, prob_ref, context_ref, bias, keep, low):
    for index in range(q_ref.shape[1] // LANES):
        lanes = slice(index * LANES, (index + 1) * LANES)
        prob, context = attend(q_ref[:, lanes], k_ref[:, lanes], v_ref[:, lanes], bias, keep, low)
        prob_ref[index] = prob
        context_ref[:, lanes] = context


def normalize_all(context_ref, gain_ref, keep, in_ref, offset, frames):
    for rows in chunks(frames):
        normed, _ = normalize(context_ref[rows, :])
        normed = jnp.where(keep[rows.start : rows.start + CHUNK, 0:1] > 0.0, normed, 0.0)
        in_ref[pl.ds(offset + rows.start, CHUNK), :] = (
            (normed * gain_ref[0:1, :]).astype(BF16).astype(F32)
        )


def mask_kernel(taps, seg_ref, bias_ref, keep_ref, mask_ref, pad_ref):
    frames = bias_ref.shape[0]
    own, _, prev_last, next_first = block_ids(seg_ref, frames)
    ids = jnp.where((own == prev_last) | (own == next_first), -5.0, own)
    ids_row = jnp.broadcast_to(ids, (frames, frames))
    ids_col = jnp.transpose(ids_row)
    bias_ref[...] = jnp.where(ids_row == ids_col, 0.0, NEG)
    keep_ref[...] = jnp.where(ids_col >= 0.0, 1.0, 0.0)
    pad_ref[...] = jnp.full(pad_ref.shape, -9.0, F32)
    pad_ref[PAD : PAD + frames, :] = ids_col
    ids_pad = pad_ref[...]
    at, view = None, None
    for turn, start, tap in shifts(frames, taps):
        if turn != at:
            at, view = turn, turned(ids_pad, turn)
        mask_ref[tap * frames : (tap + 1) * frames, :] = jnp.where(
            view[start : start + frames] == ids_col, 1.0, 0.0
        )


def own_kernel(
    qkv_ref, cot_ref, gain_row, kernel_ref, bias_row, same_ref, keep_ref, mask_ref,
    out_ref, back_ref, prob_ref, context_ref, sums_ref, gain_ref, bias_ref,
    pad_ref,
):
    q_ref, k_ref, v_ref = (qkv_ref.at[i] for i in range(3))
    frames, width = q_ref.shape
    taps = kernel_ref.shape[0]
    tiles = width // LANES
    clear_edges(pad_ref, frames)
    low = pair_masks(frames)
    gain_ref[...] = gain_row[...].reshape(1, width)
    bias_ref[...] = bias_row[...].reshape(1, width)
    bias, keep = same_ref[...], keep_ref[...]
    forward_all(q_ref, k_ref, v_ref, prob_ref, context_ref, bias, keep, low)
    normalize_all(context_ref, gain_ref, keep, pad_ref, PAD, frames)

    @pl.loop(0, tiles)
    def _(index):
        lanes = lanes_of(index)
        back_ref[:, lanes] = conv_forward(pad_ref, kernel_ref, bias_ref, mask_ref, frames, lanes)

    @pl.loop(0, tiles)
    def _(index):
        lanes = lanes_of(index)
        pre_act = back_ref[:, lanes]
        sig = gate(pre_act)
        out_ref[:, lanes] = (pre_act * sig * keep_ref[...]).astype(BF16)
        grad_pre = gate_grad(cot_ref[:, lanes].astype(F32) * keep_ref[...], pre_act, sig)
        conv_in = pad_ref[PAD : PAD + frames, lanes]
        pad_ref[PAD : PAD + frames, lanes] = grad_pre
        sums_ref[taps : taps + 1, lanes] = jnp.sum(grad_pre, 0, keepdims=True)

        def store(tap, value):
            sums_ref[tap : tap + 1, lanes] = value

        grad_in = conv_backward(pad_ref, conv_in, kernel_ref, mask_ref, frames, lanes, store)
        back_ref[:, lanes] = grad_in


def cross_forward_kernel(
    qkv_ref, other_ref, seg_ref, gain_ref, kernel_ref, bias_ref, add_ref,
    own_ref, next_ref, got_ref, prob_ref, context_ref, pre_ref, in_ref,
    out_ref,
):
    frames, width = qkv_ref.shape[1:]
    taps = kernel_ref.shape[0]
    tiles = width // LANES
    first, length = crossing(seg_ref, frames)
    pick = gather_matrix(first, length, frames)
    place = scatter_matrix(first, length, frames)
    shape = (frames, frames)
    bias = jnp.where(frame_of(shape, 1) < length, 0.0, NEG)
    keep = jnp.where(frame_of(shape, 0) < length, 1.0, 0.0)
    low = pair_masks(frames)
    for which in range(3):
        for cols in wide(width):
            both = jnp.concatenate([qkv_ref[which, :, cols], other_ref[which, :, cols]], 0)
            got_ref[which, :, cols] = dot(pick, both, NN).astype(BF16)
    forward_all(*(got_ref.at[i] for i in range(3)), prob_ref, context_ref, bias, keep, low)
    normalize_all(context_ref, gain_ref, keep, in_ref, 0, frames)

    @pl.loop(0, tiles)
    def _(index):
        lanes = lanes_of(index)
        start = jnp.broadcast_to(bias_ref[0:1, lanes], (8, LANES))
        pre_act = phase_conv(in_ref[:, lanes], lambda t: kernel_ref[t : t + 1, lanes], taps, start)
        pre_ref[:, lanes] = pre_act
        out_ref[:, lanes] = (pre_act * gate(pre_act)).astype(BF16)

    for cols in wide(width):
        placed = dot(place, out_ref[:, cols], NN).astype(BF16)
        own_ref[:, cols] = placed[:frames] + add_ref[:, cols]
        next_ref[:, cols] = placed[frames:]


def cross_sums_kernel(
    cot_ref, cotn_ref, seg_ref, pre_ref, in_ref, part_ref,
    grad_ref, mine_ref, other_ref,
    sums_ref,
):
    frames, width = cot_ref.shape
    taps = part_ref.shape[0] - 1
    first, length = crossing(seg_ref, frames)
    pick = gather_matrix(first, length, frames)
    for cols in wide(width):
        cotangent = dot(pick, jnp.concatenate([cot_ref[:, cols], cotn_ref[:, cols]], 0), NN)
        pre_act = pre_ref[:, cols]
        grad_ref[:, cols] = gate_grad(cotangent, pre_act, gate(pre_act))

    @pl.loop(0, width // LANES)
    def _(index):
        lanes = lanes_of(index)

        def store(row, value):
            sums_ref[row : row + 1, lanes] = part_ref[row : row + 1, lanes] + value

        grad_pre = grad_ref[:, lanes]
        store(taps, jnp.sum(grad_pre, 0, keepdims=True))
        phase_products(
            grad_pre, in_ref[:, lanes], taps, lambda shift, value: store(taps - 1 - shift, value)
        )

    half = width // 2
    mine = lax.rem(lax.axis_index("seq"), 2)
    mine_ref[...] = sums_ref[:, pl.ds(pl.multiple_of(mine * half, LANES), half)].astype(BF16)
    other_ref[...] = sums_ref[:, pl.ds(pl.multiple_of((1 - mine) * half, LANES), half)].astype(BF16)


def cross_back_kernel(group, tiles, qkv_ref, prob_ref, context_ref, seg_ref, *refs):
    q_ref, k_ref, v_ref = (qkv_ref.at[i] for i in range(3))
    frames, width = q_ref.shape
    first, length = crossing(seg_ref, frames)
    place = scatter_matrix(first, length, frames)
    low = pair_masks(frames)
    if group == 0:
        gain_ref, kernel_ref, pre_ref, own_ref, next_ref, grad_ref, back_ref = refs
        taps = kernel_ref.shape[0]

        @pl.loop(0, width // LANES)
        def _(index):
            lanes = lanes_of(index)
            back_ref[:, lanes] = phase_conv(
                pre_ref[:, lanes], lambda t: kernel_ref[taps - 1 - t : taps - t, lanes], taps, None
            )

        keep = jnp.where(frame_of((frames, frames), 0) < length, 1.0, 0.0)
        norm_backward(context_ref, back_ref, gain_ref, keep, grad_ref, frames)
    else:
        grad_ref, own_ref, next_ref = refs
    for step in range(tiles):
        index = group * tiles + step
        lanes = slice(index * LANES, (index + 1) * LANES)
        dest = slice(step * LANES, (step + 1) * LANES)
        results = attend_back(
            q_ref[:, lanes], k_ref[:, lanes], v_ref[:, lanes], prob_ref[index],
            context_ref[:, lanes], grad_ref[:, lanes], low,
        )
        joined = jnp.concatenate([result.astype(BF16) for result in results], 1)
        placed = dot(place, joined, NN).astype(BF16)
        for which in range(3):
            cols = slice(which * LANES, (which + 1) * LANES)
            own_ref[which, :, dest] = placed[:frames, cols]
            next_ref[which, :, dest] = placed[frames:, cols]


def own_back_kernel(first, *refs):
    if first:
        qkv_ref, prob_ref, context_ref, back_ref, gain_ref, keep_ref, cross_ref, out_ref, grad_ref = refs
        frames = keep_ref.shape[0]
        norm_backward(context_ref, back_ref, gain_ref, keep_ref[...], grad_ref, frames)
    else:
        qkv_ref, prob_ref, context_ref, grad_ref, cross_ref, out_ref = refs
    frames, part = out_ref.shape[1:]
    low = pair_masks(frames)
    tiles = part // LANES
    for step in range(tiles):
        index = step if first else step + prob_ref.shape[0] - tiles
        lanes = slice(index * LANES, (index + 1) * LANES)
        dest = slice(step * LANES, (step + 1) * LANES)
        results = attend_back(
            *(qkv_ref[i, :, lanes] for i in range(3)), prob_ref[index],
            context_ref[:, lanes], grad_ref[:, lanes], low,
        )
        for which, result in enumerate(results):
            out_ref[which, :, dest] = result.astype(BF16) + cross_ref[which, :, dest]


def merge_kernel(*refs):
    ins, outs = refs[:-6], refs[-4:-1]
    out_both_ref, out_came_ref, conv_ref = refs[-6], refs[-5], refs[-1]
    conv_ref[...] = out_both_ref[...] + out_came_ref[...]
    half = len(ins) // 2
    start = 0
    for own_ref, came_ref in zip(ins[:half], ins[half:]):
        part = own_ref.shape[2]
        for which, out_ref in enumerate(outs):
            out_ref[:, start : start + part] = own_ref[which] + came_ref[which]
        start += part


def finish_kernel(scale, mine_ref, came_ref, weight_ref, norm_ref, gain_ref, kernel_ref, bias_ref):
    taps, width = kernel_ref.shape
    even = lax.rem(lax.axis_index("seq"), 2) == 0
    mine, came = mine_ref[...].astype(F32) * scale, came_ref[...].astype(F32) * scale
    total = jnp.concatenate([jnp.where(even, mine, came), jnp.where(even, came, mine)], 1)
    kernel_ref[...] = total[:taps]
    bias_ref[...] = total[taps : taps + 1].reshape(width)
    gain = jnp.sum(total[:taps] * weight_ref[...], 0, keepdims=True) / norm_ref[...]
    gain_ref[...] = gain.reshape(width)


def call(kernel, outs, scratch, flops, *args):
    size = sum(a.size * a.dtype.itemsize for a in args) + sum(o.size * o.dtype.itemsize for o in outs)
    return pl.pallas_call(
        kernel,
        out_shape=outs,
        in_specs=[VMEM] * len(args),
        out_specs=[VMEM] * len(outs),
        scratch_shapes=scratch,
        compiler_params=pltpu.CompilerParams(vmem_limit_bytes=24 * 1024 * 1024),
        cost_estimate=pl.CostEstimate(flops=flops, bytes_accessed=size, transcendentals=0),
    )(*args)


def after(value, *others):
    return lax.optimization_barrier((value,) + others)[0]


def sum_steps():
    steps = {"seq": [], "dp": []}
    for axis, distances in steps.items():
        step = 1
        while step < lax.axis_size(axis):
            distances.append((axis, step))
            step *= 2
    return steps["seq"][:-1] + steps["dp"] + steps["seq"][-1:]


def exchange(sent, axis, step):
    return lax.ppermute(sent, axis, [(i, i ^ step) for i in range(lax.axis_size(axis))])


def added(sent, came):
    return (sent.astype(F32) + came.astype(F32)).astype(BF16)


def per_device(queries, keys, values, segment_ids, norm_gain, conv_kernel, conv_bias, cotangent):
    frames, width = queries.shape[1:]
    cot = cotangent[0]
    taps = conv_kernel.shape[0]
    tiles = width // LANES
    count = lax.axis_size("seq")
    to_left = [(i + 1, i) for i in range(count - 1)]
    to_right = [(i, i + 1) for i in range(count - 1)]
    qkv = jnp.concatenate([queries[0], keys[0], values[0]], 0)
    qkv_next = lax.ppermute(qkv, "seq", to_left).reshape(3, frames, width)
    qkv = qkv.reshape(3, frames, width)
    cot_next = lax.ppermute(cot, "seq", to_left)

    def sds(shape, dtype):
        return jax.ShapeDtypeStruct(shape, dtype)

    rows16 = sds((frames, width), BF16)
    rows32 = sds((frames, width), F32)
    three = sds((3, frames, width), BF16)
    probs = sds((tiles, frames, 2 * frames), BF16)
    half_sums = sds((taps + 1, width // 2), BF16)
    row = sds((1, width), F32)
    square = sds((frames, frames), F32)
    padded = pltpu.VMEM((frames + 2 * PAD, width), F32)
    plain = pltpu.VMEM((frames, width), F32)

    same, keep, masks = call(
        functools.partial(mask_kernel, taps),
        [square, square, sds((taps * frames, LANES), F32)],
        [pltpu.VMEM((frames + 2 * PAD, LANES), F32)],
        10**10,
        segment_ids,
    )
    out_own, back_own, prob_own, context_own, sums_own, gain, bias = call(
        own_kernel,
        [rows16, rows32, probs, rows16, sds((taps + 1, width), F32), row, row],
        [padded],
        10**10,
        qkv, cot, norm_gain, conv_kernel, conv_bias, same, keep, masks,
    )
    out_both, out_next, got, prob_cross, context_cross, pre_cross, in_cross = call(
        cross_forward_kernel,
        [rows16, rows16, three, probs, rows16, rows32, rows32],
        [pltpu.VMEM((frames, width), BF16)],
        4 * 10**9,
        qkv, qkv_next, segment_ids, gain, conv_kernel, bias, out_own,
    )
    grad_pre, mine, other = call(
        cross_sums_kernel,
        [rows32, half_sums, half_sums],
        [pltpu.VMEM((taps + 1, width), F32)],
        3 * 10**9,
        cot, cot_next, segment_ids, pre_cross, in_cross, sums_own,
    )
    steps = sum_steps()
    came = exchange(other, *steps[0])
    out_came = lax.ppermute(after(out_next, mine), "seq", to_right)
    sent = added(mine, came)
    came = exchange(sent, *steps[1])
    per_group = tiles // GROUPS
    piece = sds((3, frames, per_group * LANES), BF16)
    own_parts, came_parts = [], []
    grad_pre = after(grad_pre, sent)
    for group in range(GROUPS):
        extra = [gain, conv_kernel, grad_pre] if group == 0 else [grad_cross]
        own_part, next_part, *rest = call(
            functools.partial(cross_back_kernel, group, per_group),
            [piece, piece] + [rows16] * (group == 0),
            [plain] * (group == 0),
            2 * 10**9 + 3 * 10**9 * (group == 0),
            got, prob_cross, context_cross, segment_ids, *extra,
        )
        if group == 0:
            (grad_cross,) = rest
        own_parts.append(own_part)
        sent = added(sent, after(came, own_part))
        if group == 1:
            sent = after(sent, out_came)
        came = exchange(sent, *steps[group + 2])
        came_parts.append(lax.ppermute(after(next_part, sent), "seq", to_right))
    grads = []
    grad_own = back_own
    for group in range(GROUPS):
        extra = [gain, keep] if group == 0 else []
        part, *rest = call(
            functools.partial(own_back_kernel, group == 0),
            [piece] + [rows16] * (group == 0),
            [],
            3 * 10**9,
            qkv, prob_own, context_own, after(grad_own, sent), *extra, own_parts[group],
        )
        if group == 0:
            (grad_own,) = rest
            for step in steps[4:]:
                sent = added(sent, after(came, part, came_parts[0]))
                came = exchange(sent, *step)
        grads.append(part)
    sent = added(sent, after(came, *grads, *came_parts))
    came = exchange(sent, *steps[0])
    query_grad, key_grad, value_grad, conv_out = call(
        merge_kernel, [rows16] * 4, [], 10**9, *grads, *came_parts, out_both, out_came,
    )
    scale = (lax.axis_size("dp") * count * frames) ** (-0.5)
    gain_grad, kernel_grad, bias_grad = call(
        functools.partial(finish_kernel, scale),
        [sds((width,), F32), sds(conv_kernel.shape, F32), sds((width,), F32)],
        [],
        10**6,
        sent, came, conv_kernel, gain,
    )
    return (
        conv_out[None],
        query_grad[None],
        key_grad[None],
        value_grad[None],
        gain_grad,
        kernel_grad,
        bias_grad,
    )


def solution(mesh):
    rows = P("dp", "seq", None)
    return jax.shard_map(
        per_device,
        mesh=mesh,
        in_specs=(rows, rows, rows, P("dp", None), P(), P(), P(), rows),
        out_specs=(rows, rows, rows, rows, P(), P(), P()),
        check_vma=False,
    )
```

```python
import functools

import jax
import jax.numpy as jnp
from jax import lax
from jax.experimental import pallas as pl
from jax.experimental.pallas import tpu as pltpu
from jax.sharding import PartitionSpec as P

HEAD_DIM = 64
EPS = 1e-05
NEG = -1e30
LANES = 128
PAD = 16
GROUPS = 2
WIDE = 512
BATCH = 6
VMEM = pl.BlockSpec(memory_space=pltpu.VMEM)
F32 = jnp.float32
BF16 = jnp.bfloat16


def dot(a, b, dims):
    return lax.dot_general(a, b, (dims, ((), ())), preferred_element_type=F32)


NN = ((1,), (0,))
NT = ((1,), (1,))
TN = ((0,), (0,))


def lanes_of(index):
    return pl.ds(pl.multiple_of(index * LANES, LANES), LANES)


def block_ids(seg_ref, frames):
    me = lax.axis_index("seq")
    count = seg_ref.shape[1] // frames
    own = seg_ref[0:1, pl.ds(pl.multiple_of(me * frames, frames), frames)].astype(F32)
    before = jnp.maximum(me - 1, 0)
    after = jnp.minimum(me + 1, count - 1)
    prev = seg_ref[0:1, pl.ds(pl.multiple_of(before * frames, frames), frames)].astype(F32)
    following = seg_ref[0:1, pl.ds(pl.multiple_of(after * frames, frames), frames)].astype(F32)
    prev_last = jnp.where(me > 0, prev[:, frames - 1 :], -1.0)
    following = jnp.where(me < count - 1, following, -1.0)
    return own, following, prev_last, following[:, 0:1]


def crossing(seg_ref, frames):
    own, following, _, edge = block_ids(seg_ref, frames)
    left = jnp.sum(jnp.where((own == edge) & (edge >= 0.0), 1.0, 0.0), 1, keepdims=True)
    right = jnp.sum(jnp.where(following == edge, 1.0, 0.0), 1, keepdims=True)
    length = jnp.where(left > 0.0, left + right, 0.0)
    return frames - left, length


def iota(shape, axis):
    return lax.broadcasted_iota(jnp.int32, shape, axis).astype(F32)


def frame_of(shape, axis):
    place = lax.broadcasted_iota(jnp.int32, shape, axis)
    tiles = shape[axis] // 8
    return (lax.rem(place, 8) * tiles + lax.div(place, 8)).astype(F32)


def gather_matrix(first, length, frames):
    shape = (frames, 2 * frames)
    row = frame_of(shape, 0)
    return jnp.where((iota(shape, 1) == row + first) & (row < length), 1.0, 0.0).astype(BF16)


def scatter_matrix(first, length, frames):
    shape = (2 * frames, frames)
    col = frame_of(shape, 1)
    return jnp.where((iota(shape, 0) == col + first) & (col < length), 1.0, 0.0).astype(BF16)


def pair_masks(rows):
    low = lax.broadcasted_iota(jnp.int32, (rows, LANES), 1) < HEAD_DIM
    return low


def stack_pair(pair, low):
    zero = jnp.zeros_like(pair)
    return jnp.concatenate([jnp.where(low, pair, zero), jnp.where(low, zero, pair)], 0)


def attend(query, key, value, bias, keep, low):
    frames = query.shape[0]
    logits = dot(query * jnp.asarray(HEAD_DIM**-0.5, BF16), stack_pair(key, low), NT)
    halves = []
    for half in range(2):
        part = logits[:, half * frames : (half + 1) * frames] + bias
        top = jnp.max(part, 1, keepdims=True)
        power = jnp.exp(part - top)
        total = jnp.sum(power, 1, keepdims=True)
        halves.append((power * (1.0 / total)).astype(BF16))
    prob = jnp.concatenate(halves, 1)
    context = dot(prob, stack_pair(value, low), NN)
    return prob, (context * keep).astype(BF16)


def attend_back(query, key, value, prob, context, grad, pairs, store):
    frames = context(0).shape[0]
    low = pair_masks(frames)
    scale = HEAD_DIM**-0.5
    grad_probs = [dot(grad(p), stack_pair(value(p), low), NT) for p in pairs]
    deltas = []
    for p in pairs:
        product = grad(p).astype(F32) * context(p).astype(F32)
        zero = jnp.zeros_like(product)
        deltas.append(
            (
                jnp.sum(jnp.where(low, product, zero), 1, keepdims=True),
                jnp.sum(jnp.where(low, zero, product), 1, keepdims=True),
            )
        )
    grad_logits = []
    for p, grad_prob, delta in zip(pairs, grad_probs, deltas):
        both = prob(p)
        halves = []
        for half in range(2):
            cols = slice(half * frames, (half + 1) * frames)
            halves.append(
                (both[:, cols].astype(F32) * (grad_prob[:, cols] - delta[half]) * scale).astype(BF16)
            )
        grad_logits.append(halves)
    for p, halves in zip(pairs, grad_logits):
        store(0, p, dot(jnp.concatenate(halves, 1), stack_pair(key(p), low), NN).astype(BF16))
    for p, halves in zip(pairs, grad_logits):
        store(1, p, dot(jnp.concatenate(halves, 0), stack_pair(query(p), low), TN).astype(BF16))
    for p in pairs:
        both = prob(p)
        rows = jnp.concatenate([both[:, :frames], both[:, frames:]], 0)
        store(2, p, dot(rows, stack_pair(grad(p), low), TN).astype(BF16))


def lanes_at(index):
    return slice(index * LANES, (index + 1) * LANES)


def back_all(qkv_ref, prob_ref, context_ref, grad_ref, first, pairs, store):
    for start in range(0, pairs, BATCH):
        attend_back(
            lambda p: qkv_ref[0, :, lanes_at(first + p)],
            lambda p: qkv_ref[1, :, lanes_at(first + p)],
            lambda p: qkv_ref[2, :, lanes_at(first + p)],
            lambda p: prob_ref[first + p],
            lambda p: context_ref[:, lanes_at(first + p)],
            lambda p: grad_ref[:, lanes_at(first + p)],
            range(start, min(start + BATCH, pairs)),
            store,
        )


def normalize(context):
    context = context.astype(F32)
    centred = context - jnp.mean(context, -1, keepdims=True)
    inv_std = lax.rsqrt(jnp.mean(centred * centred, -1, keepdims=True) + EPS)
    return centred * inv_std, inv_std


CHUNK = 32


def chunks(frames):
    return [pl.ds(start, CHUNK) for start in range(0, frames, CHUNK)]


def clear_edges(pad_ref, frames):
    zero = jnp.zeros((PAD, pad_ref.shape[1]), F32)
    pad_ref[0:PAD, :] = zero
    pad_ref[PAD + frames : 2 * PAD + frames, :] = zero


def shifts(frames, taps):
    base = PAD - taps // 2
    for turn in range(8):
        for start in range(0, 2 * PAD + 1, 8):
            tap = start + turn - base
            if 0 <= tap < taps:
                yield turn, start, tap


def turned(block, turn):
    rows = block.shape[0]
    return block if turn == 0 else pltpu.roll(block, rows - turn, 0)


def conv_forward(pad_ref, kernel_ref, bias_ref, mask_ref, frames, lanes):
    taps = kernel_ref.shape[0]
    block = pad_ref[:, lanes]
    total = jnp.broadcast_to(bias_ref[0:1, lanes], (frames, LANES))
    at, view = None, None
    for turn, start, tap in shifts(frames, taps):
        if turn != at:
            at, view = turn, turned(block, turn)
        term = view[start : start + frames]
        if mask_ref is not None:
            term = term * mask_ref[tap * frames : (tap + 1) * frames, :]
        total = total + kernel_ref[tap : tap + 1, lanes] * term
    return total


def conv_backward(pad_ref, conv_in, kernel_ref, mask_ref, frames, lanes, store):
    taps = kernel_ref.shape[0]
    block = pad_ref[:, lanes]
    total = jnp.zeros((frames, LANES), F32)
    at, view = None, None
    for turn, start, mirror in shifts(frames, taps):
        if turn != at:
            at, view = turn, turned(block, turn)
        tap = taps - 1 - mirror
        term = view[start : start + frames]
        if mask_ref is not None:
            term = term * mask_ref[mirror * frames : (mirror + 1) * frames, :]
        total = total + kernel_ref[tap : tap + 1, lanes] * term
        store(tap, jnp.sum(conv_in * term, 0, keepdims=True))
    return total


def phase_views(block, half_taps):
    tiles = block.shape[0] // 8
    row = lax.broadcasted_iota(jnp.int32, (8, LANES), 0)
    views = {}
    for j in range(tiles):
        tile = block[8 * j : 8 * j + 8]
        views[j] = tile
        if j - tiles >= -half_taps:
            views[j - tiles] = jnp.where(row >= 1, pltpu.roll(tile, 1, 0), 0.0)
        if j < half_taps:
            views[j + tiles] = jnp.where(row < 7, pltpu.roll(tile, 7, 0), 0.0)
    return views


def half_rate(views, taps, tiles):
    reach = tiles // 2 + (taps + 1) // 2 - 1
    low = -(taps // 2)
    middle = [views[low + 2 * n + 1] if low + 2 * n + 1 in views else None for n in range(reach)]
    before = [views[low + 2 * n] for n in range(reach)]
    after_ = [views.get(low + 2 * n + 2) for n in range(reach)]
    return middle, before, after_


def minus(a, b):
    if b is None:
        return a
    return -b if a is None else a - b


def phase_conv(block, weight, taps, start):
    tiles = block.shape[0] // 8
    middle, before, behind = half_rate(phase_views(block, taps // 2), taps, tiles)
    pairs = tiles // 2

    def run(values, weights, total):
        for s, w in enumerate(weights):
            for a in range(pairs):
                if values[a + s] is not None:
                    term = w * values[a + s]
                    total[a] = term if total[a] is None else total[a] + term
        return total

    even = [weight(t) for t in range(0, taps, 2)]
    odd = [weight(t) for t in range(1, taps, 2)]
    both = [e + o for e, o in zip(even, odd)] + even[len(odd) :]
    shared = run(middle, both, [start] * pairs)
    first = run([minus(b, m) for b, m in zip(before, middle)], even, list(shared))
    second = run([minus(b, m) for b, m in zip(behind, middle)], odd, list(shared))
    return jnp.concatenate([tile for pair in zip(first, second) for tile in pair], 0)


def phase_products(block, rows, taps, store):
    tiles = block.shape[0] // 8
    middle, before, behind = half_rate(phase_views(block, taps // 2), taps, tiles)
    pairs = tiles // 2
    even = [rows[16 * a : 16 * a + 8] for a in range(pairs)]
    odd = [rows[16 * a + 8 : 16 * a + 16] for a in range(pairs)]
    both = [e + o for e, o in zip(even, odd)]
    first = [minus(b, m) for b, m in zip(before, middle)]
    second = [minus(b, m) for b, m in zip(behind, middle)]

    def run(values, tiles_of, s):
        total = None
        for a in range(pairs):
            if values[a + s] is not None:
                term = tiles_of[a] * values[a + s]
                total = term if total is None else total + term
        return total

    for s in range((taps + 1) // 2):
        shared = run(middle, both, s)
        store(2 * s, jnp.sum(shared + run(first, even, s), 0, keepdims=True))
        if 2 * s + 1 < taps:
            store(2 * s + 1, jnp.sum(shared + run(second, odd, s), 0, keepdims=True))


def gate(pre_act):
    return 1.0 / (1.0 + jnp.exp(-pre_act))


def gate_grad(cotangent, pre_act, sig):
    return (cotangent * sig * (1.0 + pre_act * (1.0 - sig))).astype(BF16).astype(F32)


def norm_backward(context_ref, grad_ref, gain_ref, keep, out_ref, frames):
    for rows in chunks(frames):
        normed, inv_std = normalize(context_ref[rows, :])
        grad = grad_ref[rows, :] * gain_ref[0:1, :]
        centre = jnp.mean(grad, -1, keepdims=True)
        slope = jnp.mean(grad * normed, -1, keepdims=True)
        result = (grad - centre - normed * slope) * inv_std
        out_ref[rows, :] = jnp.where(keep[rows.start : rows.start + CHUNK, 0:1] > 0.0, result, 0.0).astype(BF16)


def wide(width):
    return [slice(start, start + WIDE) for start in range(0, width, WIDE)]


def forward_all(q_ref, k_ref, v_ref, prob_ref, context_ref, bias, keep, low):
    for index in range(q_ref.shape[1] // LANES):
        lanes = slice(index * LANES, (index + 1) * LANES)
        prob, context = attend(q_ref[:, lanes], k_ref[:, lanes], v_ref[:, lanes], bias, keep, low)
        prob_ref[index] = prob
        context_ref[:, lanes] = context


def normalize_all(context_ref, gain_ref, keep, in_ref, offset, frames):
    for rows in chunks(frames):
        normed, _ = normalize(context_ref[rows, :])
        normed = jnp.where(keep[rows.start : rows.start + CHUNK, 0:1] > 0.0, normed, 0.0)
        in_ref[pl.ds(offset + rows.start, CHUNK), :] = (
            (normed * gain_ref[0:1, :]).astype(BF16).astype(F32)
        )


def mask_kernel(taps, seg_ref, bias_ref, keep_ref, mask_ref, pad_ref):
    frames = bias_ref.shape[0]
    own, _, prev_last, next_first = block_ids(seg_ref, frames)
    ids = jnp.where((own == prev_last) | (own == next_first), -5.0, own)
    ids_row = jnp.broadcast_to(ids, (frames, frames))
    ids_col = jnp.transpose(ids_row)
    bias_ref[...] = jnp.where(ids_row == ids_col, 0.0, NEG)
    keep_ref[...] = jnp.where(ids_col >= 0.0, 1.0, 0.0)
    pad_ref[...] = jnp.full(pad_ref.shape, -9.0, F32)
    pad_ref[PAD : PAD + frames, :] = ids_col
    ids_pad = pad_ref[...]
    at, view = None, None
    for turn, start, tap in shifts(frames, taps):
        if turn != at:
            at, view = turn, turned(ids_pad, turn)
        mask_ref[tap * frames : (tap + 1) * frames, :] = jnp.where(
            view[start : start + frames] == ids_col, 1.0, 0.0
        )


def own_kernel(
    qkv_ref, cot_ref, gain_row, kernel_ref, bias_row, same_ref, keep_ref, mask_ref,
    out_ref, back_ref, prob_ref, context_ref, sums_ref, gain_ref, bias_ref,
    pad_ref,
):
    q_ref, k_ref, v_ref = (qkv_ref.at[i] for i in range(3))
    frames, width = q_ref.shape
    taps = kernel_ref.shape[0]
    tiles = width // LANES
    clear_edges(pad_ref, frames)
    low = pair_masks(frames)
    gain_ref[...] = gain_row[...].reshape(1, width)
    bias_ref[...] = bias_row[...].reshape(1, width)
    bias, keep = same_ref[...], keep_ref[...]
    forward_all(q_ref, k_ref, v_ref, prob_ref, context_ref, bias, keep, low)
    normalize_all(context_ref, gain_ref, keep, pad_ref, PAD, frames)

    @pl.loop(0, tiles)
    def _(index):
        lanes = lanes_of(index)
        back_ref[:, lanes] = conv_forward(pad_ref, kernel_ref, bias_ref, mask_ref, frames, lanes)

    @pl.loop(0, tiles)
    def _(index):
        lanes = lanes_of(index)
        pre_act = back_ref[:, lanes]
        sig = gate(pre_act)
        out_ref[:, lanes] = (pre_act * sig * keep_ref[...]).astype(BF16)
        grad_pre = gate_grad(cot_ref[:, lanes].astype(F32) * keep_ref[...], pre_act, sig)
        conv_in = pad_ref[PAD : PAD + frames, lanes]
        pad_ref[PAD : PAD + frames, lanes] = grad_pre
        sums_ref[taps : taps + 1, lanes] = jnp.sum(grad_pre, 0, keepdims=True)

        def store(tap, value):
            sums_ref[tap : tap + 1, lanes] = value

        grad_in = conv_backward(pad_ref, conv_in, kernel_ref, mask_ref, frames, lanes, store)
        back_ref[:, lanes] = grad_in


def cross_forward_kernel(
    qkv_ref, other_ref, seg_ref, gain_ref, kernel_ref, bias_ref, add_ref,
    own_ref, next_ref, got_ref, prob_ref, context_ref, pre_ref, in_ref,
    out_ref,
):
    frames, width = qkv_ref.shape[1:]
    taps = kernel_ref.shape[0]
    tiles = width // LANES
    first, length = crossing(seg_ref, frames)
    pick = gather_matrix(first, length, frames)
    place = scatter_matrix(first, length, frames)
    shape = (frames, frames)
    bias = jnp.where(frame_of(shape, 1) < length, 0.0, NEG)
    keep = jnp.where(frame_of(shape, 0) < length, 1.0, 0.0)
    low = pair_masks(frames)
    for which in range(3):
        for cols in wide(width):
            both = jnp.concatenate([qkv_ref[which, :, cols], other_ref[which, :, cols]], 0)
            got_ref[which, :, cols] = dot(pick, both, NN).astype(BF16)
    forward_all(*(got_ref.at[i] for i in range(3)), prob_ref, context_ref, bias, keep, low)
    normalize_all(context_ref, gain_ref, keep, in_ref, 0, frames)

    @pl.loop(0, tiles)
    def _(index):
        lanes = lanes_of(index)
        start = jnp.broadcast_to(bias_ref[0:1, lanes], (8, LANES))
        pre_act = phase_conv(in_ref[:, lanes], lambda t: kernel_ref[t : t + 1, lanes], taps, start)
        pre_ref[:, lanes] = pre_act
        out_ref[:, lanes] = (pre_act * gate(pre_act)).astype(BF16)

    for cols in wide(width):
        placed = dot(place, out_ref[:, cols], NN).astype(BF16)
        own_ref[:, cols] = placed[:frames] + add_ref[:, cols]
        next_ref[:, cols] = placed[frames:]


def cross_sums_kernel(
    cot_ref, cotn_ref, seg_ref, pre_ref, in_ref, part_ref,
    grad_ref, mine_ref, other_ref,
    sums_ref,
):
    frames, width = cot_ref.shape
    taps = part_ref.shape[0] - 1
    first, length = crossing(seg_ref, frames)
    pick = gather_matrix(first, length, frames)
    for cols in wide(width):
        cotangent = dot(pick, jnp.concatenate([cot_ref[:, cols], cotn_ref[:, cols]], 0), NN)
        pre_act = pre_ref[:, cols]
        grad_ref[:, cols] = gate_grad(cotangent, pre_act, gate(pre_act))

    @pl.loop(0, width // LANES)
    def _(index):
        lanes = lanes_of(index)

        def store(row, value):
            sums_ref[row : row + 1, lanes] = part_ref[row : row + 1, lanes] + value

        grad_pre = grad_ref[:, lanes]
        store(taps, jnp.sum(grad_pre, 0, keepdims=True))
        phase_products(
            grad_pre, in_ref[:, lanes], taps, lambda shift, value: store(taps - 1 - shift, value)
        )

    half = width // 2
    mine = lax.rem(lax.axis_index("seq"), 2)
    mine_ref[...] = sums_ref[:, pl.ds(pl.multiple_of(mine * half, LANES), half)].astype(BF16)
    other_ref[...] = sums_ref[:, pl.ds(pl.multiple_of((1 - mine) * half, LANES), half)].astype(BF16)


def cross_back_kernel(group, tiles, qkv_ref, prob_ref, context_ref, seg_ref, *refs):
    frames, width = context_ref.shape
    first, length = crossing(seg_ref, frames)
    place = scatter_matrix(first, length, frames)
    if group == 0:
        gain_ref, kernel_ref, pre_ref, own_ref, next_ref, grad_ref, result_ref, back_ref = refs
        taps = kernel_ref.shape[0]

        @pl.loop(0, width // LANES)
        def _(index):
            lanes = lanes_of(index)
            back_ref[:, lanes] = phase_conv(
                pre_ref[:, lanes], lambda t: kernel_ref[taps - 1 - t : taps - t, lanes], taps, None
            )

        keep = jnp.where(frame_of((frames, frames), 0) < length, 1.0, 0.0)
        norm_backward(context_ref, back_ref, gain_ref, keep, grad_ref, frames)
    else:
        grad_ref, own_ref, next_ref, result_ref = refs

    def store(which, pair, result):
        result_ref[which, :, lanes_at(pair)] = result

    back_all(qkv_ref, prob_ref, context_ref, grad_ref, group * tiles, tiles, store)
    for which in range(3):
        placed = dot(place, result_ref[which], NN).astype(BF16)
        own_ref[which] = placed[:frames]
        next_ref[which] = placed[frames:]


def own_back_kernel(
    qkv_ref, prob_ref, context_ref, back_ref, gain_ref, keep_ref, out_ref, grad_ref
):
    frames, width = context_ref.shape
    norm_backward(context_ref, back_ref, gain_ref, keep_ref[...], grad_ref, frames)

    def store(which, pair, result):
        out_ref[which, :, lanes_at(pair)] = result

    back_all(qkv_ref, prob_ref, context_ref, grad_ref, 0, width // LANES, store)


def merge_kernel(grads_ref, out_both_ref, out_came_ref, *refs):
    parts, outs = refs[:-4], refs[-4:]
    outs[3][...] = out_both_ref[...] + out_came_ref[...]
    start = 0
    for cross_ref, came_ref in zip(parts[::2], parts[1::2]):
        cols = slice(start, start + came_ref.shape[2])
        for which in range(3):
            outs[which][:, cols] = grads_ref[which, :, cols] + cross_ref[which] + came_ref[which]
        start = cols.stop


def finish_kernel(scale, mine_ref, came_ref, weight_ref, norm_ref, gain_ref, kernel_ref, bias_ref):
    taps, width = kernel_ref.shape
    even = lax.rem(lax.axis_index("seq"), 2) == 0
    mine, came = mine_ref[...].astype(F32) * scale, came_ref[...].astype(F32) * scale
    total = jnp.concatenate([jnp.where(even, mine, came), jnp.where(even, came, mine)], 1)
    kernel_ref[...] = total[:taps]
    bias_ref[...] = total[taps : taps + 1].reshape(width)
    gain = jnp.sum(total[:taps] * weight_ref[...], 0, keepdims=True) / norm_ref[...]
    gain_ref[...] = gain.reshape(width)


def call(kernel, outs, scratch, flops, *args):
    size = sum(a.size * a.dtype.itemsize for a in args) + sum(o.size * o.dtype.itemsize for o in outs)
    return pl.pallas_call(
        kernel,
        out_shape=outs,
        in_specs=[VMEM] * len(args),
        out_specs=[VMEM] * len(outs),
        scratch_shapes=scratch,
        compiler_params=pltpu.CompilerParams(vmem_limit_bytes=24 * 1024 * 1024),
        cost_estimate=pl.CostEstimate(flops=flops, bytes_accessed=size, transcendentals=0),
    )(*args)


def after(value, *others):
    return lax.optimization_barrier((value,) + others)[0]


def sum_steps():
    steps = {"seq": [], "dp": []}
    for axis, distances in steps.items():
        step = 1
        while step < lax.axis_size(axis):
            distances.append((axis, step))
            step *= 2
    return steps["seq"][:-1] + steps["dp"] + steps["seq"][-1:]


def exchange(sent, axis, step):
    return lax.ppermute(sent, axis, [(i, i ^ step) for i in range(lax.axis_size(axis))])


def added(sent, came):
    return (sent.astype(F32) + came.astype(F32)).astype(BF16)


def per_device(queries, keys, values, segment_ids, norm_gain, conv_kernel, conv_bias, cotangent):
    frames, width = queries.shape[1:]
    cot = cotangent[0]
    taps = conv_kernel.shape[0]
    tiles = width // LANES
    count = lax.axis_size("seq")
    to_left = [(i + 1, i) for i in range(count - 1)]
    to_right = [(i, i + 1) for i in range(count - 1)]
    qkv = jnp.concatenate([queries[0], keys[0], values[0]], 0)
    qkv_next = lax.ppermute(qkv, "seq", to_left).reshape(3, frames, width)
    qkv = qkv.reshape(3, frames, width)
    cot_next = lax.ppermute(cot, "seq", to_left)

    def sds(shape, dtype):
        return jax.ShapeDtypeStruct(shape, dtype)

    rows16 = sds((frames, width), BF16)
    rows32 = sds((frames, width), F32)
    three = sds((3, frames, width), BF16)
    probs = sds((tiles, frames, 2 * frames), BF16)
    half_sums = sds((taps + 1, width // 2), BF16)
    row = sds((1, width), F32)
    square = sds((frames, frames), F32)
    padded = pltpu.VMEM((frames + 2 * PAD, width), F32)
    plain = pltpu.VMEM((frames, width), F32)

    same, keep, masks = call(
        functools.partial(mask_kernel, taps),
        [square, square, sds((taps * frames, LANES), F32)],
        [pltpu.VMEM((frames + 2 * PAD, LANES), F32)],
        10**10,
        segment_ids,
    )
    out_own, back_own, prob_own, context_own, sums_own, gain, bias = call(
        own_kernel,
        [rows16, rows32, probs, rows16, sds((taps + 1, width), F32), row, row],
        [padded],
        10**10,
        qkv, cot, norm_gain, conv_kernel, conv_bias, same, keep, masks,
    )
    out_both, out_next, got, prob_cross, context_cross, pre_cross, in_cross = call(
        cross_forward_kernel,
        [rows16, rows16, three, probs, rows16, rows32, rows32],
        [pltpu.VMEM((frames, width), BF16)],
        4 * 10**9,
        qkv, qkv_next, segment_ids, gain, conv_kernel, bias, out_own,
    )
    grad_pre, mine, other = call(
        cross_sums_kernel,
        [rows32, half_sums, half_sums],
        [pltpu.VMEM((taps + 1, width), F32)],
        3 * 10**9,
        cot, cot_next, segment_ids, pre_cross, in_cross, sums_own,
    )
    steps = sum_steps()
    came = exchange(other, *steps[0])
    (grads_own,) = call(
        own_back_kernel,
        [three],
        [pltpu.VMEM((frames, width), BF16)],
        4 * 10**9,
        qkv, prob_own, context_own, after(back_own, mine), gain, keep,
    )
    sent = added(mine, after(came, grads_own))
    came = exchange(sent, *steps[1])
    out_came = lax.ppermute(after(out_next, sent), "seq", to_right)
    per_group = tiles // GROUPS
    piece = sds((3, frames, per_group * LANES), BF16)
    parts = []
    grad_pre = after(grad_pre, sent)
    for group in range(GROUPS):
        extra = [gain, conv_kernel, grad_pre] if group == 0 else [grad_cross]
        own_part, next_part, *rest = call(
            functools.partial(cross_back_kernel, group, per_group),
            [piece, piece] + [rows16] * (group == 0),
            [pltpu.VMEM(piece.shape, BF16)] + [plain] * (group == 0),
            2 * 10**9 + 3 * 10**9 * (group == 0),
            got, prob_cross, context_cross, segment_ids, *extra,
        )
        if group == 0:
            (grad_cross,) = rest
        sent = added(sent, after(came, own_part))
        if group == 1:
            sent = after(sent, out_came)
        came = exchange(sent, *steps[group + 2])
        parts += [own_part, lax.ppermute(after(next_part, sent), "seq", to_right)]
    for step in steps[GROUPS + 2 :]:
        sent = added(sent, after(came, parts[1]))
        came = exchange(sent, *step)
    sent = added(sent, after(came, parts[3]))
    came = exchange(sent, *steps[0])
    query_grad, key_grad, value_grad, conv_out = call(
        merge_kernel, [rows16] * 4, [], 10**9, grads_own, out_both, out_came, *parts,
    )
    scale = (lax.axis_size("dp") * count * frames) ** (-0.5)
    gain_grad, kernel_grad, bias_grad = call(
        functools.partial(finish_kernel, scale),
        [sds((width,), F32), sds(conv_kernel.shape, F32), sds((width,), F32)],
        [],
        10**6,
        sent, came, conv_kernel, gain,
    )
    return (
        conv_out[None],
        query_grad[None],
        key_grad[None],
        value_grad[None],
        gain_grad,
        kernel_grad,
        bias_grad,
    )


def solution(mesh):
    rows = P("dp", "seq", None)
    return jax.shard_map(
        per_device,
        mesh=mesh,
        in_specs=(rows, rows, rows, P("dp", None), P(), P(), P(), rows),
        out_specs=(rows, rows, rows, rows, P(), P(), P()),
        check_vma=False,
    )
```

```python
import functools

import jax
import jax.numpy as jnp
from jax import lax
from jax.experimental import pallas as pl
from jax.experimental.pallas import tpu as pltpu
from jax.sharding import PartitionSpec as P

HEAD_DIM = 64
EPS = 1e-05
NEG = -1e30
LANES = 128
PAD = 16
GROUPS = 2
WIDE = 512
BATCH = 6
VMEM = pl.BlockSpec(memory_space=pltpu.VMEM)
F32 = jnp.float32
BF16 = jnp.bfloat16


def dot(a, b, dims):
    return lax.dot_general(a, b, (dims, ((), ())), preferred_element_type=F32)


NN = ((1,), (0,))
NT = ((1,), (1,))
TN = ((0,), (0,))


def lanes_of(index):
    return pl.ds(pl.multiple_of(index * LANES, LANES), LANES)


def block_ids(seg_ref, frames):
    me = lax.axis_index("seq")
    count = seg_ref.shape[1] // frames
    own = seg_ref[0:1, pl.ds(pl.multiple_of(me * frames, frames), frames)].astype(F32)
    before = jnp.maximum(me - 1, 0)
    after = jnp.minimum(me + 1, count - 1)
    prev = seg_ref[0:1, pl.ds(pl.multiple_of(before * frames, frames), frames)].astype(F32)
    following = seg_ref[0:1, pl.ds(pl.multiple_of(after * frames, frames), frames)].astype(F32)
    prev_last = jnp.where(me > 0, prev[:, frames - 1 :], -1.0)
    following = jnp.where(me < count - 1, following, -1.0)
    return own, following, prev_last, following[:, 0:1]


def crossing(seg_ref, frames):
    own, following, _, edge = block_ids(seg_ref, frames)
    left = jnp.sum(jnp.where((own == edge) & (edge >= 0.0), 1.0, 0.0), 1, keepdims=True)
    right = jnp.sum(jnp.where(following == edge, 1.0, 0.0), 1, keepdims=True)
    length = jnp.where(left > 0.0, left + right, 0.0)
    return frames - left, length


def iota(shape, axis):
    return lax.broadcasted_iota(jnp.int32, shape, axis).astype(F32)


def frame_of(shape, axis):
    place = lax.broadcasted_iota(jnp.int32, shape, axis)
    tiles = shape[axis] // 8
    return (lax.rem(place, 8) * tiles + lax.div(place, 8)).astype(F32)


def gather_matrix(first, length, frames):
    shape = (frames, 2 * frames)
    row = frame_of(shape, 0)
    return jnp.where((iota(shape, 1) == row + first) & (row < length), 1.0, 0.0).astype(BF16)


def scatter_matrix(first, length, frames):
    shape = (2 * frames, frames)
    col = frame_of(shape, 1)
    return jnp.where((iota(shape, 0) == col + first) & (col < length), 1.0, 0.0).astype(BF16)


def pair_masks(rows):
    low = lax.broadcasted_iota(jnp.int32, (rows, LANES), 1) < HEAD_DIM
    return low


def stack_pair(pair, low):
    zero = jnp.zeros_like(pair)
    return jnp.concatenate([jnp.where(low, pair, zero), jnp.where(low, zero, pair)], 0)


def attend(query, key, value, bias, keep, low):
    frames = query.shape[0]
    logits = dot(query * jnp.asarray(HEAD_DIM**-0.5, BF16), stack_pair(key, low), NT)
    halves = []
    for half in range(2):
        part = logits[:, half * frames : (half + 1) * frames] + bias
        top = jnp.max(part, 1, keepdims=True)
        power = jnp.exp(part - top)
        total = jnp.sum(power, 1, keepdims=True)
        halves.append((power * (1.0 / total)).astype(BF16))
    prob = jnp.concatenate(halves, 1)
    context = dot(prob, stack_pair(value, low), NN)
    return prob, (context * keep).astype(BF16)


def attend_back(query, key, value, prob, context, grad, pairs, store):
    frames = context(0).shape[0]
    low = pair_masks(frames)
    scale = HEAD_DIM**-0.5
    grad_probs = [dot(grad(p), stack_pair(value(p), low), NT) for p in pairs]
    deltas = []
    for p in pairs:
        product = grad(p).astype(F32) * context(p).astype(F32)
        zero = jnp.zeros_like(product)
        deltas.append(
            (
                jnp.sum(jnp.where(low, product, zero), 1, keepdims=True),
                jnp.sum(jnp.where(low, zero, product), 1, keepdims=True),
            )
        )
    grad_logits = []
    for p, grad_prob, delta in zip(pairs, grad_probs, deltas):
        both = prob(p)
        halves = []
        for half in range(2):
            cols = slice(half * frames, (half + 1) * frames)
            halves.append(
                (both[:, cols].astype(F32) * (grad_prob[:, cols] - delta[half]) * scale).astype(BF16)
            )
        grad_logits.append(halves)
    for p, halves in zip(pairs, grad_logits):
        store(0, p, dot(jnp.concatenate(halves, 1), stack_pair(key(p), low), NN).astype(BF16))
    for p, halves in zip(pairs, grad_logits):
        store(1, p, dot(jnp.concatenate(halves, 0), stack_pair(query(p), low), TN).astype(BF16))
    for p in pairs:
        both = prob(p)
        rows = jnp.concatenate([both[:, :frames], both[:, frames:]], 0)
        store(2, p, dot(rows, stack_pair(grad(p), low), TN).astype(BF16))


def lanes_at(index):
    return slice(index * LANES, (index + 1) * LANES)


def back_all(q_ref, k_ref, v_ref, prob_ref, context_ref, grad_ref, first, pairs, store):
    for start in range(0, pairs, BATCH):
        attend_back(
            lambda p: q_ref[:, lanes_at(first + p)],
            lambda p: k_ref[:, lanes_at(first + p)],
            lambda p: v_ref[:, lanes_at(first + p)],
            lambda p: prob_ref[first + p],
            lambda p: context_ref[:, lanes_at(first + p)],
            lambda p: grad_ref[:, lanes_at(first + p)],
            range(start, min(start + BATCH, pairs)),
            store,
        )


def normalize(context):
    context = context.astype(F32)
    centred = context - jnp.mean(context, -1, keepdims=True)
    inv_std = lax.rsqrt(jnp.mean(centred * centred, -1, keepdims=True) + EPS)
    return centred * inv_std, inv_std


CHUNK = 32


def chunks(frames):
    return [pl.ds(start, CHUNK) for start in range(0, frames, CHUNK)]


def clear_edges(pad_ref, frames):
    zero = jnp.zeros((PAD, pad_ref.shape[1]), F32)
    pad_ref[0:PAD, :] = zero
    pad_ref[PAD + frames : 2 * PAD + frames, :] = zero


def shifts(frames, taps):
    base = PAD - taps // 2
    for turn in range(8):
        for start in range(0, 2 * PAD + 1, 8):
            tap = start + turn - base
            if 0 <= tap < taps:
                yield turn, start, tap


def turned(block, turn):
    rows = block.shape[0]
    return block if turn == 0 else pltpu.roll(block, rows - turn, 0)


def masked_conv(pad_ref, mask_ref, weight, taps, start, lanes, keep_view=None):
    frames = start.shape[0]
    block = pad_ref[:, lanes]
    total = start
    at, view = None, None
    for turn, row, tap in shifts(frames, taps):
        if turn != at:
            at, view = turn, turned(block, turn)
        term = view[row : row + frames] * mask_ref[tap * frames : (tap + 1) * frames, :]
        if keep_view is not None:
            keep_view(tap, term)
        total = total + weight(tap) * term
    return total


def phase_views(block, half_taps):
    tiles = block.shape[0] // 8
    row = lax.broadcasted_iota(jnp.int32, (8, LANES), 0)
    views = {}
    for j in range(tiles):
        tile = block[8 * j : 8 * j + 8]
        views[j] = tile
        if j - tiles >= -half_taps:
            views[j - tiles] = jnp.where(row >= 1, pltpu.roll(tile, 1, 0), 0.0)
        if j < half_taps:
            views[j + tiles] = jnp.where(row < 7, pltpu.roll(tile, 7, 0), 0.0)
    return views


def half_rate(views, taps, tiles):
    reach = tiles // 2 + (taps + 1) // 2 - 1
    low = -(taps // 2)
    middle = [views[low + 2 * n + 1] if low + 2 * n + 1 in views else None for n in range(reach)]
    before = [views[low + 2 * n] for n in range(reach)]
    after_ = [views.get(low + 2 * n + 2) for n in range(reach)]
    return middle, before, after_


def minus(a, b):
    if b is None:
        return a
    return -b if a is None else a - b


def phase_conv(block, weight, taps, start):
    tiles = block.shape[0] // 8
    middle, before, behind = half_rate(phase_views(block, taps // 2), taps, tiles)
    pairs = tiles // 2

    def run(values, weights, total):
        for s, w in enumerate(weights):
            for a in range(pairs):
                if values[a + s] is not None:
                    term = w * values[a + s]
                    total[a] = term if total[a] is None else total[a] + term
        return total

    even = [weight(t) for t in range(0, taps, 2)]
    odd = [weight(t) for t in range(1, taps, 2)]
    both = [e + o for e, o in zip(even, odd)] + even[len(odd) :]
    shared = run(middle, both, [start] * pairs)
    first = run([minus(b, m) for b, m in zip(before, middle)], even, list(shared))
    second = run([minus(b, m) for b, m in zip(behind, middle)], odd, list(shared))
    return jnp.concatenate([tile for pair in zip(first, second) for tile in pair], 0)


def phase_products(block, rows, taps, store):
    tiles = block.shape[0] // 8
    middle, before, behind = half_rate(phase_views(block, taps // 2), taps, tiles)
    pairs = tiles // 2
    even = [rows[16 * a : 16 * a + 8] for a in range(pairs)]
    odd = [rows[16 * a + 8 : 16 * a + 16] for a in range(pairs)]
    both = [e + o for e, o in zip(even, odd)]
    first = [minus(b, m) for b, m in zip(before, middle)]
    second = [minus(b, m) for b, m in zip(behind, middle)]

    def run(values, tiles_of, s):
        total = None
        for a in range(pairs):
            if values[a + s] is not None:
                term = tiles_of[a] * values[a + s]
                total = term if total is None else total + term
        return total

    for s in range((taps + 1) // 2):
        shared = run(middle, both, s)
        store(2 * s, jnp.sum(shared + run(first, even, s), 0, keepdims=True))
        if 2 * s + 1 < taps:
            store(2 * s + 1, jnp.sum(shared + run(second, odd, s), 0, keepdims=True))


def gate(pre_act):
    return 1.0 / (1.0 + jnp.exp(-pre_act))


def gate_grad(cotangent, pre_act, sig):
    return (cotangent * sig * (1.0 + pre_act * (1.0 - sig))).astype(BF16).astype(F32)


def norm_backward(context_ref, grad_ref, gain_ref, keep, out_ref, frames):
    for rows in chunks(frames):
        normed, inv_std = normalize(context_ref[rows, :])
        grad = grad_ref[rows, :] * gain_ref[0:1, :]
        centre = jnp.mean(grad, -1, keepdims=True)
        slope = jnp.mean(grad * normed, -1, keepdims=True)
        result = (grad - centre - normed * slope) * inv_std
        out_ref[rows, :] = jnp.where(keep[rows.start : rows.start + CHUNK, 0:1] > 0.0, result, 0.0).astype(BF16)


def wide(width):
    return [slice(start, start + WIDE) for start in range(0, width, WIDE)]


def forward_all(q_ref, k_ref, v_ref, prob_ref, context_ref, bias, keep, low):
    for index in range(q_ref.shape[1] // LANES):
        lanes = slice(index * LANES, (index + 1) * LANES)
        prob, context = attend(q_ref[:, lanes], k_ref[:, lanes], v_ref[:, lanes], bias, keep, low)
        prob_ref[index] = prob
        context_ref[:, lanes] = context


def normalize_all(context_ref, gain_ref, keep, in_ref, offset, frames):
    for rows in chunks(frames):
        normed, _ = normalize(context_ref[rows, :])
        normed = jnp.where(keep[rows.start : rows.start + CHUNK, 0:1] > 0.0, normed, 0.0)
        in_ref[pl.ds(offset + rows.start, CHUNK), :] = (
            (normed * gain_ref[0:1, :]).astype(BF16).astype(F32)
        )


def mask_kernel(taps, seg_ref, bias_ref, keep_ref, mask_ref, pad_ref):
    frames = bias_ref.shape[0]
    own, _, prev_last, next_first = block_ids(seg_ref, frames)
    ids = jnp.where((own == prev_last) | (own == next_first), -5.0, own)
    ids_row = jnp.broadcast_to(ids, (frames, frames))
    ids_col = jnp.transpose(ids_row)
    bias_ref[...] = jnp.where(ids_row == ids_col, 0.0, NEG)
    keep_ref[...] = jnp.where(ids_col >= 0.0, 1.0, 0.0)
    pad_ref[...] = jnp.full(pad_ref.shape, -9.0, F32)
    pad_ref[PAD : PAD + frames, :] = ids_col
    ids_pad = pad_ref[...]
    at, view = None, None
    for turn, start, tap in shifts(frames, taps):
        if turn != at:
            at, view = turn, turned(ids_pad, turn)
        mask_ref[tap * frames : (tap + 1) * frames, :] = jnp.where(
            view[start : start + frames] == ids_col, 1.0, 0.0
        )


def own_kernel(
    q_ref, kv_ref, cot_ref, gain_row, kernel_ref, bias_row, same_ref, keep_ref, mask_ref,
    out_ref, grad_ref, prob_ref, context_ref, sums_ref, gain_ref, bias_ref,
    pad_ref, view_ref,
):
    frames, width = q_ref.shape
    taps = kernel_ref.shape[0]
    clear_edges(pad_ref, frames)
    clear_edges(grad_ref, frames)
    low = pair_masks(frames)
    gain_ref[...] = gain_row[...].reshape(1, width)
    bias_ref[...] = bias_row[...].reshape(1, width)
    bias, keep = same_ref[...], keep_ref[...]
    forward_all(q_ref, kv_ref.at[0], kv_ref.at[1], prob_ref, context_ref, bias, keep, low)
    normalize_all(context_ref, gain_ref, keep, pad_ref, PAD, frames)

    @pl.loop(0, width // LANES)
    def _(index):
        lanes = lanes_of(index)

        def keep_view(tap, term):
            view_ref[tap] = term

        pre_act = masked_conv(
            pad_ref, mask_ref, lambda t: kernel_ref[t : t + 1, lanes], taps,
            jnp.broadcast_to(bias_ref[0:1, lanes], (frames, LANES)), lanes, keep_view,
        )
        sig = gate(pre_act)
        out_ref[:, lanes] = (pre_act * sig * keep_ref[...]).astype(BF16)
        grad_pre = gate_grad(cot_ref[:, lanes].astype(F32) * keep_ref[...], pre_act, sig)
        grad_ref[PAD : PAD + frames, lanes] = grad_pre
        sums_ref[taps : taps + 1, lanes] = jnp.sum(grad_pre, 0, keepdims=True)
        for tap in range(taps):
            sums_ref[tap : tap + 1, lanes] = jnp.sum(grad_pre * view_ref[tap], 0, keepdims=True)


def own_grad_kernel(
    pad_ref, context_ref, mask_ref, keep_ref, gain_ref, kernel_ref, grad_ref, back_ref
):
    frames, width = context_ref.shape
    taps = kernel_ref.shape[0]

    @pl.loop(0, width // LANES)
    def _(index):
        lanes = lanes_of(index)
        back_ref[:, lanes] = masked_conv(
            pad_ref, mask_ref, lambda t: kernel_ref[taps - 1 - t : taps - t, lanes], taps,
            jnp.zeros((frames, LANES), F32), lanes,
        )

    norm_backward(context_ref, back_ref, gain_ref, keep_ref[...], grad_ref, frames)


def cross_forward_kernel(
    q_ref, kv_ref, qn_ref, kvn_ref, seg_ref, gain_ref, kernel_ref, bias_ref, add_ref,
    own_ref, next_ref, got_ref, prob_ref, context_ref, pre_ref, in_ref,
    out_ref,
):
    frames, width = q_ref.shape
    taps = kernel_ref.shape[0]
    tiles = width // LANES
    first, length = crossing(seg_ref, frames)
    pick = gather_matrix(first, length, frames)
    place = scatter_matrix(first, length, frames)
    shape = (frames, frames)
    bias = jnp.where(frame_of(shape, 1) < length, 0.0, NEG)
    keep = jnp.where(frame_of(shape, 0) < length, 1.0, 0.0)
    low = pair_masks(frames)
    sources = ((q_ref, qn_ref), (kv_ref.at[0], kvn_ref.at[0]), (kv_ref.at[1], kvn_ref.at[1]))
    for which, (own, other) in enumerate(sources):
        for cols in wide(width):
            both = jnp.concatenate([own[:, cols], other[:, cols]], 0)
            got_ref[which, :, cols] = dot(pick, both, NN).astype(BF16)
    forward_all(*(got_ref.at[i] for i in range(3)), prob_ref, context_ref, bias, keep, low)
    normalize_all(context_ref, gain_ref, keep, in_ref, 0, frames)

    @pl.loop(0, tiles)
    def _(index):
        lanes = lanes_of(index)
        start = jnp.broadcast_to(bias_ref[0:1, lanes], (8, LANES))
        pre_act = phase_conv(in_ref[:, lanes], lambda t: kernel_ref[t : t + 1, lanes], taps, start)
        pre_ref[:, lanes] = pre_act
        out_ref[:, lanes] = (pre_act * gate(pre_act)).astype(BF16)

    for cols in wide(width):
        placed = dot(place, out_ref[:, cols], NN).astype(BF16)
        own_ref[:, cols] = placed[:frames] + add_ref[:, cols]
        next_ref[:, cols] = placed[frames:]


def cross_sums_kernel(
    cot_ref, cotn_ref, seg_ref, pre_ref, in_ref, part_ref,
    grad_ref, mine_ref, other_ref,
    sums_ref,
):
    frames, width = cot_ref.shape
    taps = part_ref.shape[0] - 1
    first, length = crossing(seg_ref, frames)
    pick = gather_matrix(first, length, frames)
    for cols in wide(width):
        cotangent = dot(pick, jnp.concatenate([cot_ref[:, cols], cotn_ref[:, cols]], 0), NN)
        pre_act = pre_ref[:, cols]
        grad_ref[:, cols] = gate_grad(cotangent, pre_act, gate(pre_act))

    @pl.loop(0, width // LANES)
    def _(index):
        lanes = lanes_of(index)

        def store(row, value):
            sums_ref[row : row + 1, lanes] = part_ref[row : row + 1, lanes] + value

        grad_pre = grad_ref[:, lanes]
        store(taps, jnp.sum(grad_pre, 0, keepdims=True))
        phase_products(
            grad_pre, in_ref[:, lanes], taps, lambda shift, value: store(taps - 1 - shift, value)
        )

    half = width // 2
    mine = lax.rem(lax.axis_index("seq"), 2)
    mine_ref[...] = sums_ref[:, pl.ds(pl.multiple_of(mine * half, LANES), half)].astype(BF16)
    other_ref[...] = sums_ref[:, pl.ds(pl.multiple_of((1 - mine) * half, LANES), half)].astype(BF16)


def cross_back_kernel(group, tiles, qkv_ref, prob_ref, context_ref, seg_ref, *refs):
    frames, width = context_ref.shape
    first, length = crossing(seg_ref, frames)
    place = scatter_matrix(first, length, frames)
    if group == 0:
        gain_ref, kernel_ref, pre_ref, own_ref, next_ref, grad_ref, result_ref, back_ref = refs
        taps = kernel_ref.shape[0]

        @pl.loop(0, width // LANES)
        def _(index):
            lanes = lanes_of(index)
            back_ref[:, lanes] = phase_conv(
                pre_ref[:, lanes], lambda t: kernel_ref[taps - 1 - t : taps - t, lanes], taps, None
            )

        keep = jnp.where(frame_of((frames, frames), 0) < length, 1.0, 0.0)
        norm_backward(context_ref, back_ref, gain_ref, keep, grad_ref, frames)
    else:
        grad_ref, own_ref, next_ref, result_ref = refs

    def store(which, pair, result):
        result_ref[which, :, lanes_at(pair)] = result

    got = [qkv_ref.at[i] for i in range(3)]
    back_all(*got, prob_ref, context_ref, grad_ref, group * tiles, tiles, store)
    for which in range(3):
        placed = dot(place, result_ref[which], NN).astype(BF16)
        own_ref[which] = placed[:frames]
        next_ref[which] = placed[frames:]


def own_back_kernel(q_ref, kv_ref, prob_ref, context_ref, grad_ref, out_ref):
    def store(which, pair, result):
        out_ref[which, :, lanes_at(pair)] = result

    back_all(
        q_ref, kv_ref.at[0], kv_ref.at[1], prob_ref, context_ref, grad_ref,
        0, q_ref.shape[1] // LANES, store,
    )


def merge_kernel(grads_ref, out_both_ref, out_came_ref, *refs):
    parts, outs = refs[:-4], refs[-4:]
    outs[3][...] = out_both_ref[...] + out_came_ref[...]
    start = 0
    for cross_ref, came_ref in zip(parts[::2], parts[1::2]):
        cols = slice(start, start + came_ref.shape[2])
        for which in range(3):
            outs[which][:, cols] = grads_ref[which, :, cols] + cross_ref[which] + came_ref[which]
        start = cols.stop


def finish_kernel(scale, mine_ref, came_ref, weight_ref, norm_ref, gain_ref, kernel_ref, bias_ref):
    taps, width = kernel_ref.shape
    even = lax.rem(lax.axis_index("seq"), 2) == 0
    mine, came = mine_ref[...].astype(F32) * scale, came_ref[...].astype(F32) * scale
    total = jnp.concatenate([jnp.where(even, mine, came), jnp.where(even, came, mine)], 1)
    kernel_ref[...] = total[:taps]
    bias_ref[...] = total[taps : taps + 1].reshape(width)
    gain = jnp.sum(total[:taps] * weight_ref[...], 0, keepdims=True) / norm_ref[...]
    gain_ref[...] = gain.reshape(width)


def call(kernel, outs, scratch, flops, *args, limit=24):
    size = sum(a.size * a.dtype.itemsize for a in args) + sum(o.size * o.dtype.itemsize for o in outs)
    return pl.pallas_call(
        kernel,
        out_shape=outs,
        in_specs=[VMEM] * len(args),
        out_specs=[VMEM] * len(outs),
        scratch_shapes=scratch,
        compiler_params=pltpu.CompilerParams(vmem_limit_bytes=limit * 1024 * 1024),
        cost_estimate=pl.CostEstimate(flops=flops, bytes_accessed=size, transcendentals=0),
    )(*args)


def after(value, *others):
    return lax.optimization_barrier((value,) + others)[0]


def sum_steps():
    steps = {"seq": [], "dp": []}
    for axis, distances in steps.items():
        step = 1
        while step < lax.axis_size(axis):
            distances.append((axis, step))
            step *= 2
    core, x, *rest = steps["seq"]
    return [core, x] + rest[1:] + steps["dp"] + rest[:1]


def exchange(sent, axis, step):
    return lax.ppermute(sent, axis, [(i, i ^ step) for i in range(lax.axis_size(axis))])


def added(sent, came):
    return (sent.astype(F32) + came.astype(F32)).astype(BF16)


def per_device(queries, keys, values, segment_ids, norm_gain, conv_kernel, conv_bias, cotangent):
    frames, width = queries.shape[1:]
    q, cot = queries[0], cotangent[0]
    taps = conv_kernel.shape[0]
    tiles = width // LANES
    count = lax.axis_size("seq")
    to_left = [(i + 1, i) for i in range(count - 1)]
    to_right = [(i, i + 1) for i in range(count - 1)]
    q_next = lax.ppermute(q, "seq", to_left)
    kv = jnp.concatenate([keys[0], values[0]], 0)
    kv_next = lax.ppermute(kv, "seq", to_left).reshape(2, frames, width)
    kv = kv.reshape(2, frames, width)
    cot_next = lax.ppermute(cot, "seq", to_left)

    def sds(shape, dtype):
        return jax.ShapeDtypeStruct(shape, dtype)

    rows16 = sds((frames, width), BF16)
    rows32 = sds((frames, width), F32)
    three = sds((3, frames, width), BF16)
    probs = sds((tiles, frames, 2 * frames), BF16)
    half_sums = sds((taps + 1, width // 2), BF16)
    row = sds((1, width), F32)
    square = sds((frames, frames), F32)
    padded = pltpu.VMEM((frames + 2 * PAD, width), F32)
    plain = pltpu.VMEM((frames, width), F32)

    same, keep, masks = call(
        functools.partial(mask_kernel, taps),
        [square, square, sds((taps * frames, LANES), F32)],
        [pltpu.VMEM((frames + 2 * PAD, LANES), F32)],
        10**10,
        segment_ids,
    )
    out_own, pre_own, prob_own, context_own, sums_own, gain, bias = call(
        own_kernel,
        [rows16, sds((frames + 2 * PAD, width), F32), probs, rows16, sds((taps + 1, width), F32), row, row],
        [padded, pltpu.VMEM((taps, frames, LANES), F32)],
        10**10,
        q, kv, cot, norm_gain, conv_kernel, conv_bias, same, keep, masks,
    )
    out_both, out_next, got, prob_cross, context_cross, pre_cross, in_cross = call(
        cross_forward_kernel,
        [rows16, rows16, three, probs, rows16, rows32, rows32],
        [pltpu.VMEM((frames, width), BF16)],
        4 * 10**9,
        q, kv, q_next, kv_next, segment_ids, gain, conv_kernel, bias, out_own,
    )
    grad_pre, mine, other = call(
        cross_sums_kernel,
        [rows32, half_sums, half_sums],
        [pltpu.VMEM((taps + 1, width), F32)],
        3 * 10**9,
        cot, cot_next, segment_ids, pre_cross, in_cross, sums_own,
    )
    steps = sum_steps()
    came = exchange(other, *steps[0])
    out_came = lax.ppermute(after(out_next, mine), "seq", to_right)
    sent = added(mine, came)
    came = exchange(sent, *steps[1])
    per_group = tiles // GROUPS
    piece = sds((3, frames, per_group * LANES), BF16)
    parts = []
    grad_pre = after(grad_pre, sent)
    for group in range(GROUPS):
        extra = [gain, conv_kernel, grad_pre] if group == 0 else [grad_cross]
        own_part, next_part, *rest = call(
            functools.partial(cross_back_kernel, group, per_group),
            [piece, piece] + [rows16] * (group == 0),
            [pltpu.VMEM(piece.shape, BF16)] + [plain] * (group == 0),
            2 * 10**9 + 3 * 10**9 * (group == 0),
            got, prob_cross, context_cross, segment_ids, *extra,
        )
        if group == 0:
            (grad_cross,) = rest
        sent = added(sent, after(came, own_part))
        if group == 0:
            sent = after(sent, out_came)
        came = exchange(sent, *steps[group + 2])
        parts += [own_part, lax.ppermute(after(next_part, sent), "seq", to_right)]
    (grad_own,) = call(
        own_grad_kernel,
        [rows16],
        [plain],
        4 * 10**9,
        after(pre_own, sent), context_own, masks, keep, gain, conv_kernel,
    )
    for step in steps[GROUPS + 2 :]:
        sent = added(sent, after(came, grad_own, parts[1]))
        came = exchange(sent, *step)
    (grads_own,) = call(
        own_back_kernel,
        [three],
        [],
        4 * 10**9,
        q, kv, prob_own, context_own, after(grad_own, sent),
    )
    sent = added(sent, after(came, grads_own, parts[3]))
    came = exchange(sent, *steps[0])
    query_grad, key_grad, value_grad, conv_out = call(
        merge_kernel, [rows16] * 4, [], 10**9, grads_own, out_both, out_came, *parts,
    )
    scale = (lax.axis_size("dp") * count * frames) ** (-0.5)
    gain_grad, kernel_grad, bias_grad = call(
        functools.partial(finish_kernel, scale),
        [sds((width,), F32), sds(conv_kernel.shape, F32), sds((width,), F32)],
        [],
        10**6,
        sent, came, conv_kernel, gain,
    )
    return (
        conv_out[None],
        query_grad[None],
        key_grad[None],
        value_grad[None],
        gain_grad,
        kernel_grad,
        bias_grad,
    )


def solution(mesh):
    rows = P("dp", "seq", None)
    return jax.shard_map(
        per_device,
        mesh=mesh,
        in_specs=(rows, rows, rows, P("dp", None), P(), P(), P(), rows),
        out_specs=(rows, rows, rows, rows, P(), P(), P()),
        check_vma=False,
    )
```

```python
import functools

import jax
import jax.numpy as jnp
from jax import lax
from jax.experimental import pallas as pl
from jax.experimental.pallas import tpu as pltpu
from jax.sharding import PartitionSpec as P

HEAD_DIM = 64
EPS = 1e-05
NEG = -1e30
LANES = 128
PAD = 16
GROUPS = 2
WIDE = 512
BATCH = 6
VMEM = pl.BlockSpec(memory_space=pltpu.VMEM)
F32 = jnp.float32
BF16 = jnp.bfloat16


def dot(a, b, dims):
    return lax.dot_general(a, b, (dims, ((), ())), preferred_element_type=F32)


NN = ((1,), (0,))
NT = ((1,), (1,))
TN = ((0,), (0,))


def lanes_of(index):
    return pl.ds(pl.multiple_of(index * LANES, LANES), LANES)


def block_ids(seg_ref, frames):
    me = lax.axis_index("seq")
    count = seg_ref.shape[1] // frames
    own = seg_ref[0:1, pl.ds(pl.multiple_of(me * frames, frames), frames)].astype(F32)
    before = jnp.maximum(me - 1, 0)
    after = jnp.minimum(me + 1, count - 1)
    prev = seg_ref[0:1, pl.ds(pl.multiple_of(before * frames, frames), frames)].astype(F32)
    following = seg_ref[0:1, pl.ds(pl.multiple_of(after * frames, frames), frames)].astype(F32)
    prev_last = jnp.where(me > 0, prev[:, frames - 1 :], -1.0)
    following = jnp.where(me < count - 1, following, -1.0)
    return own, following, prev_last, following[:, 0:1]


def crossing(seg_ref, frames):
    own, following, _, edge = block_ids(seg_ref, frames)
    left = jnp.sum(jnp.where((own == edge) & (edge >= 0.0), 1.0, 0.0), 1, keepdims=True)
    right = jnp.sum(jnp.where(following == edge, 1.0, 0.0), 1, keepdims=True)
    length = jnp.where(left > 0.0, left + right, 0.0)
    return frames - left, length


def iota(shape, axis):
    return lax.broadcasted_iota(jnp.int32, shape, axis).astype(F32)


def frame_of(shape, axis):
    place = lax.broadcasted_iota(jnp.int32, shape, axis)
    tiles = shape[axis] // 8
    return (lax.rem(place, 8) * tiles + lax.div(place, 8)).astype(F32)


def gather_matrix(first, length, frames):
    shape = (frames, 2 * frames)
    row = frame_of(shape, 0)
    return jnp.where((iota(shape, 1) == row + first) & (row < length), 1.0, 0.0).astype(BF16)


def scatter_matrix(first, length, frames):
    shape = (2 * frames, frames)
    col = frame_of(shape, 1)
    return jnp.where((iota(shape, 0) == col + first) & (col < length), 1.0, 0.0).astype(BF16)


def pair_masks(rows):
    low = lax.broadcasted_iota(jnp.int32, (rows, LANES), 1) < HEAD_DIM
    return low


def stack_pair(pair, low):
    zero = jnp.zeros_like(pair)
    return jnp.concatenate([jnp.where(low, pair, zero), jnp.where(low, zero, pair)], 0)


def attend(query, key, value, bias, keep, low):
    frames = query.shape[0]
    logits = dot(query * jnp.asarray(HEAD_DIM**-0.5, BF16), stack_pair(key, low), NT)
    halves = []
    for half in range(2):
        part = logits[:, half * frames : (half + 1) * frames] + bias
        top = jnp.max(part, 1, keepdims=True)
        power = jnp.exp(part - top)
        total = jnp.sum(power, 1, keepdims=True)
        halves.append((power * (1.0 / total)).astype(BF16))
    prob = jnp.concatenate(halves, 1)
    context = dot(prob, stack_pair(value, low), NN)
    return prob, (context * keep).astype(BF16)


def attend_back(query, key, value, prob, context, grad, pairs, store):
    frames = context(0).shape[0]
    low = pair_masks(frames)
    scale = HEAD_DIM**-0.5
    grad_probs = [dot(grad(p), stack_pair(value(p), low), NT) for p in pairs]
    deltas = []
    for p in pairs:
        product = grad(p).astype(F32) * context(p).astype(F32)
        zero = jnp.zeros_like(product)
        deltas.append(
            (
                jnp.sum(jnp.where(low, product, zero), 1, keepdims=True),
                jnp.sum(jnp.where(low, zero, product), 1, keepdims=True),
            )
        )
    grad_logits = []
    for p, grad_prob, delta in zip(pairs, grad_probs, deltas):
        both = prob(p)
        halves = []
        for half in range(2):
            cols = slice(half * frames, (half + 1) * frames)
            halves.append(
                (both[:, cols].astype(F32) * (grad_prob[:, cols] - delta[half]) * scale).astype(BF16)
            )
        grad_logits.append(halves)
    for p, halves in zip(pairs, grad_logits):
        store(0, p, dot(jnp.concatenate(halves, 1), stack_pair(key(p), low), NN).astype(BF16))
    for p, halves in zip(pairs, grad_logits):
        store(1, p, dot(jnp.concatenate(halves, 0), stack_pair(query(p), low), TN).astype(BF16))
    for p in pairs:
        both = prob(p)
        rows = jnp.concatenate([both[:, :frames], both[:, frames:]], 0)
        store(2, p, dot(rows, stack_pair(grad(p), low), TN).astype(BF16))


def lanes_at(index):
    return slice(index * LANES, (index + 1) * LANES)


def back_all(q_ref, k_ref, v_ref, prob_ref, context_ref, grad_ref, first, pairs, store):
    for start in range(0, pairs, BATCH):
        attend_back(
            lambda p: q_ref[:, lanes_at(first + p)],
            lambda p: k_ref[:, lanes_at(first + p)],
            lambda p: v_ref[:, lanes_at(first + p)],
            lambda p: prob_ref[first + p],
            lambda p: context_ref[:, lanes_at(first + p)],
            lambda p: grad_ref[:, lanes_at(first + p)],
            range(start, min(start + BATCH, pairs)),
            store,
        )


def normalize(context):
    context = context.astype(F32)
    centred = context - jnp.mean(context, -1, keepdims=True)
    inv_std = lax.rsqrt(jnp.mean(centred * centred, -1, keepdims=True) + EPS)
    return centred * inv_std, inv_std


CHUNK = 32


def chunks(frames):
    return [pl.ds(start, CHUNK) for start in range(0, frames, CHUNK)]


def clear_edges(pad_ref, frames):
    zero = jnp.zeros((PAD, pad_ref.shape[1]), F32)
    pad_ref[0:PAD, :] = zero
    pad_ref[PAD + frames : 2 * PAD + frames, :] = zero


def shifts(frames, taps):
    base = PAD - taps // 2
    for turn in range(8):
        for start in range(0, 2 * PAD + 1, 8):
            tap = start + turn - base
            if 0 <= tap < taps:
                yield turn, start, tap


def turned(block, turn):
    rows = block.shape[0]
    return block if turn == 0 else pltpu.roll(block, rows - turn, 0)


def masked_conv(pad_ref, mask_ref, weight, taps, start, lanes, keep_view=None):
    frames = start.shape[0]
    block = pad_ref[:, lanes]
    total = start
    at, view = None, None
    for turn, row, tap in shifts(frames, taps):
        if turn != at:
            at, view = turn, turned(block, turn)
        term = view[row : row + frames] * mask_ref[tap * frames : (tap + 1) * frames, :]
        if keep_view is not None:
            keep_view(tap, term)
        total = total + weight(tap) * term
    return total


def phase_views(block, half_taps):
    tiles = block.shape[0] // 8
    row = lax.broadcasted_iota(jnp.int32, (8, LANES), 0)
    views = {}
    for j in range(tiles):
        tile = block[8 * j : 8 * j + 8]
        views[j] = tile
        if j - tiles >= -half_taps:
            views[j - tiles] = jnp.where(row >= 1, pltpu.roll(tile, 1, 0), 0.0)
        if j < half_taps:
            views[j + tiles] = jnp.where(row < 7, pltpu.roll(tile, 7, 0), 0.0)
    return views


def half_rate(views, taps, tiles):
    reach = tiles // 2 + (taps + 1) // 2 - 1
    low = -(taps // 2)
    middle = [views[low + 2 * n + 1] if low + 2 * n + 1 in views else None for n in range(reach)]
    before = [views[low + 2 * n] for n in range(reach)]
    after_ = [views.get(low + 2 * n + 2) for n in range(reach)]
    return middle, before, after_


def minus(a, b):
    if b is None:
        return a
    return -b if a is None else a - b


def phase_conv(block, weight, taps, start):
    tiles = block.shape[0] // 8
    middle, before, behind = half_rate(phase_views(block, taps // 2), taps, tiles)
    pairs = tiles // 2

    def run(values, weights, total):
        for s, w in enumerate(weights):
            for a in range(pairs):
                if values[a + s] is not None:
                    term = w * values[a + s]
                    total[a] = term if total[a] is None else total[a] + term
        return total

    even = [weight(t) for t in range(0, taps, 2)]
    odd = [weight(t) for t in range(1, taps, 2)]
    both = [e + o for e, o in zip(even, odd)] + even[len(odd) :]
    shared = run(middle, both, [start] * pairs)
    first = run([minus(b, m) for b, m in zip(before, middle)], even, list(shared))
    second = run([minus(b, m) for b, m in zip(behind, middle)], odd, list(shared))
    return jnp.concatenate([tile for pair in zip(first, second) for tile in pair], 0)


def phase_products(block, rows, taps, store):
    tiles = block.shape[0] // 8
    middle, before, behind = half_rate(phase_views(block, taps // 2), taps, tiles)
    pairs = tiles // 2
    even = [rows[16 * a : 16 * a + 8] for a in range(pairs)]
    odd = [rows[16 * a + 8 : 16 * a + 16] for a in range(pairs)]
    both = [e + o for e, o in zip(even, odd)]
    first = [minus(b, m) for b, m in zip(before, middle)]
    second = [minus(b, m) for b, m in zip(behind, middle)]

    def run(values, tiles_of, s):
        total = None
        for a in range(pairs):
            if values[a + s] is not None:
                term = tiles_of[a] * values[a + s]
                total = term if total is None else total + term
        return total

    for s in range((taps + 1) // 2):
        shared = run(middle, both, s)
        store(2 * s, jnp.sum(shared + run(first, even, s), 0, keepdims=True))
        if 2 * s + 1 < taps:
            store(2 * s + 1, jnp.sum(shared + run(second, odd, s), 0, keepdims=True))


def gate(pre_act):
    return 1.0 / (1.0 + jnp.exp(-pre_act))


def gate_grad(cotangent, pre_act, sig):
    return (cotangent * sig * (1.0 + pre_act * (1.0 - sig))).astype(BF16).astype(F32)


def norm_backward(context_ref, grad_ref, gain_ref, keep, out_ref, frames):
    for rows in chunks(frames):
        normed, inv_std = normalize(context_ref[rows, :])
        grad = grad_ref[rows, :] * gain_ref[0:1, :]
        centre = jnp.mean(grad, -1, keepdims=True)
        slope = jnp.mean(grad * normed, -1, keepdims=True)
        result = (grad - centre - normed * slope) * inv_std
        out_ref[rows, :] = jnp.where(keep[rows.start : rows.start + CHUNK, 0:1] > 0.0, result, 0.0).astype(BF16)


def wide(width):
    return [slice(start, start + WIDE) for start in range(0, width, WIDE)]


def forward_all(q_ref, k_ref, v_ref, prob_ref, context_ref, bias, keep, low):
    for index in range(q_ref.shape[1] // LANES):
        lanes = slice(index * LANES, (index + 1) * LANES)
        prob, context = attend(q_ref[:, lanes], k_ref[:, lanes], v_ref[:, lanes], bias, keep, low)
        prob_ref[index] = prob
        context_ref[:, lanes] = context


def normalize_all(context_ref, gain_ref, keep, in_ref, offset, frames):
    for rows in chunks(frames):
        normed, _ = normalize(context_ref[rows, :])
        normed = jnp.where(keep[rows.start : rows.start + CHUNK, 0:1] > 0.0, normed, 0.0)
        in_ref[pl.ds(offset + rows.start, CHUNK), :] = (
            (normed * gain_ref[0:1, :]).astype(BF16).astype(F32)
        )


def mask_kernel(taps, seg_ref, bias_ref, keep_ref, mask_ref, pad_ref):
    frames = bias_ref.shape[0]
    own, _, prev_last, next_first = block_ids(seg_ref, frames)
    ids = jnp.where((own == prev_last) | (own == next_first), -5.0, own)
    ids_row = jnp.broadcast_to(ids, (frames, frames))
    ids_col = jnp.transpose(ids_row)
    bias_ref[...] = jnp.where(ids_row == ids_col, 0.0, NEG)
    keep_ref[...] = jnp.where(ids_col >= 0.0, 1.0, 0.0)
    pad_ref[...] = jnp.full(pad_ref.shape, -9.0, F32)
    pad_ref[PAD : PAD + frames, :] = ids_col
    ids_pad = pad_ref[...]
    at, view = None, None
    for turn, start, tap in shifts(frames, taps):
        if turn != at:
            at, view = turn, turned(ids_pad, turn)
        mask_ref[tap * frames : (tap + 1) * frames, :] = jnp.where(
            view[start : start + frames] == ids_col, 1.0, 0.0
        )


def own_kernel(
    q_ref, kv_ref, cot_ref, gain_row, kernel_ref, bias_row, same_ref, keep_ref, mask_ref,
    out_ref, grad_ref, prob_ref, context_ref, sums_ref, gain_ref, bias_ref,
    pad_ref, view_ref,
):
    frames, width = q_ref.shape
    taps = kernel_ref.shape[0]
    clear_edges(pad_ref, frames)
    clear_edges(grad_ref, frames)
    low = pair_masks(frames)
    gain_ref[...] = gain_row[...].reshape(1, width)
    bias_ref[...] = bias_row[...].reshape(1, width)
    bias, keep = same_ref[...], keep_ref[...]
    forward_all(q_ref, kv_ref.at[0], kv_ref.at[1], prob_ref, context_ref, bias, keep, low)
    normalize_all(context_ref, gain_ref, keep, pad_ref, PAD, frames)

    @pl.loop(0, width // LANES)
    def _(index):
        lanes = lanes_of(index)

        def keep_view(tap, term):
            view_ref[tap] = term

        pre_act = masked_conv(
            pad_ref, mask_ref, lambda t: kernel_ref[t : t + 1, lanes], taps,
            jnp.broadcast_to(bias_ref[0:1, lanes], (frames, LANES)), lanes, keep_view,
        )
        sig = gate(pre_act)
        out_ref[:, lanes] = (pre_act * sig * keep_ref[...]).astype(BF16)
        grad_pre = gate_grad(cot_ref[:, lanes].astype(F32) * keep_ref[...], pre_act, sig)
        grad_ref[PAD : PAD + frames, lanes] = grad_pre
        sums_ref[taps : taps + 1, lanes] = jnp.sum(grad_pre, 0, keepdims=True)
        for tap in range(taps):
            sums_ref[tap : tap + 1, lanes] = jnp.sum(grad_pre * view_ref[tap], 0, keepdims=True)


def own_grad_kernel(
    pad_ref, context_ref, mask_ref, keep_ref, gain_ref, kernel_ref, grad_ref, back_ref
):
    frames, width = context_ref.shape
    taps = kernel_ref.shape[0]

    @pl.loop(0, width // LANES)
    def _(index):
        lanes = lanes_of(index)
        back_ref[:, lanes] = masked_conv(
            pad_ref, mask_ref, lambda t: kernel_ref[taps - 1 - t : taps - t, lanes], taps,
            jnp.zeros((frames, LANES), F32), lanes,
        )

    norm_backward(context_ref, back_ref, gain_ref, keep_ref[...], grad_ref, frames)


def cross_forward_kernel(
    q_ref, kv_ref, qn_ref, kvn_ref, seg_ref, gain_ref, kernel_ref, bias_ref, add_ref,
    own_ref, next_ref, got_ref, prob_ref, context_ref, pre_ref, in_ref,
    out_ref,
):
    frames, width = q_ref.shape
    taps = kernel_ref.shape[0]
    tiles = width // LANES
    first, length = crossing(seg_ref, frames)
    pick = gather_matrix(first, length, frames)
    place = scatter_matrix(first, length, frames)
    shape = (frames, frames)
    bias = jnp.where(frame_of(shape, 1) < length, 0.0, NEG)
    keep = jnp.where(frame_of(shape, 0) < length, 1.0, 0.0)
    low = pair_masks(frames)
    sources = ((q_ref, qn_ref), (kv_ref.at[0], kvn_ref.at[0]), (kv_ref.at[1], kvn_ref.at[1]))
    for which, (own, other) in enumerate(sources):
        for cols in wide(width):
            both = jnp.concatenate([own[:, cols], other[:, cols]], 0)
            got_ref[which, :, cols] = dot(pick, both, NN).astype(BF16)
    forward_all(*(got_ref.at[i] for i in range(3)), prob_ref, context_ref, bias, keep, low)
    normalize_all(context_ref, gain_ref, keep, in_ref, 0, frames)

    @pl.loop(0, tiles)
    def _(index):
        lanes = lanes_of(index)
        start = jnp.broadcast_to(bias_ref[0:1, lanes], (8, LANES))
        pre_act = phase_conv(in_ref[:, lanes], lambda t: kernel_ref[t : t + 1, lanes], taps, start)
        pre_ref[:, lanes] = pre_act
        out_ref[:, lanes] = (pre_act * gate(pre_act)).astype(BF16)

    for cols in wide(width):
        placed = dot(place, out_ref[:, cols], NN).astype(BF16)
        own_ref[:, cols] = placed[:frames] + add_ref[:, cols]
        next_ref[:, cols] = placed[frames:]


def cross_sums_kernel(
    cot_ref, cotn_ref, seg_ref, pre_ref, in_ref, part_ref,
    grad_ref, mine_ref, other_ref,
    sums_ref,
):
    frames, width = cot_ref.shape
    taps = part_ref.shape[0] - 1
    first, length = crossing(seg_ref, frames)
    pick = gather_matrix(first, length, frames)
    for cols in wide(width):
        cotangent = dot(pick, jnp.concatenate([cot_ref[:, cols], cotn_ref[:, cols]], 0), NN)
        pre_act = pre_ref[:, cols]
        grad_ref[:, cols] = gate_grad(cotangent, pre_act, gate(pre_act))

    @pl.loop(0, width // LANES)
    def _(index):
        lanes = lanes_of(index)

        def store(row, value):
            sums_ref[row : row + 1, lanes] = part_ref[row : row + 1, lanes] + value

        grad_pre = grad_ref[:, lanes]
        store(taps, jnp.sum(grad_pre, 0, keepdims=True))
        phase_products(
            grad_pre, in_ref[:, lanes], taps, lambda shift, value: store(taps - 1 - shift, value)
        )

    half = width // 2
    mine = lax.rem(lax.axis_index("seq"), 2)
    mine_ref[...] = sums_ref[:, pl.ds(pl.multiple_of(mine * half, LANES), half)].astype(BF16)
    other_ref[...] = sums_ref[:, pl.ds(pl.multiple_of((1 - mine) * half, LANES), half)].astype(BF16)


def cross_back_kernel(group, tiles, qkv_ref, prob_ref, context_ref, seg_ref, *refs):
    frames, width = context_ref.shape
    first, length = crossing(seg_ref, frames)
    place = scatter_matrix(first, length, frames)
    if group == 0:
        gain_ref, kernel_ref, pre_ref, own_ref, next_ref, grad_ref, result_ref, back_ref = refs
        taps = kernel_ref.shape[0]

        @pl.loop(0, width // LANES)
        def _(index):
            lanes = lanes_of(index)
            back_ref[:, lanes] = phase_conv(
                pre_ref[:, lanes], lambda t: kernel_ref[taps - 1 - t : taps - t, lanes], taps, None
            )

        keep = jnp.where(frame_of((frames, frames), 0) < length, 1.0, 0.0)
        norm_backward(context_ref, back_ref, gain_ref, keep, grad_ref, frames)
    else:
        grad_ref, own_ref, next_ref, result_ref = refs

    def store(which, pair, result):
        result_ref[which, :, lanes_at(pair)] = result

    got = [qkv_ref.at[i] for i in range(3)]
    back_all(*got, prob_ref, context_ref, grad_ref, group * tiles, tiles, store)
    for which in range(3):
        placed = dot(place, result_ref[which], NN).astype(BF16)
        own_ref[which] = placed[:frames]
        next_ref[which] = placed[frames:]


def own_back_kernel(q_ref, kv_ref, prob_ref, context_ref, grad_ref, out_ref):
    def store(which, pair, result):
        out_ref[which, :, lanes_at(pair)] = result

    back_all(
        q_ref, kv_ref.at[0], kv_ref.at[1], prob_ref, context_ref, grad_ref,
        0, q_ref.shape[1] // LANES, store,
    )


def merge_kernel(grads_ref, out_both_ref, out_came_ref, *refs):
    parts, outs = refs[:-4], refs[-4:]
    outs[3][...] = out_both_ref[...] + out_came_ref[...]
    start = 0
    for cross_ref, came_ref in zip(parts[::2], parts[1::2]):
        cols = slice(start, start + came_ref.shape[2])
        for which in range(3):
            outs[which][:, cols] = grads_ref[which, :, cols] + cross_ref[which] + came_ref[which]
        start = cols.stop


def finish_kernel(scale, mine_ref, came_ref, weight_ref, norm_ref, gain_ref, kernel_ref, bias_ref):
    taps, width = kernel_ref.shape
    even = lax.rem(lax.axis_index("seq"), 2) == 0
    mine, came = mine_ref[...].astype(F32) * scale, came_ref[...].astype(F32) * scale
    total = jnp.concatenate([jnp.where(even, mine, came), jnp.where(even, came, mine)], 1)
    kernel_ref[...] = total[:taps]
    bias_ref[...] = total[taps : taps + 1].reshape(width)
    gain = jnp.sum(total[:taps] * weight_ref[...], 0, keepdims=True) / norm_ref[...]
    gain_ref[...] = gain.reshape(width)


def call(kernel, outs, scratch, flops, *args, limit=24):
    size = sum(a.size * a.dtype.itemsize for a in args) + sum(o.size * o.dtype.itemsize for o in outs)
    return pl.pallas_call(
        kernel,
        out_shape=outs,
        in_specs=[VMEM] * len(args),
        out_specs=[VMEM] * len(outs),
        scratch_shapes=scratch,
        compiler_params=pltpu.CompilerParams(vmem_limit_bytes=limit * 1024 * 1024),
        cost_estimate=pl.CostEstimate(flops=flops, bytes_accessed=size, transcendentals=0),
    )(*args)


def after(value, *others):
    return lax.optimization_barrier((value,) + others)[0]


def sum_steps():
    steps = {"seq": [], "dp": []}
    for axis, distances in steps.items():
        step = 1
        while step < lax.axis_size(axis):
            distances.append((axis, step))
            step *= 2
    core, x, *rest = steps["seq"]
    return [core, x] + rest[::-1] + steps["dp"]


def exchange(sent, axis, step):
    return lax.ppermute(sent, axis, [(i, i ^ step) for i in range(lax.axis_size(axis))])


def added(sent, came):
    return (sent.astype(F32) + came.astype(F32)).astype(BF16)


def per_device(queries, keys, values, segment_ids, norm_gain, conv_kernel, conv_bias, cotangent):
    frames, width = queries.shape[1:]
    q, cot = queries[0], cotangent[0]
    taps = conv_kernel.shape[0]
    tiles = width // LANES
    count = lax.axis_size("seq")
    to_left = [(i + 1, i) for i in range(count - 1)]
    to_right = [(i, i + 1) for i in range(count - 1)]
    q_next = lax.ppermute(q, "seq", to_left)
    kv = jnp.concatenate([keys[0], values[0]], 0)
    kv_next = lax.ppermute(kv, "seq", to_left).reshape(2, frames, width)
    kv = kv.reshape(2, frames, width)
    cot_next = lax.ppermute(cot, "seq", to_left)

    def sds(shape, dtype):
        return jax.ShapeDtypeStruct(shape, dtype)

    rows16 = sds((frames, width), BF16)
    rows32 = sds((frames, width), F32)
    three = sds((3, frames, width), BF16)
    probs = sds((tiles, frames, 2 * frames), BF16)
    half_sums = sds((taps + 1, width // 2), BF16)
    row = sds((1, width), F32)
    square = sds((frames, frames), F32)
    padded = pltpu.VMEM((frames + 2 * PAD, width), F32)
    plain = pltpu.VMEM((frames, width), F32)

    same, keep, masks = call(
        functools.partial(mask_kernel, taps),
        [square, square, sds((taps * frames, LANES), F32)],
        [pltpu.VMEM((frames + 2 * PAD, LANES), F32)],
        10**10,
        segment_ids,
    )
    out_own, pre_own, prob_own, context_own, sums_own, gain, bias = call(
        own_kernel,
        [rows16, sds((frames + 2 * PAD, width), F32), probs, rows16, sds((taps + 1, width), F32), row, row],
        [padded, pltpu.VMEM((taps, frames, LANES), F32)],
        10**10,
        q, kv, cot, norm_gain, conv_kernel, conv_bias, same, keep, masks,
    )
    out_both, out_next, got, prob_cross, context_cross, pre_cross, in_cross = call(
        cross_forward_kernel,
        [rows16, rows16, three, probs, rows16, rows32, rows32],
        [pltpu.VMEM((frames, width), BF16)],
        4 * 10**9,
        q, kv, q_next, kv_next, segment_ids, gain, conv_kernel, bias, out_own,
    )
    grad_pre, mine, other = call(
        cross_sums_kernel,
        [rows32, half_sums, half_sums],
        [pltpu.VMEM((taps + 1, width), F32)],
        3 * 10**9,
        cot, cot_next, segment_ids, pre_cross, in_cross, sums_own,
    )
    out_came = lax.ppermute(out_next, "seq", to_right)
    steps = sum_steps()
    came = exchange(other, *steps[0])
    sent = added(mine, after(came, out_came))
    came = exchange(sent, *steps[1])
    per_group = tiles // GROUPS
    piece = sds((3, frames, per_group * LANES), BF16)
    parts = []
    grad_pre = after(grad_pre, sent)
    for group in range(GROUPS):
        extra = [gain, conv_kernel, grad_pre] if group == 0 else [grad_cross]
        own_part, next_part, *rest = call(
            functools.partial(cross_back_kernel, group, per_group),
            [piece, piece] + [rows16] * (group == 0),
            [pltpu.VMEM(piece.shape, BF16)] + [plain] * (group == 0),
            2 * 10**9 + 3 * 10**9 * (group == 0),
            got, prob_cross, context_cross, segment_ids, *extra,
        )
        if group == 0:
            (grad_cross,) = rest
        sent = added(sent, after(came, own_part))
        came = exchange(sent, *steps[group + 2])
        parts += [own_part, lax.ppermute(after(next_part, sent), "seq", to_right)]
    (grad_own,) = call(
        own_grad_kernel,
        [rows16],
        [plain],
        4 * 10**9,
        after(pre_own, sent), context_own, masks, keep, gain, conv_kernel,
    )
    for step in steps[GROUPS + 2 :]:
        sent = added(sent, after(came, grad_own, parts[1]))
        came = exchange(sent, *step)
    (grads_own,) = call(
        own_back_kernel,
        [three],
        [],
        4 * 10**9,
        q, kv, prob_own, context_own, after(grad_own, sent),
    )
    sent = added(sent, after(came, grads_own))
    came = exchange(sent, *steps[0])
    query_grad, key_grad, value_grad, conv_out = call(
        merge_kernel, [rows16] * 4, [], 10**9, grads_own, out_both, out_came, *parts,
    )
    scale = (lax.axis_size("dp") * count * frames) ** (-0.5)
    gain_grad, kernel_grad, bias_grad = call(
        functools.partial(finish_kernel, scale),
        [sds((width,), F32), sds(conv_kernel.shape, F32), sds((width,), F32)],
        [],
        10**6,
        sent, came, conv_kernel, gain,
    )
    return (
        conv_out[None],
        query_grad[None],
        key_grad[None],
        value_grad[None],
        gain_grad,
        kernel_grad,
        bias_grad,
    )


def solution(mesh):
    rows = P("dp", "seq", None)
    return jax.shard_map(
        per_device,
        mesh=mesh,
        in_specs=(rows, rows, rows, P("dp", None), P(), P(), P(), rows),
        out_specs=(rows, rows, rows, rows, P(), P(), P()),
        check_vma=False,
    )
```

```python
import functools

import jax
import jax.numpy as jnp
from jax import lax
from jax.experimental import pallas as pl
from jax.experimental.pallas import tpu as pltpu
from jax.sharding import PartitionSpec as P

HEAD_DIM = 64
EPS = 1e-05
NEG = -1e30
LANES = 128
PAD = 16
GROUPS = 2
WIDE = 512
BATCH = 6
VMEM = pl.BlockSpec(memory_space=pltpu.VMEM)
F32 = jnp.float32
BF16 = jnp.bfloat16


def dot(a, b, dims):
    return lax.dot_general(a, b, (dims, ((), ())), preferred_element_type=F32)


NN = ((1,), (0,))
NT = ((1,), (1,))
TN = ((0,), (0,))


def lanes_of(index):
    return pl.ds(pl.multiple_of(index * LANES, LANES), LANES)


def block_ids(seg_ref, frames):
    me = lax.axis_index("seq")
    count = seg_ref.shape[1] // frames
    own = seg_ref[0:1, pl.ds(pl.multiple_of(me * frames, frames), frames)].astype(F32)
    before = jnp.maximum(me - 1, 0)
    after = jnp.minimum(me + 1, count - 1)
    prev = seg_ref[0:1, pl.ds(pl.multiple_of(before * frames, frames), frames)].astype(F32)
    following = seg_ref[0:1, pl.ds(pl.multiple_of(after * frames, frames), frames)].astype(F32)
    prev_last = jnp.where(me > 0, prev[:, frames - 1 :], -1.0)
    following = jnp.where(me < count - 1, following, -1.0)
    return own, following, prev_last, following[:, 0:1]


def crossing(seg_ref, frames):
    own, following, _, edge = block_ids(seg_ref, frames)
    left = jnp.sum(jnp.where((own == edge) & (edge >= 0.0), 1.0, 0.0), 1, keepdims=True)
    right = jnp.sum(jnp.where(following == edge, 1.0, 0.0), 1, keepdims=True)
    length = jnp.where(left > 0.0, left + right, 0.0)
    return frames - left, length


def iota(shape, axis):
    return lax.broadcasted_iota(jnp.int32, shape, axis).astype(F32)


def frame_of(shape, axis):
    place = lax.broadcasted_iota(jnp.int32, shape, axis)
    tiles = shape[axis] // 8
    return (lax.rem(place, 8) * tiles + lax.div(place, 8)).astype(F32)


def gather_matrix(first, length, frames):
    shape = (frames, 2 * frames)
    row = frame_of(shape, 0)
    return jnp.where((iota(shape, 1) == row + first) & (row < length), 1.0, 0.0).astype(BF16)


def scatter_matrix(first, length, frames):
    shape = (2 * frames, frames)
    col = frame_of(shape, 1)
    return jnp.where((iota(shape, 0) == col + first) & (col < length), 1.0, 0.0).astype(BF16)


def pair_masks(rows):
    low = lax.broadcasted_iota(jnp.int32, (rows, LANES), 1) < HEAD_DIM
    return low


def stack_pair(pair, low):
    zero = jnp.zeros_like(pair)
    return jnp.concatenate([jnp.where(low, pair, zero), jnp.where(low, zero, pair)], 0)


def attend(query, key, value, bias, keep, low):
    frames = query.shape[0]
    logits = dot(query * jnp.asarray(HEAD_DIM**-0.5, BF16), stack_pair(key, low), NT)
    halves = []
    for half in range(2):
        part = logits[:, half * frames : (half + 1) * frames] + bias
        top = jnp.max(part, 1, keepdims=True)
        power = jnp.exp(part - top)
        total = jnp.sum(power, 1, keepdims=True)
        halves.append((power * (1.0 / total)).astype(BF16))
    prob = jnp.concatenate(halves, 1)
    context = dot(prob, stack_pair(value, low), NN)
    return prob, (context * keep).astype(BF16)


def attend_back(query, key, value, prob, context, grad, pairs, store):
    frames = context(0).shape[0]
    low = pair_masks(frames)
    scale = HEAD_DIM**-0.5
    grad_probs = [dot(grad(p), stack_pair(value(p), low), NT) for p in pairs]
    deltas = []
    for p in pairs:
        product = grad(p).astype(F32) * context(p).astype(F32)
        zero = jnp.zeros_like(product)
        deltas.append(
            (
                jnp.sum(jnp.where(low, product, zero), 1, keepdims=True),
                jnp.sum(jnp.where(low, zero, product), 1, keepdims=True),
            )
        )
    grad_logits = []
    for p, grad_prob, delta in zip(pairs, grad_probs, deltas):
        both = prob(p)
        halves = []
        for half in range(2):
            cols = slice(half * frames, (half + 1) * frames)
            halves.append(
                (both[:, cols].astype(F32) * (grad_prob[:, cols] - delta[half]) * scale).astype(BF16)
            )
        grad_logits.append(halves)
    for p, halves in zip(pairs, grad_logits):
        store(0, p, dot(jnp.concatenate(halves, 1), stack_pair(key(p), low), NN).astype(BF16))
    for p, halves in zip(pairs, grad_logits):
        store(1, p, dot(jnp.concatenate(halves, 0), stack_pair(query(p), low), TN).astype(BF16))
    for p in pairs:
        both = prob(p)
        rows = jnp.concatenate([both[:, :frames], both[:, frames:]], 0)
        store(2, p, dot(rows, stack_pair(grad(p), low), TN).astype(BF16))


def lanes_at(index):
    return slice(index * LANES, (index + 1) * LANES)


def back_all(q_ref, k_ref, v_ref, prob_ref, context_ref, grad_ref, first, pairs, store):
    for start in range(0, pairs, BATCH):
        attend_back(
            lambda p: q_ref[:, lanes_at(first + p)],
            lambda p: k_ref[:, lanes_at(first + p)],
            lambda p: v_ref[:, lanes_at(first + p)],
            lambda p: prob_ref[first + p],
            lambda p: context_ref[:, lanes_at(first + p)],
            lambda p: grad_ref[:, lanes_at(first + p)],
            range(start, min(start + BATCH, pairs)),
            store,
        )


def normalize(context):
    context = context.astype(F32)
    centred = context - jnp.mean(context, -1, keepdims=True)
    inv_std = lax.rsqrt(jnp.mean(centred * centred, -1, keepdims=True) + EPS)
    return centred * inv_std, inv_std


CHUNK = 32


def chunks(frames):
    return [pl.ds(start, CHUNK) for start in range(0, frames, CHUNK)]


def clear_edges(pad_ref, frames):
    zero = jnp.zeros((PAD, pad_ref.shape[1]), F32)
    pad_ref[0:PAD, :] = zero
    pad_ref[PAD + frames : 2 * PAD + frames, :] = zero


def shifts(frames, taps):
    base = PAD - taps // 2
    for turn in range(8):
        for start in range(0, 2 * PAD + 1, 8):
            tap = start + turn - base
            if 0 <= tap < taps:
                yield turn, start, tap


def turned(block, turn):
    rows = block.shape[0]
    return block if turn == 0 else pltpu.roll(block, rows - turn, 0)


def masked_conv(pad_ref, mask_ref, weight, taps, start, lanes, keep_view=None):
    frames = start.shape[0]
    block = pad_ref[:, lanes]
    total = start
    at, view = None, None
    for turn, row, tap in shifts(frames, taps):
        if turn != at:
            at, view = turn, turned(block, turn)
        term = view[row : row + frames] * mask_ref[tap * frames : (tap + 1) * frames, :]
        if keep_view is not None:
            keep_view(tap, term)
        total = total + weight(tap) * term
    return total


def phase_views(block, half_taps):
    tiles = block.shape[0] // 8
    row = lax.broadcasted_iota(jnp.int32, (8, LANES), 0)
    views = {}
    for j in range(tiles):
        tile = block[8 * j : 8 * j + 8]
        views[j] = tile
        if j - tiles >= -half_taps:
            views[j - tiles] = jnp.where(row >= 1, pltpu.roll(tile, 1, 0), 0.0)
        if j < half_taps:
            views[j + tiles] = jnp.where(row < 7, pltpu.roll(tile, 7, 0), 0.0)
    return views


def half_rate(views, taps, tiles):
    reach = tiles // 2 + (taps + 1) // 2 - 1
    low = -(taps // 2)
    middle = [views[low + 2 * n + 1] if low + 2 * n + 1 in views else None for n in range(reach)]
    before = [views[low + 2 * n] for n in range(reach)]
    after_ = [views.get(low + 2 * n + 2) for n in range(reach)]
    return middle, before, after_


def minus(a, b):
    if b is None:
        return a
    return -b if a is None else a - b


def phase_conv(block, weight, taps, start):
    tiles = block.shape[0] // 8
    middle, before, behind = half_rate(phase_views(block, taps // 2), taps, tiles)
    pairs = tiles // 2

    def run(values, weights, total):
        for s, w in enumerate(weights):
            for a in range(pairs):
                if values[a + s] is not None:
                    term = w * values[a + s]
                    total[a] = term if total[a] is None else total[a] + term
        return total

    even = [weight(t) for t in range(0, taps, 2)]
    odd = [weight(t) for t in range(1, taps, 2)]
    both = [e + o for e, o in zip(even, odd)] + even[len(odd) :]
    shared = run(middle, both, [start] * pairs)
    first = run([minus(b, m) for b, m in zip(before, middle)], even, list(shared))
    second = run([minus(b, m) for b, m in zip(behind, middle)], odd, list(shared))
    return jnp.concatenate([tile for pair in zip(first, second) for tile in pair], 0)


def phase_products(block, rows, taps, store):
    tiles = block.shape[0] // 8
    middle, before, behind = half_rate(phase_views(block, taps // 2), taps, tiles)
    pairs = tiles // 2
    even = [rows[16 * a : 16 * a + 8] for a in range(pairs)]
    odd = [rows[16 * a + 8 : 16 * a + 16] for a in range(pairs)]
    both = [e + o for e, o in zip(even, odd)]
    first = [minus(b, m) for b, m in zip(before, middle)]
    second = [minus(b, m) for b, m in zip(behind, middle)]

    def run(values, tiles_of, s):
        total = None
        for a in range(pairs):
            if values[a + s] is not None:
                term = tiles_of[a] * values[a + s]
                total = term if total is None else total + term
        return total

    for s in range((taps + 1) // 2):
        shared = run(middle, both, s)
        store(2 * s, jnp.sum(shared + run(first, even, s), 0, keepdims=True))
        if 2 * s + 1 < taps:
            store(2 * s + 1, jnp.sum(shared + run(second, odd, s), 0, keepdims=True))


def gate(pre_act):
    return 1.0 / (1.0 + jnp.exp(-pre_act))


def gate_grad(cotangent, pre_act, sig):
    return (cotangent * sig * (1.0 + pre_act * (1.0 - sig))).astype(BF16).astype(F32)


def norm_backward(context_ref, grad_ref, gain_ref, keep, out_ref, frames):
    for rows in chunks(frames):
        normed, inv_std = normalize(context_ref[rows, :])
        grad = grad_ref[rows, :] * gain_ref[0:1, :]
        centre = jnp.mean(grad, -1, keepdims=True)
        slope = jnp.mean(grad * normed, -1, keepdims=True)
        result = (grad - centre - normed * slope) * inv_std
        out_ref[rows, :] = jnp.where(keep[rows.start : rows.start + CHUNK, 0:1] > 0.0, result, 0.0).astype(BF16)


def wide(width):
    return [slice(start, start + WIDE) for start in range(0, width, WIDE)]


def forward_all(q_ref, k_ref, v_ref, prob_ref, context_ref, bias, keep, low):
    for index in range(q_ref.shape[1] // LANES):
        lanes = slice(index * LANES, (index + 1) * LANES)
        prob, context = attend(q_ref[:, lanes], k_ref[:, lanes], v_ref[:, lanes], bias, keep, low)
        prob_ref[index] = prob
        context_ref[:, lanes] = context


def normalize_all(context_ref, gain_ref, keep, in_ref, offset, frames):
    for rows in chunks(frames):
        normed, _ = normalize(context_ref[rows, :])
        normed = jnp.where(keep[rows.start : rows.start + CHUNK, 0:1] > 0.0, normed, 0.0)
        in_ref[pl.ds(offset + rows.start, CHUNK), :] = (
            (normed * gain_ref[0:1, :]).astype(BF16).astype(F32)
        )


def mask_kernel(taps, seg_ref, bias_ref, keep_ref, mask_ref, pad_ref):
    frames = bias_ref.shape[0]
    own, _, prev_last, next_first = block_ids(seg_ref, frames)
    ids = jnp.where((own == prev_last) | (own == next_first), -5.0, own)
    ids_row = jnp.broadcast_to(ids, (frames, frames))
    ids_col = jnp.transpose(ids_row)
    bias_ref[...] = jnp.where(ids_row == ids_col, 0.0, NEG)
    keep_ref[...] = jnp.where(ids_col >= 0.0, 1.0, 0.0)
    pad_ref[...] = jnp.full(pad_ref.shape, -9.0, F32)
    pad_ref[PAD : PAD + frames, :] = ids_col
    ids_pad = pad_ref[...]
    at, view = None, None
    for turn, start, tap in shifts(frames, taps):
        if turn != at:
            at, view = turn, turned(ids_pad, turn)
        mask_ref[tap * frames : (tap + 1) * frames, :] = jnp.where(
            view[start : start + frames] == ids_col, 1.0, 0.0
        )


def own_kernel(
    q_ref, kv_ref, cot_ref, gain_row, kernel_ref, bias_row, same_ref, keep_ref, mask_ref,
    out_ref, grad_ref, prob_ref, context_ref, sums_ref, gain_ref, bias_ref,
    pad_ref, view_ref,
):
    frames, width = q_ref.shape
    taps = kernel_ref.shape[0]
    clear_edges(pad_ref, frames)
    clear_edges(grad_ref, frames)
    low = pair_masks(frames)
    gain_ref[...] = gain_row[...].reshape(1, width)
    bias_ref[...] = bias_row[...].reshape(1, width)
    bias, keep = same_ref[...], keep_ref[...]
    forward_all(q_ref, kv_ref.at[0], kv_ref.at[1], prob_ref, context_ref, bias, keep, low)
    normalize_all(context_ref, gain_ref, keep, pad_ref, PAD, frames)

    @pl.loop(0, width // LANES)
    def _(index):
        lanes = lanes_of(index)

        def keep_view(tap, term):
            view_ref[tap] = term

        pre_act = masked_conv(
            pad_ref, mask_ref, lambda t: kernel_ref[t : t + 1, lanes], taps,
            jnp.broadcast_to(bias_ref[0:1, lanes], (frames, LANES)), lanes, keep_view,
        )
        sig = gate(pre_act)
        out_ref[:, lanes] = (pre_act * sig * keep_ref[...]).astype(BF16)
        grad_pre = gate_grad(cot_ref[:, lanes].astype(F32) * keep_ref[...], pre_act, sig)
        grad_ref[PAD : PAD + frames, lanes] = grad_pre
        sums_ref[taps : taps + 1, lanes] = jnp.sum(grad_pre, 0, keepdims=True)
        for tap in range(taps):
            sums_ref[tap : tap + 1, lanes] = jnp.sum(grad_pre * view_ref[tap], 0, keepdims=True)


def own_conv_back(pad_ref, mask_ref, kernel_ref, back_ref, first, tiles):
    frames = back_ref.shape[0]
    taps = kernel_ref.shape[0]

    @pl.loop(first, first + tiles)
    def _(index):
        lanes = lanes_of(index)
        back_ref[:, lanes_of(index)] = masked_conv(
            pad_ref, mask_ref, lambda t: kernel_ref[taps - 1 - t : taps - t, lanes], taps,
            jnp.zeros((frames, LANES), F32), lanes,
        )


def own_half_kernel(pad_ref, mask_ref, kernel_ref, back_ref):
    own_conv_back(pad_ref, mask_ref, kernel_ref, back_ref, 0, back_ref.shape[1] // LANES)


def own_grad_kernel(
    pad_ref, context_ref, mask_ref, keep_ref, gain_ref, kernel_ref, half_ref, grad_ref, back_ref
):
    frames, width = context_ref.shape
    half = half_ref.shape[1]
    back_ref[:, :half] = half_ref[...]
    own_conv_back(pad_ref, mask_ref, kernel_ref, back_ref, half // LANES, (width - half) // LANES)
    norm_backward(context_ref, back_ref, gain_ref, keep_ref[...], grad_ref, frames)


def cross_forward_kernel(
    q_ref, kv_ref, qn_ref, kvn_ref, seg_ref, gain_ref, kernel_ref, bias_ref, add_ref,
    own_ref, next_ref, got_ref, prob_ref, context_ref, slope_ref, in_ref,
    out_ref,
):
    frames, width = q_ref.shape
    taps = kernel_ref.shape[0]
    tiles = width // LANES
    first, length = crossing(seg_ref, frames)
    pick = gather_matrix(first, length, frames)
    place = scatter_matrix(first, length, frames)
    shape = (frames, frames)
    bias = jnp.where(frame_of(shape, 1) < length, 0.0, NEG)
    keep = jnp.where(frame_of(shape, 0) < length, 1.0, 0.0)
    low = pair_masks(frames)
    sources = ((q_ref, qn_ref), (kv_ref.at[0], kvn_ref.at[0]), (kv_ref.at[1], kvn_ref.at[1]))
    for which, (own, other) in enumerate(sources):
        for cols in wide(width):
            both = jnp.concatenate([own[:, cols], other[:, cols]], 0)
            got_ref[which, :, cols] = dot(pick, both, NN).astype(BF16)
    forward_all(*(got_ref.at[i] for i in range(3)), prob_ref, context_ref, bias, keep, low)
    normalize_all(context_ref, gain_ref, keep, in_ref, 0, frames)

    @pl.loop(0, tiles)
    def _(index):
        lanes = lanes_of(index)
        start = jnp.broadcast_to(bias_ref[0:1, lanes], (8, LANES))
        pre_act = phase_conv(in_ref[:, lanes], lambda t: kernel_ref[t : t + 1, lanes], taps, start)
        sig = gate(pre_act)
        slope_ref[:, lanes] = sig * (1.0 + pre_act * (1.0 - sig))
        out_ref[:, lanes] = (pre_act * sig).astype(BF16)

    for cols in wide(width):
        placed = dot(place, out_ref[:, cols], NN).astype(BF16)
        own_ref[:, cols] = placed[:frames] + add_ref[:, cols]
        next_ref[:, cols] = placed[frames:]


def cross_sums_kernel(
    cot_ref, cotn_ref, seg_ref, slope_ref, in_ref, part_ref,
    grad_ref, mine_ref, other_ref,
    sums_ref,
):
    frames, width = cot_ref.shape
    taps = part_ref.shape[0] - 1
    first, length = crossing(seg_ref, frames)
    pick = gather_matrix(first, length, frames)
    for cols in wide(width):
        cotangent = dot(pick, jnp.concatenate([cot_ref[:, cols], cotn_ref[:, cols]], 0), NN)
        grad_ref[:, cols] = (cotangent * slope_ref[:, cols]).astype(BF16).astype(F32)

    @pl.loop(0, width // LANES)
    def _(index):
        lanes = lanes_of(index)

        def store(row, value):
            sums_ref[row : row + 1, lanes] = part_ref[row : row + 1, lanes] + value

        grad_pre = grad_ref[:, lanes]
        store(taps, jnp.sum(grad_pre, 0, keepdims=True))
        phase_products(
            grad_pre, in_ref[:, lanes], taps, lambda shift, value: store(taps - 1 - shift, value)
        )

    half = width // 2
    mine = lax.rem(lax.axis_index("seq"), 2)
    mine_ref[...] = sums_ref[:, pl.ds(pl.multiple_of(mine * half, LANES), half)].astype(BF16)
    other_ref[...] = sums_ref[:, pl.ds(pl.multiple_of((1 - mine) * half, LANES), half)].astype(BF16)


def cross_back_kernel(group, tiles, qkv_ref, prob_ref, context_ref, seg_ref, *refs):
    frames, width = context_ref.shape
    first, length = crossing(seg_ref, frames)
    place = scatter_matrix(first, length, frames)
    if group == 0:
        gain_ref, kernel_ref, pre_ref, own_ref, next_ref, grad_ref, result_ref, back_ref = refs
        taps = kernel_ref.shape[0]

        @pl.loop(0, width // LANES)
        def _(index):
            lanes = lanes_of(index)
            back_ref[:, lanes] = phase_conv(
                pre_ref[:, lanes], lambda t: kernel_ref[taps - 1 - t : taps - t, lanes], taps, None
            )

        keep = jnp.where(frame_of((frames, frames), 0) < length, 1.0, 0.0)
        norm_backward(context_ref, back_ref, gain_ref, keep, grad_ref, frames)
    else:
        grad_ref, own_ref, next_ref, result_ref = refs

    def store(which, pair, result):
        result_ref[which, :, lanes_at(pair)] = result

    got = [qkv_ref.at[i] for i in range(3)]
    back_all(*got, prob_ref, context_ref, grad_ref, group * tiles, tiles, store)
    for which in range(3):
        placed = dot(place, result_ref[which], NN).astype(BF16)
        own_ref[which] = placed[:frames]
        next_ref[which] = placed[frames:]


def own_back_kernel(q_ref, kv_ref, prob_ref, context_ref, grad_ref, out_ref):
    def store(which, pair, result):
        out_ref[which, :, lanes_at(pair)] = result

    back_all(
        q_ref, kv_ref.at[0], kv_ref.at[1], prob_ref, context_ref, grad_ref,
        0, q_ref.shape[1] // LANES, store,
    )


def merge_kernel(grads_ref, out_both_ref, out_came_ref, *refs):
    parts, outs = refs[:-4], refs[-4:]
    outs[3][...] = out_both_ref[...] + out_came_ref[...]
    start = 0
    for cross_ref, came_ref in zip(parts[::2], parts[1::2]):
        cols = slice(start, start + came_ref.shape[2])
        for which in range(3):
            outs[which][:, cols] = grads_ref[which, :, cols] + cross_ref[which] + came_ref[which]
        start = cols.stop


def finish_kernel(scale, mine_ref, came_ref, weight_ref, norm_ref, gain_ref, kernel_ref, bias_ref):
    taps, width = kernel_ref.shape
    even = lax.rem(lax.axis_index("seq"), 2) == 0
    mine, came = mine_ref[...].astype(F32) * scale, came_ref[...].astype(F32) * scale
    total = jnp.concatenate([jnp.where(even, mine, came), jnp.where(even, came, mine)], 1)
    kernel_ref[...] = total[:taps]
    bias_ref[...] = total[taps : taps + 1].reshape(width)
    gain = jnp.sum(total[:taps] * weight_ref[...], 0, keepdims=True) / norm_ref[...]
    gain_ref[...] = gain.reshape(width)


def call(kernel, outs, scratch, flops, *args, limit=24):
    size = sum(a.size * a.dtype.itemsize for a in args) + sum(o.size * o.dtype.itemsize for o in outs)
    return pl.pallas_call(
        kernel,
        out_shape=outs,
        in_specs=[VMEM] * len(args),
        out_specs=[VMEM] * len(outs),
        scratch_shapes=scratch,
        compiler_params=pltpu.CompilerParams(vmem_limit_bytes=limit * 1024 * 1024),
        cost_estimate=pl.CostEstimate(flops=flops, bytes_accessed=size, transcendentals=0),
    )(*args)


def after(value, *others):
    return lax.optimization_barrier((value,) + others)[0]


def sum_steps():
    steps = {"seq": [], "dp": []}
    for axis, distances in steps.items():
        step = 1
        while step < lax.axis_size(axis):
            distances.append((axis, step))
            step *= 2
    core, x, *rest = steps["seq"]
    return [core, x] + rest[::-1] + steps["dp"]


def exchange(sent, axis, step):
    return lax.ppermute(sent, axis, [(i, i ^ step) for i in range(lax.axis_size(axis))])


def added(sent, came):
    return (sent.astype(F32) + came.astype(F32)).astype(BF16)


def per_device(queries, keys, values, segment_ids, norm_gain, conv_kernel, conv_bias, cotangent):
    frames, width = queries.shape[1:]
    q, cot = queries[0], cotangent[0]
    taps = conv_kernel.shape[0]
    tiles = width // LANES
    count = lax.axis_size("seq")
    to_left = [(i + 1, i) for i in range(count - 1)]
    to_right = [(i, i + 1) for i in range(count - 1)]
    q_next = lax.ppermute(q, "seq", to_left)
    kv = jnp.concatenate([keys[0], values[0]], 0)
    kv_next = lax.ppermute(kv, "seq", to_left).reshape(2, frames, width)
    kv = kv.reshape(2, frames, width)
    cot_next = lax.ppermute(cot, "seq", to_left)

    def sds(shape, dtype):
        return jax.ShapeDtypeStruct(shape, dtype)

    rows16 = sds((frames, width), BF16)
    rows32 = sds((frames, width), F32)
    three = sds((3, frames, width), BF16)
    probs = sds((tiles, frames, 2 * frames), BF16)
    half_sums = sds((taps + 1, width // 2), BF16)
    row = sds((1, width), F32)
    square = sds((frames, frames), F32)
    padded = pltpu.VMEM((frames + 2 * PAD, width), F32)
    plain = pltpu.VMEM((frames, width), F32)

    same, keep, masks = call(
        functools.partial(mask_kernel, taps),
        [square, square, sds((taps * frames, LANES), F32)],
        [pltpu.VMEM((frames + 2 * PAD, LANES), F32)],
        10**10,
        segment_ids,
    )
    out_own, pre_own, prob_own, context_own, sums_own, gain, bias = call(
        own_kernel,
        [rows16, sds((frames + 2 * PAD, width), F32), probs, rows16, sds((taps + 1, width), F32), row, row],
        [padded, pltpu.VMEM((taps, frames, LANES), F32)],
        10**10,
        q, kv, cot, norm_gain, conv_kernel, conv_bias, same, keep, masks,
    )
    out_both, out_next, got, prob_cross, context_cross, slope_cross, in_cross = call(
        cross_forward_kernel,
        [rows16, rows16, three, probs, rows16, rows32, rows32],
        [pltpu.VMEM((frames, width), BF16)],
        4 * 10**9,
        q, kv, q_next, kv_next, segment_ids, gain, conv_kernel, bias, out_own,
    )
    grad_pre, mine, other = call(
        cross_sums_kernel,
        [rows32, half_sums, half_sums],
        [pltpu.VMEM((taps + 1, width), F32)],
        3 * 10**9,
        cot, cot_next, segment_ids, slope_cross, in_cross, sums_own,
    )
    steps = sum_steps()
    came = exchange(other, *steps[0])
    (half_own,) = call(
        own_half_kernel,
        [sds((frames, width // 2), F32)],
        [],
        2 * 10**9,
        after(pre_own, mine), masks, conv_kernel,
    )
    sent = added(mine, after(came, half_own))
    came = exchange(sent, *steps[1])
    out_came = lax.ppermute(after(out_next, sent), "seq", to_right)
    per_group = tiles // GROUPS
    piece = sds((3, frames, per_group * LANES), BF16)
    parts = []
    grad_pre = after(grad_pre, sent)
    for group in range(GROUPS):
        if group == 1:
            sent = added(sent, after(came, out_came, grad_own))
            came = exchange(sent, *steps[3])
        extra = [gain, conv_kernel, grad_pre] if group == 0 else [after(grad_cross, sent)]
        own_part, next_part, *rest = call(
            functools.partial(cross_back_kernel, group, per_group),
            [piece, piece] + [rows16] * (group == 0),
            [pltpu.VMEM(piece.shape, BF16)] + [plain] * (group == 0),
            2 * 10**9 + 3 * 10**9 * (group == 0),
            got, prob_cross, context_cross, segment_ids, *extra,
        )
        if group == 0:
            (grad_cross,) = rest
            sent = added(sent, after(came, own_part))
            came = exchange(sent, *steps[2])
            (grad_own,) = call(
                own_grad_kernel,
                [rows16],
                [plain],
                3 * 10**9,
                after(pre_own, sent), context_own, masks, keep, gain, conv_kernel, half_own,
            )
        parts += [own_part, lax.ppermute(after(next_part, sent), "seq", to_right)]
    for step in steps[GROUPS + 2 :]:
        sent = added(sent, came)
        came = exchange(sent, *step)
    (grads_own,) = call(
        own_back_kernel,
        [three],
        [],
        4 * 10**9,
        q, kv, prob_own, context_own, after(grad_own, sent),
    )
    sent = added(sent, after(came, grads_own))
    came = exchange(sent, *steps[0])
    query_grad, key_grad, value_grad, conv_out = call(
        merge_kernel, [rows16] * 4, [], 10**9, grads_own, out_both, out_came, *parts,
    )
    scale = (lax.axis_size("dp") * count * frames) ** (-0.5)
    gain_grad, kernel_grad, bias_grad = call(
        functools.partial(finish_kernel, scale),
        [sds((width,), F32), sds(conv_kernel.shape, F32), sds((width,), F32)],
        [],
        10**6,
        sent, came, conv_kernel, gain,
    )
    return (
        conv_out[None],
        query_grad[None],
        key_grad[None],
        value_grad[None],
        gain_grad,
        kernel_grad,
        bias_grad,
    )


def solution(mesh):
    rows = P("dp", "seq", None)
    return jax.shard_map(
        per_device,
        mesh=mesh,
        in_specs=(rows, rows, rows, P("dp", None), P(), P(), P(), rows),
        out_specs=(rows, rows, rows, rows, P(), P(), P()),
        check_vma=False,
    )
```

```python
import functools

import jax
import jax.numpy as jnp
from jax import lax
from jax.experimental import pallas as pl
from jax.experimental.pallas import tpu as pltpu
from jax.sharding import PartitionSpec as P

HEAD_DIM = 64
EPS = 1e-05
NEG = -1e30
LANES = 128
PAD = 16
GROUPS = 2
WIDE = 512
BATCH = 6
VMEM = pl.BlockSpec(memory_space=pltpu.VMEM)
F32 = jnp.float32
BF16 = jnp.bfloat16


def dot(a, b, dims):
    return lax.dot_general(a, b, (dims, ((), ())), preferred_element_type=F32)


NN = ((1,), (0,))
NT = ((1,), (1,))
TN = ((0,), (0,))


def lanes_of(index):
    return pl.ds(pl.multiple_of(index * LANES, LANES), LANES)


def block_ids(seg_ref, frames):
    me = lax.axis_index("seq")
    count = seg_ref.shape[1] // frames
    own = seg_ref[0:1, pl.ds(pl.multiple_of(me * frames, frames), frames)].astype(F32)
    before = jnp.maximum(me - 1, 0)
    after = jnp.minimum(me + 1, count - 1)
    prev = seg_ref[0:1, pl.ds(pl.multiple_of(before * frames, frames), frames)].astype(F32)
    following = seg_ref[0:1, pl.ds(pl.multiple_of(after * frames, frames), frames)].astype(F32)
    prev_last = jnp.where(me > 0, prev[:, frames - 1 :], -1.0)
    following = jnp.where(me < count - 1, following, -1.0)
    return own, following, prev_last, following[:, 0:1]


def crossing(seg_ref, frames):
    own, following, _, edge = block_ids(seg_ref, frames)
    left = jnp.sum(jnp.where((own == edge) & (edge >= 0.0), 1.0, 0.0), 1, keepdims=True)
    right = jnp.sum(jnp.where(following == edge, 1.0, 0.0), 1, keepdims=True)
    length = jnp.where(left > 0.0, left + right, 0.0)
    return frames - left, length


def iota(shape, axis):
    return lax.broadcasted_iota(jnp.int32, shape, axis).astype(F32)


def frame_of(shape, axis):
    place = lax.broadcasted_iota(jnp.int32, shape, axis)
    tiles = shape[axis] // 8
    return (lax.rem(place, 8) * tiles + lax.div(place, 8)).astype(F32)


def gather_matrix(first, length, frames):
    shape = (frames, 2 * frames)
    row = frame_of(shape, 0)
    return jnp.where((iota(shape, 1) == row + first) & (row < length), 1.0, 0.0).astype(BF16)


def scatter_matrix(first, length, frames):
    shape = (2 * frames, frames)
    col = frame_of(shape, 1)
    return jnp.where((iota(shape, 0) == col + first) & (col < length), 1.0, 0.0).astype(BF16)


def pair_masks(rows):
    low = lax.broadcasted_iota(jnp.int32, (rows, LANES), 1) < HEAD_DIM
    return low


def stack_pair(pair, low):
    zero = jnp.zeros_like(pair)
    return jnp.concatenate([jnp.where(low, pair, zero), jnp.where(low, zero, pair)], 0)


def attend(query, key, value, bias, keep, low):
    frames = query.shape[0]
    logits = dot(query * jnp.asarray(HEAD_DIM**-0.5, BF16), stack_pair(key, low), NT)
    halves = []
    for half in range(2):
        part = logits[:, half * frames : (half + 1) * frames] + bias
        top = jnp.max(part, 1, keepdims=True)
        power = jnp.exp(part - top)
        total = jnp.sum(power, 1, keepdims=True)
        halves.append((power * (1.0 / total)).astype(BF16))
    prob = jnp.concatenate(halves, 1)
    context = dot(prob, stack_pair(value, low), NN)
    return prob, (context * keep).astype(BF16)


def attend_back(query, key, value, prob, context, grad, pairs, store):
    frames = context(0).shape[0]
    low = pair_masks(frames)
    scale = HEAD_DIM**-0.5
    grad_probs = [dot(grad(p), stack_pair(value(p), low), NT) for p in pairs]
    deltas = []
    for p in pairs:
        product = grad(p).astype(F32) * context(p).astype(F32)
        zero = jnp.zeros_like(product)
        deltas.append(
            (
                jnp.sum(jnp.where(low, product, zero), 1, keepdims=True),
                jnp.sum(jnp.where(low, zero, product), 1, keepdims=True),
            )
        )
    grad_logits = []
    for p, grad_prob, delta in zip(pairs, grad_probs, deltas):
        both = prob(p)
        halves = []
        for half in range(2):
            cols = slice(half * frames, (half + 1) * frames)
            halves.append(
                (both[:, cols].astype(F32) * (grad_prob[:, cols] - delta[half]) * scale).astype(BF16)
            )
        grad_logits.append(halves)
    for p, halves in zip(pairs, grad_logits):
        store(0, p, dot(jnp.concatenate(halves, 1), stack_pair(key(p), low), NN).astype(BF16))
    for p, halves in zip(pairs, grad_logits):
        store(1, p, dot(jnp.concatenate(halves, 0), stack_pair(query(p), low), TN).astype(BF16))
    for p in pairs:
        both = prob(p)
        rows = jnp.concatenate([both[:, :frames], both[:, frames:]], 0)
        store(2, p, dot(rows, stack_pair(grad(p), low), TN).astype(BF16))


def lanes_at(index):
    return slice(index * LANES, (index + 1) * LANES)


def back_all(q_ref, k_ref, v_ref, prob_ref, context_ref, grad_ref, first, pairs, store):
    for start in range(0, pairs, BATCH):
        attend_back(
            lambda p: q_ref[:, lanes_at(first + p)],
            lambda p: k_ref[:, lanes_at(first + p)],
            lambda p: v_ref[:, lanes_at(first + p)],
            lambda p: prob_ref[first + p],
            lambda p: context_ref[:, lanes_at(first + p)],
            lambda p: grad_ref[:, lanes_at(first + p)],
            range(start, min(start + BATCH, pairs)),
            store,
        )


def normalize(context):
    context = context.astype(F32)
    centred = context - jnp.mean(context, -1, keepdims=True)
    inv_std = lax.rsqrt(jnp.mean(centred * centred, -1, keepdims=True) + EPS)
    return centred * inv_std, inv_std


CHUNK = 32


def chunks(frames):
    return [pl.ds(start, CHUNK) for start in range(0, frames, CHUNK)]


def clear_edges(pad_ref, frames):
    zero = jnp.zeros((PAD, pad_ref.shape[1]), F32)
    pad_ref[0:PAD, :] = zero
    pad_ref[PAD + frames : 2 * PAD + frames, :] = zero


def shifts(frames, taps):
    base = PAD - taps // 2
    for turn in range(8):
        for start in range(0, 2 * PAD + 1, 8):
            tap = start + turn - base
            if 0 <= tap < taps:
                yield turn, start, tap


def turned(block, turn):
    rows = block.shape[0]
    return block if turn == 0 else pltpu.roll(block, rows - turn, 0)


def masked_conv(pad_ref, mask_ref, weight, taps, start, lanes, keep_view=None):
    frames = start.shape[0]
    block = pad_ref[:, lanes]
    total = start
    at, view = None, None
    for turn, row, tap in shifts(frames, taps):
        if turn != at:
            at, view = turn, turned(block, turn)
        term = view[row : row + frames] * mask_ref[tap * frames : (tap + 1) * frames, :]
        if keep_view is not None:
            keep_view(tap, term)
        total = total + weight(tap) * term
    return total


def phase_views(block, half_taps):
    tiles = block.shape[0] // 8
    row = lax.broadcasted_iota(jnp.int32, (8, LANES), 0)
    views = {}
    for j in range(tiles):
        tile = block[8 * j : 8 * j + 8]
        views[j] = tile
        if j - tiles >= -half_taps:
            views[j - tiles] = jnp.where(row >= 1, pltpu.roll(tile, 1, 0), 0.0)
        if j < half_taps:
            views[j + tiles] = jnp.where(row < 7, pltpu.roll(tile, 7, 0), 0.0)
    return views


def half_rate(views, taps, tiles):
    reach = tiles // 2 + (taps + 1) // 2 - 1
    low = -(taps // 2)
    middle = [views[low + 2 * n + 1] if low + 2 * n + 1 in views else None for n in range(reach)]
    before = [views[low + 2 * n] for n in range(reach)]
    after_ = [views.get(low + 2 * n + 2) for n in range(reach)]
    return middle, before, after_


def minus(a, b):
    if b is None:
        return a
    return -b if a is None else a - b


def phase_conv(block, weight, taps, start):
    tiles = block.shape[0] // 8
    middle, before, behind = half_rate(phase_views(block, taps // 2), taps, tiles)
    pairs = tiles // 2

    def run(values, weights, total):
        for s, w in enumerate(weights):
            for a in range(pairs):
                if values[a + s] is not None:
                    term = w * values[a + s]
                    total[a] = term if total[a] is None else total[a] + term
        return total

    even = [weight(t) for t in range(0, taps, 2)]
    odd = [weight(t) for t in range(1, taps, 2)]
    both = [e + o for e, o in zip(even, odd)] + even[len(odd) :]
    shared = run(middle, both, [start] * pairs)
    first = run([minus(b, m) for b, m in zip(before, middle)], even, list(shared))
    second = run([minus(b, m) for b, m in zip(behind, middle)], odd, list(shared))
    return jnp.concatenate([tile for pair in zip(first, second) for tile in pair], 0)


def phase_products(block, rows, taps, store):
    tiles = block.shape[0] // 8
    middle, before, behind = half_rate(phase_views(block, taps // 2), taps, tiles)
    pairs = tiles // 2
    even = [rows[16 * a : 16 * a + 8] for a in range(pairs)]
    odd = [rows[16 * a + 8 : 16 * a + 16] for a in range(pairs)]
    both = [e + o for e, o in zip(even, odd)]
    first = [minus(b, m) for b, m in zip(before, middle)]
    second = [minus(b, m) for b, m in zip(behind, middle)]

    def run(values, tiles_of, s):
        total = None
        for a in range(pairs):
            if values[a + s] is not None:
                term = tiles_of[a] * values[a + s]
                total = term if total is None else total + term
        return total

    for s in range((taps + 1) // 2):
        shared = run(middle, both, s)
        store(2 * s, jnp.sum(shared + run(first, even, s), 0, keepdims=True))
        if 2 * s + 1 < taps:
            store(2 * s + 1, jnp.sum(shared + run(second, odd, s), 0, keepdims=True))


def gate(pre_act):
    return 1.0 / (1.0 + jnp.exp(-pre_act))


def gate_grad(cotangent, pre_act, sig):
    return (cotangent * sig * (1.0 + pre_act * (1.0 - sig))).astype(BF16).astype(F32)


def norm_backward(context_ref, grad_ref, gain_ref, keep, out_ref, frames):
    for rows in chunks(frames):
        normed, inv_std = normalize(context_ref[rows, :])
        grad = grad_ref[rows, :] * gain_ref[0:1, :]
        centre = jnp.mean(grad, -1, keepdims=True)
        slope = jnp.mean(grad * normed, -1, keepdims=True)
        result = (grad - centre - normed * slope) * inv_std
        out_ref[rows, :] = jnp.where(keep[rows.start : rows.start + CHUNK, 0:1] > 0.0, result, 0.0).astype(BF16)


def wide(width):
    return [slice(start, start + WIDE) for start in range(0, width, WIDE)]


def forward_all(q_ref, k_ref, v_ref, prob_ref, context_ref, bias, keep, low):
    for index in range(q_ref.shape[1] // LANES):
        lanes = slice(index * LANES, (index + 1) * LANES)
        prob, context = attend(q_ref[:, lanes], k_ref[:, lanes], v_ref[:, lanes], bias, keep, low)
        prob_ref[index] = prob
        context_ref[:, lanes] = context


def normalize_all(context_ref, gain_ref, keep, in_ref, offset, frames):
    for rows in chunks(frames):
        normed, _ = normalize(context_ref[rows, :])
        normed = jnp.where(keep[rows.start : rows.start + CHUNK, 0:1] > 0.0, normed, 0.0)
        in_ref[pl.ds(offset + rows.start, CHUNK), :] = (
            (normed * gain_ref[0:1, :]).astype(BF16).astype(F32)
        )


def mask_kernel(taps, seg_ref, bias_ref, keep_ref, mask_ref, pad_ref):
    frames = bias_ref.shape[0]
    own, _, prev_last, next_first = block_ids(seg_ref, frames)
    ids = jnp.where((own == prev_last) | (own == next_first), -5.0, own)
    ids_row = jnp.broadcast_to(ids, (frames, frames))
    ids_col = jnp.transpose(ids_row)
    bias_ref[...] = jnp.where(ids_row == ids_col, 0.0, NEG)
    keep_ref[...] = jnp.where(ids_col >= 0.0, 1.0, 0.0)
    pad_ref[...] = jnp.full(pad_ref.shape, -9.0, F32)
    pad_ref[PAD : PAD + frames, :] = ids_col
    ids_pad = pad_ref[...]
    at, view = None, None
    for turn, start, tap in shifts(frames, taps):
        if turn != at:
            at, view = turn, turned(ids_pad, turn)
        mask_ref[tap * frames : (tap + 1) * frames, :] = jnp.where(
            view[start : start + frames] == ids_col, 1.0, 0.0
        )


def own_kernel(
    qkv_ref, cot_ref, gain_row, kernel_ref, bias_row, same_ref, keep_ref, mask_ref,
    out_ref, grad_ref, prob_ref, context_ref, sums_ref, gain_ref, bias_ref,
    pad_ref, view_ref,
):
    frames, width = cot_ref.shape
    taps = kernel_ref.shape[0]
    clear_edges(pad_ref, frames)
    clear_edges(grad_ref, frames)
    low = pair_masks(frames)
    gain_ref[...] = gain_row[...].reshape(1, width)
    bias_ref[...] = bias_row[...].reshape(1, width)
    bias, keep = same_ref[...], keep_ref[...]
    forward_all(qkv_ref.at[0], qkv_ref.at[1], qkv_ref.at[2], prob_ref, context_ref, bias, keep, low)
    normalize_all(context_ref, gain_ref, keep, pad_ref, PAD, frames)

    @pl.loop(0, width // LANES)
    def _(index):
        lanes = lanes_of(index)

        def keep_view(tap, term):
            view_ref[tap] = term

        pre_act = masked_conv(
            pad_ref, mask_ref, lambda t: kernel_ref[t : t + 1, lanes], taps,
            jnp.broadcast_to(bias_ref[0:1, lanes], (frames, LANES)), lanes, keep_view,
        )
        sig = gate(pre_act)
        out_ref[:, lanes] = (pre_act * sig * keep_ref[...]).astype(BF16)
        grad_pre = gate_grad(cot_ref[:, lanes].astype(F32) * keep_ref[...], pre_act, sig)
        grad_ref[PAD : PAD + frames, lanes] = grad_pre
        sums_ref[taps : taps + 1, lanes] = jnp.sum(grad_pre, 0, keepdims=True)
        for tap in range(taps):
            sums_ref[tap : tap + 1, lanes] = jnp.sum(grad_pre * view_ref[tap], 0, keepdims=True)


def own_conv_back(pad_ref, mask_ref, kernel_ref, back_ref, first, tiles):
    frames = back_ref.shape[0]
    taps = kernel_ref.shape[0]

    @pl.loop(first, first + tiles)
    def _(index):
        lanes = lanes_of(index)
        back_ref[:, lanes_of(index)] = masked_conv(
            pad_ref, mask_ref, lambda t: kernel_ref[taps - 1 - t : taps - t, lanes], taps,
            jnp.zeros((frames, LANES), F32), lanes,
        )


def own_half_kernel(pad_ref, mask_ref, kernel_ref, back_ref):
    own_conv_back(pad_ref, mask_ref, kernel_ref, back_ref, 0, back_ref.shape[1] // LANES)


def own_grad_kernel(
    pad_ref, context_ref, mask_ref, keep_ref, gain_ref, kernel_ref, half_ref, grad_ref, back_ref
):
    frames, width = context_ref.shape
    half = half_ref.shape[1]
    back_ref[:, :half] = half_ref[...]
    own_conv_back(pad_ref, mask_ref, kernel_ref, back_ref, half // LANES, (width - half) // LANES)
    norm_backward(context_ref, back_ref, gain_ref, keep_ref[...], grad_ref, frames)


def cross_forward_kernel(
    qkv_ref, other_ref, seg_ref, gain_ref, kernel_ref, bias_ref,
    out_ref, got_ref, prob_ref, context_ref, slope_ref, in_ref,
):
    frames, width = qkv_ref.shape[1:]
    taps = kernel_ref.shape[0]
    tiles = width // LANES
    first, length = crossing(seg_ref, frames)
    pick = gather_matrix(first, length, frames)
    shape = (frames, frames)
    bias = jnp.where(frame_of(shape, 1) < length, 0.0, NEG)
    keep = jnp.where(frame_of(shape, 0) < length, 1.0, 0.0)
    low = pair_masks(frames)
    for which in range(3):
        for cols in wide(width):
            both = jnp.concatenate([qkv_ref[which, :, cols], other_ref[which, :, cols]], 0)
            got_ref[which, :, cols] = dot(pick, both, NN).astype(BF16)
    forward_all(*(got_ref.at[i] for i in range(3)), prob_ref, context_ref, bias, keep, low)
    normalize_all(context_ref, gain_ref, keep, in_ref, 0, frames)

    @pl.loop(0, tiles)
    def _(index):
        lanes = lanes_of(index)
        start = jnp.broadcast_to(bias_ref[0:1, lanes], (8, LANES))
        pre_act = phase_conv(in_ref[:, lanes], lambda t: kernel_ref[t : t + 1, lanes], taps, start)
        sig = gate(pre_act)
        slope_ref[:, lanes] = sig * (1.0 + pre_act * (1.0 - sig))
        out_ref[:, lanes] = (pre_act * sig).astype(BF16)


def cross_place_kernel(out_ref, add_ref, seg_ref, own_ref, next_ref):
    frames, width = out_ref.shape
    place = scatter_matrix(*crossing(seg_ref, frames), frames)
    for cols in wide(width):
        placed = dot(place, out_ref[:, cols], NN).astype(BF16)
        own_ref[:, cols] = placed[:frames] + add_ref[:, cols]
        next_ref[:, cols] = placed[frames:]


def cross_sums_kernel(
    cot_ref, cotn_ref, seg_ref, slope_ref, in_ref, part_ref,
    grad_ref, mine_ref, other_ref,
    sums_ref,
):
    frames, width = cot_ref.shape
    taps = part_ref.shape[0] - 1
    first, length = crossing(seg_ref, frames)
    pick = gather_matrix(first, length, frames)
    for cols in wide(width):
        cotangent = dot(pick, jnp.concatenate([cot_ref[:, cols], cotn_ref[:, cols]], 0), NN)
        grad_ref[:, cols] = (cotangent * slope_ref[:, cols]).astype(BF16).astype(F32)

    @pl.loop(0, width // LANES)
    def _(index):
        lanes = lanes_of(index)

        def store(row, value):
            sums_ref[row : row + 1, lanes] = part_ref[row : row + 1, lanes] + value

        grad_pre = grad_ref[:, lanes]
        store(taps, jnp.sum(grad_pre, 0, keepdims=True))
        phase_products(
            grad_pre, in_ref[:, lanes], taps, lambda shift, value: store(taps - 1 - shift, value)
        )

    half = width // 2
    mine = lax.rem(lax.axis_index("seq"), 2)
    mine_ref[...] = sums_ref[:, pl.ds(pl.multiple_of(mine * half, LANES), half)].astype(BF16)
    other_ref[...] = sums_ref[:, pl.ds(pl.multiple_of((1 - mine) * half, LANES), half)].astype(BF16)


def cross_back_kernel(group, tiles, qkv_ref, prob_ref, context_ref, seg_ref, *refs):
    frames, width = context_ref.shape
    first, length = crossing(seg_ref, frames)
    place = scatter_matrix(first, length, frames)
    if group == 0:
        gain_ref, kernel_ref, pre_ref, own_ref, next_ref, grad_ref, result_ref, back_ref = refs
        taps = kernel_ref.shape[0]

        @pl.loop(0, width // LANES)
        def _(index):
            lanes = lanes_of(index)
            back_ref[:, lanes] = phase_conv(
                pre_ref[:, lanes], lambda t: kernel_ref[taps - 1 - t : taps - t, lanes], taps, None
            )

        keep = jnp.where(frame_of((frames, frames), 0) < length, 1.0, 0.0)
        norm_backward(context_ref, back_ref, gain_ref, keep, grad_ref, frames)
    else:
        grad_ref, own_ref, next_ref, result_ref = refs

    def store(which, pair, result):
        result_ref[which, :, lanes_at(pair)] = result

    got = [qkv_ref.at[i] for i in range(3)]
    back_all(*got, prob_ref, context_ref, grad_ref, group * tiles, tiles, store)
    for which in range(3):
        placed = dot(place, result_ref[which], NN).astype(BF16)
        own_ref[which] = placed[:frames]
        next_ref[which] = placed[frames:]


def own_back_kernel(qkv_ref, prob_ref, context_ref, grad_ref, out_ref):
    def store(which, pair, result):
        out_ref[which, :, lanes_at(pair)] = result

    back_all(
        qkv_ref.at[0], qkv_ref.at[1], qkv_ref.at[2], prob_ref, context_ref, grad_ref,
        0, context_ref.shape[1] // LANES, store,
    )


def merge_kernel(grads_ref, out_both_ref, out_came_ref, *refs):
    parts, outs = refs[:-4], refs[-4:]
    outs[3][...] = out_both_ref[...] + out_came_ref[...]
    start = 0
    for cross_ref, came_ref in zip(parts[::2], parts[1::2]):
        cols = slice(start, start + came_ref.shape[2])
        for which in range(3):
            outs[which][:, cols] = grads_ref[which, :, cols] + cross_ref[which] + came_ref[which]
        start = cols.stop


def finish_kernel(scale, mine_ref, came_ref, weight_ref, norm_ref, gain_ref, kernel_ref, bias_ref):
    taps, width = kernel_ref.shape
    even = lax.rem(lax.axis_index("seq"), 2) == 0
    mine, came = mine_ref[...].astype(F32) * scale, came_ref[...].astype(F32) * scale
    total = jnp.concatenate([jnp.where(even, mine, came), jnp.where(even, came, mine)], 1)
    kernel_ref[...] = total[:taps]
    bias_ref[...] = total[taps : taps + 1].reshape(width)
    gain = jnp.sum(total[:taps] * weight_ref[...], 0, keepdims=True) / norm_ref[...]
    gain_ref[...] = gain.reshape(width)


def call(kernel, outs, scratch, flops, *args, limit=24):
    size = sum(a.size * a.dtype.itemsize for a in args) + sum(o.size * o.dtype.itemsize for o in outs)
    return pl.pallas_call(
        kernel,
        out_shape=outs,
        in_specs=[VMEM] * len(args),
        out_specs=[VMEM] * len(outs),
        scratch_shapes=scratch,
        compiler_params=pltpu.CompilerParams(vmem_limit_bytes=limit * 1024 * 1024),
        cost_estimate=pl.CostEstimate(flops=flops, bytes_accessed=size, transcendentals=0),
    )(*args)


def after(value, *others):
    return lax.optimization_barrier((value,) + others)[0]


def sum_steps():
    steps = {"seq": [], "dp": []}
    for axis, distances in steps.items():
        step = 1
        while step < lax.axis_size(axis):
            distances.append((axis, step))
            step *= 2
    core, x, *rest = steps["seq"]
    return [core, x] + rest[::-1] + steps["dp"]


def exchange(sent, axis, step):
    return lax.ppermute(sent, axis, [(i, i ^ step) for i in range(lax.axis_size(axis))])


def added(sent, came):
    return (sent.astype(F32) + came.astype(F32)).astype(BF16)


def per_device(queries, keys, values, segment_ids, norm_gain, conv_kernel, conv_bias, cotangent):
    frames, width = queries.shape[1:]
    cot = cotangent[0]
    taps = conv_kernel.shape[0]
    tiles = width // LANES
    count = lax.axis_size("seq")
    to_left = [(i + 1, i) for i in range(count - 1)]
    to_right = [(i, i + 1) for i in range(count - 1)]
    qkv = jnp.concatenate([queries[0], keys[0], values[0]], 0)
    qkv_next = lax.ppermute(qkv, "seq", to_left).reshape(3, frames, width)
    qkv = qkv.reshape(3, frames, width)
    cot_next = lax.ppermute(cot, "seq", to_left)

    def sds(shape, dtype):
        return jax.ShapeDtypeStruct(shape, dtype)

    rows16 = sds((frames, width), BF16)
    rows32 = sds((frames, width), F32)
    three = sds((3, frames, width), BF16)
    probs = sds((tiles, frames, 2 * frames), BF16)
    half_sums = sds((taps + 1, width // 2), BF16)
    row = sds((1, width), F32)
    square = sds((frames, frames), F32)
    padded = pltpu.VMEM((frames + 2 * PAD, width), F32)
    plain = pltpu.VMEM((frames, width), F32)

    same, keep, masks = call(
        functools.partial(mask_kernel, taps),
        [square, square, sds((taps * frames, LANES), F32)],
        [pltpu.VMEM((frames + 2 * PAD, LANES), F32)],
        10**10,
        segment_ids,
    )
    out_own, pre_own, prob_own, context_own, sums_own, gain, bias = call(
        own_kernel,
        [rows16, sds((frames + 2 * PAD, width), F32), probs, rows16, sds((taps + 1, width), F32), row, row],
        [padded, pltpu.VMEM((taps, frames, LANES), F32)],
        10**10,
        qkv, cot, norm_gain, conv_kernel, conv_bias, same, keep, masks,
    )
    (half_own,) = call(
        own_half_kernel,
        [sds((frames, width // 2), F32)],
        [],
        2 * 10**9,
        pre_own, masks, conv_kernel,
    )
    out_cross, got, prob_cross, context_cross, slope_cross, in_cross = call(
        cross_forward_kernel,
        [rows16, three, probs, rows16, rows32, rows32],
        [],
        4 * 10**9,
        after(qkv, half_own), qkv_next, segment_ids, gain, conv_kernel, bias,
    )
    grad_pre, mine, other = call(
        cross_sums_kernel,
        [rows32, half_sums, half_sums],
        [pltpu.VMEM((taps + 1, width), F32)],
        3 * 10**9,
        cot, cot_next, segment_ids, slope_cross, in_cross, sums_own,
    )
    steps = sum_steps()
    came = exchange(other, *steps[0])
    out_both, out_next = call(
        cross_place_kernel, [rows16, rows16], [], 10**9, after(out_cross, mine), out_own, segment_ids,
    )
    sent = added(mine, after(came, out_next))
    came = exchange(sent, *steps[1])
    out_came = lax.ppermute(after(out_next, sent), "seq", to_right)
    per_group = tiles // GROUPS
    piece = sds((3, frames, per_group * LANES), BF16)
    parts = []
    grad_pre = after(grad_pre, sent)
    for group in range(GROUPS):
        if group == 1:
            sent = added(sent, after(came, out_came))
            came = exchange(sent, *steps[3])
        extra = [gain, conv_kernel, grad_pre] if group == 0 else [after(grad_cross, sent)]
        own_part, next_part, *rest = call(
            functools.partial(cross_back_kernel, group, per_group),
            [piece, piece] + [rows16] * (group == 0),
            [pltpu.VMEM(piece.shape, BF16)] + [plain] * (group == 0),
            2 * 10**9 + 3 * 10**9 * (group == 0),
            got, prob_cross, context_cross, segment_ids, *extra,
        )
        if group == 0:
            (grad_cross,) = rest
            sent = added(sent, after(came, own_part))
            came = exchange(sent, *steps[2])
        parts += [own_part, lax.ppermute(after(next_part, sent), "seq", to_right)]
    (grad_own,) = call(
        own_grad_kernel,
        [rows16],
        [plain],
        3 * 10**9,
        after(pre_own, sent), context_own, masks, keep, gain, conv_kernel, half_own,
    )
    for step in steps[GROUPS + 2 :]:
        sent = added(sent, after(came, grad_own))
        came = exchange(sent, *step)
    (grads_own,) = call(
        own_back_kernel,
        [three],
        [],
        4 * 10**9,
        qkv, prob_own, context_own, after(grad_own, sent),
    )
    sent = added(sent, after(came, grads_own))
    came = exchange(sent, *steps[0])
    query_grad, key_grad, value_grad, conv_out = call(
        merge_kernel, [rows16] * 4, [], 10**9, grads_own, out_both, out_came, *parts,
    )
    scale = (lax.axis_size("dp") * count * frames) ** (-0.5)
    gain_grad, kernel_grad, bias_grad = call(
        functools.partial(finish_kernel, scale),
        [sds((width,), F32), sds(conv_kernel.shape, F32), sds((width,), F32)],
        [],
        10**6,
        sent, came, conv_kernel, gain,
    )
    return (
        conv_out[None],
        query_grad[None],
        key_grad[None],
        value_grad[None],
        gain_grad,
        kernel_grad,
        bias_grad,
    )


def solution(mesh):
    rows = P("dp", "seq", None)
    return jax.shard_map(
        per_device,
        mesh=mesh,
        in_specs=(rows, rows, rows, P("dp", None), P(), P(), P(), rows),
        out_specs=(rows, rows, rows, rows, P(), P(), P()),
        check_vma=False,
    )
```

```python
import functools

import jax
import jax.numpy as jnp
from jax import lax
from jax.experimental import pallas as pl
from jax.experimental.pallas import tpu as pltpu
from jax.sharding import PartitionSpec as P

HEAD_DIM = 64
EPS = 1e-05
NEG = -1e30
LANES = 128
PAD = 16
GROUPS = 2
WIDE = 512
BATCH = 6
VMEM = pl.BlockSpec(memory_space=pltpu.VMEM)
F32 = jnp.float32
BF16 = jnp.bfloat16


def dot(a, b, dims):
    return lax.dot_general(a, b, (dims, ((), ())), preferred_element_type=F32)


NN = ((1,), (0,))
NT = ((1,), (1,))
TN = ((0,), (0,))


def lanes_of(index):
    return pl.ds(pl.multiple_of(index * LANES, LANES), LANES)


def block_ids(seg_ref, frames):
    me = lax.axis_index("seq")
    count = seg_ref.shape[1] // frames
    own = seg_ref[0:1, pl.ds(pl.multiple_of(me * frames, frames), frames)].astype(F32)
    before = jnp.maximum(me - 1, 0)
    after = jnp.minimum(me + 1, count - 1)
    prev = seg_ref[0:1, pl.ds(pl.multiple_of(before * frames, frames), frames)].astype(F32)
    following = seg_ref[0:1, pl.ds(pl.multiple_of(after * frames, frames), frames)].astype(F32)
    prev_last = jnp.where(me > 0, prev[:, frames - 1 :], -1.0)
    following = jnp.where(me < count - 1, following, -1.0)
    return own, following, prev_last, following[:, 0:1]


def crossing(seg_ref, frames):
    own, following, _, edge = block_ids(seg_ref, frames)
    left = jnp.sum(jnp.where((own == edge) & (edge >= 0.0), 1.0, 0.0), 1, keepdims=True)
    right = jnp.sum(jnp.where(following == edge, 1.0, 0.0), 1, keepdims=True)
    length = jnp.where(left > 0.0, left + right, 0.0)
    return frames - left, length


def iota(shape, axis):
    return lax.broadcasted_iota(jnp.int32, shape, axis).astype(F32)


def frame_of(shape, axis):
    place = lax.broadcasted_iota(jnp.int32, shape, axis)
    tiles = shape[axis] // 8
    return (lax.rem(place, 8) * tiles + lax.div(place, 8)).astype(F32)


def gather_matrix(first, length, frames):
    shape = (frames, 2 * frames)
    row = frame_of(shape, 0)
    return jnp.where((iota(shape, 1) == row + first) & (row < length), 1.0, 0.0).astype(BF16)


def scatter_matrix(first, length, frames):
    shape = (2 * frames, frames)
    col = frame_of(shape, 1)
    return jnp.where((iota(shape, 0) == col + first) & (col < length), 1.0, 0.0).astype(BF16)


def pair_masks(rows):
    low = lax.broadcasted_iota(jnp.int32, (rows, LANES), 1) < HEAD_DIM
    return low


def stack_pair(pair, low):
    zero = jnp.zeros_like(pair)
    return jnp.concatenate([jnp.where(low, pair, zero), jnp.where(low, zero, pair)], 0)


def attend(query, key, value, bias, keep, low):
    frames = query.shape[0]
    logits = dot(query * jnp.asarray(HEAD_DIM**-0.5, BF16), stack_pair(key, low), NT)
    halves = []
    for half in range(2):
        part = logits[:, half * frames : (half + 1) * frames] + bias
        top = jnp.max(part, 1, keepdims=True)
        power = jnp.exp(part - top)
        total = jnp.sum(power, 1, keepdims=True)
        halves.append((power * (1.0 / total)).astype(BF16))
    prob = jnp.concatenate(halves, 1)
    context = dot(prob, stack_pair(value, low), NN)
    return prob, (context * keep).astype(BF16)


def attend_back(query, key, value, prob, context, grad, pairs, store):
    frames = context(0).shape[0]
    low = pair_masks(frames)
    scale = HEAD_DIM**-0.5
    grad_probs = [dot(grad(p), stack_pair(value(p), low), NT) for p in pairs]
    deltas = []
    for p in pairs:
        product = grad(p).astype(F32) * context(p).astype(F32)
        zero = jnp.zeros_like(product)
        deltas.append(
            (
                jnp.sum(jnp.where(low, product, zero), 1, keepdims=True),
                jnp.sum(jnp.where(low, zero, product), 1, keepdims=True),
            )
        )
    grad_logits = []
    for p, grad_prob, delta in zip(pairs, grad_probs, deltas):
        both = prob(p)
        halves = []
        for half in range(2):
            cols = slice(half * frames, (half + 1) * frames)
            halves.append(
                (both[:, cols].astype(F32) * (grad_prob[:, cols] - delta[half]) * scale).astype(BF16)
            )
        grad_logits.append(halves)
    for p, halves in zip(pairs, grad_logits):
        store(0, p, dot(jnp.concatenate(halves, 1), stack_pair(key(p), low), NN).astype(BF16))
    for p, halves in zip(pairs, grad_logits):
        store(1, p, dot(jnp.concatenate(halves, 0), stack_pair(query(p), low), TN).astype(BF16))
    for p in pairs:
        both = prob(p)
        rows = jnp.concatenate([both[:, :frames], both[:, frames:]], 0)
        store(2, p, dot(rows, stack_pair(grad(p), low), TN).astype(BF16))


def lanes_at(index):
    return slice(index * LANES, (index + 1) * LANES)


def back_all(q_ref, k_ref, v_ref, prob_ref, context_ref, grad_ref, first, pairs, store):
    for start in range(0, pairs, BATCH):
        attend_back(
            lambda p: q_ref[:, lanes_at(first + p)],
            lambda p: k_ref[:, lanes_at(first + p)],
            lambda p: v_ref[:, lanes_at(first + p)],
            lambda p: prob_ref[first + p],
            lambda p: context_ref[:, lanes_at(first + p)],
            lambda p: grad_ref[:, lanes_at(first + p)],
            range(start, min(start + BATCH, pairs)),
            store,
        )


def normalize(context):
    context = context.astype(F32)
    centred = context - jnp.mean(context, -1, keepdims=True)
    inv_std = lax.rsqrt(jnp.mean(centred * centred, -1, keepdims=True) + EPS)
    return centred * inv_std, inv_std


CHUNK = 32


def chunks(frames):
    return [pl.ds(start, CHUNK) for start in range(0, frames, CHUNK)]


def clear_edges(pad_ref, frames):
    zero = jnp.zeros((PAD, pad_ref.shape[1]), F32)
    pad_ref[0:PAD, :] = zero
    pad_ref[PAD + frames : 2 * PAD + frames, :] = zero


def shifts(frames, taps):
    base = PAD - taps // 2
    for turn in range(8):
        for start in range(0, 2 * PAD + 1, 8):
            tap = start + turn - base
            if 0 <= tap < taps:
                yield turn, start, tap


def turned(block, turn):
    rows = block.shape[0]
    return block if turn == 0 else pltpu.roll(block, rows - turn, 0)


def masked_conv(pad_ref, mask_ref, weight, taps, start, lanes, keep_view=None):
    frames = start.shape[0]
    block = pad_ref[:, lanes]
    total = start
    at, view = None, None
    for turn, row, tap in shifts(frames, taps):
        if turn != at:
            at, view = turn, turned(block, turn)
        term = view[row : row + frames] * mask_ref[tap * frames : (tap + 1) * frames, :]
        if keep_view is not None:
            keep_view(tap, term)
        total = total + weight(tap) * term
    return total


def phase_views(block, half_taps):
    tiles = block.shape[0] // 8
    row = lax.broadcasted_iota(jnp.int32, (8, LANES), 0)
    views = {}
    for j in range(tiles):
        tile = block[8 * j : 8 * j + 8]
        views[j] = tile
        if j - tiles >= -half_taps:
            views[j - tiles] = jnp.where(row >= 1, pltpu.roll(tile, 1, 0), 0.0)
        if j < half_taps:
            views[j + tiles] = jnp.where(row < 7, pltpu.roll(tile, 7, 0), 0.0)
    return views


def half_rate(views, taps, tiles):
    reach = tiles // 2 + (taps + 1) // 2 - 1
    low = -(taps // 2)
    middle = [views[low + 2 * n + 1] if low + 2 * n + 1 in views else None for n in range(reach)]
    before = [views[low + 2 * n] for n in range(reach)]
    after_ = [views.get(low + 2 * n + 2) for n in range(reach)]
    return middle, before, after_


def minus(a, b):
    if b is None:
        return a
    return -b if a is None else a - b


def phase_conv(block, weight, taps, start):
    tiles = block.shape[0] // 8
    middle, before, behind = half_rate(phase_views(block, taps // 2), taps, tiles)
    pairs = tiles // 2

    def run(values, weights, total):
        for s, w in enumerate(weights):
            for a in range(pairs):
                if values[a + s] is not None:
                    term = w * values[a + s]
                    total[a] = term if total[a] is None else total[a] + term
        return total

    even = [weight(t) for t in range(0, taps, 2)]
    odd = [weight(t) for t in range(1, taps, 2)]
    both = [e + o for e, o in zip(even, odd)] + even[len(odd) :]
    shared = run(middle, both, [start] * pairs)
    first = run([minus(b, m) for b, m in zip(before, middle)], even, list(shared))
    second = run([minus(b, m) for b, m in zip(behind, middle)], odd, list(shared))
    return jnp.concatenate([tile for pair in zip(first, second) for tile in pair], 0)


def phase_products(block, rows, taps, store):
    tiles = block.shape[0] // 8
    middle, before, behind = half_rate(phase_views(block, taps // 2), taps, tiles)
    pairs = tiles // 2
    even = [rows[16 * a : 16 * a + 8] for a in range(pairs)]
    odd = [rows[16 * a + 8 : 16 * a + 16] for a in range(pairs)]
    both = [e + o for e, o in zip(even, odd)]
    first = [minus(b, m) for b, m in zip(before, middle)]
    second = [minus(b, m) for b, m in zip(behind, middle)]

    def run(values, tiles_of, s):
        total = None
        for a in range(pairs):
            if values[a + s] is not None:
                term = tiles_of[a] * values[a + s]
                total = term if total is None else total + term
        return total

    for s in range((taps + 1) // 2):
        shared = run(middle, both, s)
        store(2 * s, jnp.sum(shared + run(first, even, s), 0, keepdims=True))
        if 2 * s + 1 < taps:
            store(2 * s + 1, jnp.sum(shared + run(second, odd, s), 0, keepdims=True))


def gate(pre_act):
    return 1.0 / (1.0 + jnp.exp(-pre_act))


def gate_grad(cotangent, pre_act, sig):
    return (cotangent * sig * (1.0 + pre_act * (1.0 - sig))).astype(BF16).astype(F32)


def norm_backward(context_ref, grad_ref, gain_ref, keep, out_ref, frames):
    for rows in chunks(frames):
        normed, inv_std = normalize(context_ref[rows, :])
        grad = grad_ref[rows, :] * gain_ref[0:1, :]
        centre = jnp.mean(grad, -1, keepdims=True)
        slope = jnp.mean(grad * normed, -1, keepdims=True)
        result = (grad - centre - normed * slope) * inv_std
        out_ref[rows, :] = jnp.where(keep[rows.start : rows.start + CHUNK, 0:1] > 0.0, result, 0.0).astype(BF16)


def wide(width):
    return [slice(start, start + WIDE) for start in range(0, width, WIDE)]


def forward_all(q_ref, k_ref, v_ref, prob_ref, context_ref, bias, keep, low):
    for index in range(q_ref.shape[1] // LANES):
        lanes = slice(index * LANES, (index + 1) * LANES)
        prob, context = attend(q_ref[:, lanes], k_ref[:, lanes], v_ref[:, lanes], bias, keep, low)
        prob_ref[index] = prob
        context_ref[:, lanes] = context


def normalize_all(context_ref, gain_ref, keep, in_ref, offset, frames):
    for rows in chunks(frames):
        normed, _ = normalize(context_ref[rows, :])
        normed = jnp.where(keep[rows.start : rows.start + CHUNK, 0:1] > 0.0, normed, 0.0)
        in_ref[pl.ds(offset + rows.start, CHUNK), :] = (
            (normed * gain_ref[0:1, :]).astype(BF16).astype(F32)
        )


def mask_kernel(taps, seg_ref, bias_ref, keep_ref, mask_ref, pad_ref):
    frames = bias_ref.shape[0]
    own, _, prev_last, next_first = block_ids(seg_ref, frames)
    ids = jnp.where((own == prev_last) | (own == next_first), -5.0, own)
    ids_row = jnp.broadcast_to(ids, (frames, frames))
    ids_col = jnp.transpose(ids_row)
    bias_ref[...] = jnp.where(ids_row == ids_col, 0.0, NEG)
    keep_ref[...] = jnp.where(ids_col >= 0.0, 1.0, 0.0)
    pad_ref[...] = jnp.full(pad_ref.shape, -9.0, F32)
    pad_ref[PAD : PAD + frames, :] = ids_col
    ids_pad = pad_ref[...]
    at, view = None, None
    for turn, start, tap in shifts(frames, taps):
        if turn != at:
            at, view = turn, turned(ids_pad, turn)
        mask_ref[tap * frames : (tap + 1) * frames, :] = jnp.where(
            view[start : start + frames] == ids_col, 1.0, 0.0
        )


def own_kernel(
    qkv_ref, cot_ref, gain_row, kernel_ref, bias_row, same_ref, keep_ref, mask_ref,
    out_ref, grad_ref, prob_ref, context_ref, sums_ref, gain_ref, bias_ref,
    pad_ref, view_ref,
):
    frames, width = cot_ref.shape
    taps = kernel_ref.shape[0]
    clear_edges(pad_ref, frames)
    clear_edges(grad_ref, frames)
    low = pair_masks(frames)
    gain_ref[...] = gain_row[...].reshape(1, width)
    bias_ref[...] = bias_row[...].reshape(1, width)
    bias, keep = same_ref[...], keep_ref[...]
    forward_all(qkv_ref.at[0], qkv_ref.at[1], qkv_ref.at[2], prob_ref, context_ref, bias, keep, low)
    normalize_all(context_ref, gain_ref, keep, pad_ref, PAD, frames)

    @pl.loop(0, width // LANES)
    def _(index):
        lanes = lanes_of(index)

        def keep_view(tap, term):
            view_ref[tap] = term

        pre_act = masked_conv(
            pad_ref, mask_ref, lambda t: kernel_ref[t : t + 1, lanes], taps,
            jnp.broadcast_to(bias_ref[0:1, lanes], (frames, LANES)), lanes, keep_view,
        )
        sig = gate(pre_act)
        out_ref[:, lanes] = (pre_act * sig * keep_ref[...]).astype(BF16)
        grad_pre = gate_grad(cot_ref[:, lanes].astype(F32) * keep_ref[...], pre_act, sig)
        grad_ref[PAD : PAD + frames, lanes] = grad_pre
        sums_ref[taps : taps + 1, lanes] = jnp.sum(grad_pre, 0, keepdims=True)
        for tap in range(taps):
            sums_ref[tap : tap + 1, lanes] = jnp.sum(grad_pre * view_ref[tap], 0, keepdims=True)


def own_conv_back(pad_ref, mask_ref, kernel_ref, back_ref, first, tiles):
    frames = back_ref.shape[0]
    taps = kernel_ref.shape[0]

    @pl.loop(first, first + tiles)
    def _(index):
        lanes = lanes_of(index)
        back_ref[:, lanes_of(index)] = masked_conv(
            pad_ref, mask_ref, lambda t: kernel_ref[taps - 1 - t : taps - t, lanes], taps,
            jnp.zeros((frames, LANES), F32), lanes,
        )


def own_half_kernel(pad_ref, mask_ref, kernel_ref, back_ref):
    own_conv_back(pad_ref, mask_ref, kernel_ref, back_ref, 0, back_ref.shape[1] // LANES)


def own_grad_kernel(
    pad_ref, context_ref, mask_ref, keep_ref, gain_ref, kernel_ref, half_ref, grad_ref, back_ref
):
    frames, width = context_ref.shape
    half = half_ref.shape[1]
    back_ref[:, :half] = half_ref[...]
    own_conv_back(pad_ref, mask_ref, kernel_ref, back_ref, half // LANES, (width - half) // LANES)
    norm_backward(context_ref, back_ref, gain_ref, keep_ref[...], grad_ref, frames)


def cross_forward_kernel(
    qkv_ref, other_ref, seg_ref, gain_ref, kernel_ref, bias_ref,
    out_ref, got_ref, prob_ref, context_ref, slope_ref, in_ref,
):
    frames, width = qkv_ref.shape[1:]
    taps = kernel_ref.shape[0]
    tiles = width // LANES
    first, length = crossing(seg_ref, frames)
    pick = gather_matrix(first, length, frames)
    shape = (frames, frames)
    bias = jnp.where(frame_of(shape, 1) < length, 0.0, NEG)
    keep = jnp.where(frame_of(shape, 0) < length, 1.0, 0.0)
    low = pair_masks(frames)
    for which in range(3):
        for cols in wide(width):
            both = jnp.concatenate([qkv_ref[which, :, cols], other_ref[which, :, cols]], 0)
            got_ref[which, :, cols] = dot(pick, both, NN).astype(BF16)
    forward_all(*(got_ref.at[i] for i in range(3)), prob_ref, context_ref, bias, keep, low)
    normalize_all(context_ref, gain_ref, keep, in_ref, 0, frames)

    @pl.loop(0, tiles)
    def _(index):
        lanes = lanes_of(index)
        start = jnp.broadcast_to(bias_ref[0:1, lanes], (8, LANES))
        pre_act = phase_conv(in_ref[:, lanes], lambda t: kernel_ref[t : t + 1, lanes], taps, start)
        sig = gate(pre_act)
        slope_ref[:, lanes] = sig * (1.0 + pre_act * (1.0 - sig))
        out_ref[:, lanes] = (pre_act * sig).astype(BF16)


def cross_place_kernel(out_ref, add_ref, seg_ref, own_ref, next_ref):
    frames, width = out_ref.shape
    place = scatter_matrix(*crossing(seg_ref, frames), frames)
    for cols in wide(width):
        placed = dot(place, out_ref[:, cols], NN).astype(BF16)
        own_ref[:, cols] = placed[:frames] + add_ref[:, cols]
        next_ref[:, cols] = placed[frames:]


def cross_sums_kernel(
    cot_ref, cotn_ref, seg_ref, slope_ref, in_ref, part_ref,
    grad_ref, mine_ref, other_ref,
    sums_ref,
):
    frames, width = cot_ref.shape
    taps = part_ref.shape[0] - 1
    first, length = crossing(seg_ref, frames)
    pick = gather_matrix(first, length, frames)
    for cols in wide(width):
        cotangent = dot(pick, jnp.concatenate([cot_ref[:, cols], cotn_ref[:, cols]], 0), NN)
        grad_ref[:, cols] = (cotangent * slope_ref[:, cols]).astype(BF16).astype(F32)

    @pl.loop(0, width // LANES)
    def _(index):
        lanes = lanes_of(index)

        def store(row, value):
            sums_ref[row : row + 1, lanes] = part_ref[row : row + 1, lanes] + value

        grad_pre = grad_ref[:, lanes]
        store(taps, jnp.sum(grad_pre, 0, keepdims=True))
        phase_products(
            grad_pre, in_ref[:, lanes], taps, lambda shift, value: store(taps - 1 - shift, value)
        )

    half = width // 2
    mine = lax.rem(lax.axis_index("seq"), 2)
    mine_ref[...] = sums_ref[:, pl.ds(pl.multiple_of(mine * half, LANES), half)].astype(BF16)
    other_ref[...] = sums_ref[:, pl.ds(pl.multiple_of((1 - mine) * half, LANES), half)].astype(BF16)


def cross_back_kernel(group, tiles, qkv_ref, prob_ref, context_ref, seg_ref, *refs):
    frames, width = context_ref.shape
    first, length = crossing(seg_ref, frames)
    place = scatter_matrix(first, length, frames)
    if group == 0:
        gain_ref, kernel_ref, pre_ref, own_ref, next_ref, grad_ref, result_ref, back_ref = refs
        taps = kernel_ref.shape[0]

        @pl.loop(0, width // LANES)
        def _(index):
            lanes = lanes_of(index)
            back_ref[:, lanes] = phase_conv(
                pre_ref[:, lanes], lambda t: kernel_ref[taps - 1 - t : taps - t, lanes], taps, None
            )

        keep = jnp.where(frame_of((frames, frames), 0) < length, 1.0, 0.0)
        norm_backward(context_ref, back_ref, gain_ref, keep, grad_ref, frames)
    else:
        grad_ref, own_ref, next_ref, result_ref = refs

    def store(which, pair, result):
        result_ref[which, :, lanes_at(pair)] = result

    got = [qkv_ref.at[i] for i in range(3)]
    back_all(*got, prob_ref, context_ref, grad_ref, group * tiles, tiles, store)
    for which in range(3):
        placed = dot(place, result_ref[which], NN).astype(BF16)
        own_ref[which] = placed[:frames]
        next_ref[which] = placed[frames:]


def own_back_kernel(qkv_ref, prob_ref, context_ref, grad_ref, out_ref):
    def store(which, pair, result):
        out_ref[which, :, lanes_at(pair)] = result

    back_all(
        qkv_ref.at[0], qkv_ref.at[1], qkv_ref.at[2], prob_ref, context_ref, grad_ref,
        0, context_ref.shape[1] // LANES, store,
    )


def merge_kernel(grads_ref, out_both_ref, out_came_ref, *refs):
    parts, outs = refs[:-4], refs[-4:]
    outs[3][...] = out_both_ref[...] + out_came_ref[...]
    start = 0
    for cross_ref, came_ref in zip(parts[::2], parts[1::2]):
        cols = slice(start, start + came_ref.shape[2])
        for which in range(3):
            outs[which][:, cols] = grads_ref[which, :, cols] + cross_ref[which] + came_ref[which]
        start = cols.stop


def finish_kernel(scale, mine_ref, came_ref, weight_ref, norm_ref, gain_ref, kernel_ref, bias_ref):
    taps, width = kernel_ref.shape
    even = lax.rem(lax.axis_index("seq"), 2) == 0
    mine, came = mine_ref[...].astype(F32) * scale, came_ref[...].astype(F32) * scale
    total = jnp.concatenate([jnp.where(even, mine, came), jnp.where(even, came, mine)], 1)
    kernel_ref[...] = total[:taps]
    bias_ref[...] = total[taps : taps + 1].reshape(width)
    gain = jnp.sum(total[:taps] * weight_ref[...], 0, keepdims=True) / norm_ref[...]
    gain_ref[...] = gain.reshape(width)


def last_kernel(scale, *refs):
    ins, outs = refs[:-7], refs[-7:]
    finish_kernel(scale, *ins[:4], *outs[:3])
    merge_kernel(*ins[4:], *outs[3:])


def call(kernel, outs, scratch, flops, *args, limit=24):
    size = sum(a.size * a.dtype.itemsize for a in args) + sum(o.size * o.dtype.itemsize for o in outs)
    return pl.pallas_call(
        kernel,
        out_shape=outs,
        in_specs=[VMEM] * len(args),
        out_specs=[VMEM] * len(outs),
        scratch_shapes=scratch,
        compiler_params=pltpu.CompilerParams(vmem_limit_bytes=limit * 1024 * 1024),
        cost_estimate=pl.CostEstimate(flops=flops, bytes_accessed=size, transcendentals=0),
    )(*args)


def after(value, *others):
    return lax.optimization_barrier((value,) + others)[0]


def sum_steps():
    steps = {"seq": [], "dp": []}
    for axis, distances in steps.items():
        step = 1
        while step < lax.axis_size(axis):
            distances.append((axis, step))
            step *= 2
    core, x, *rest = steps["seq"]
    return [core, x] + rest[::-1] + steps["dp"]


def exchange(sent, axis, step):
    return lax.ppermute(sent, axis, [(i, i ^ step) for i in range(lax.axis_size(axis))])


def added(sent, came):
    return (sent.astype(F32) + came.astype(F32)).astype(BF16)


def per_device(queries, keys, values, segment_ids, norm_gain, conv_kernel, conv_bias, cotangent):
    frames, width = queries.shape[1:]
    cot = cotangent[0]
    taps = conv_kernel.shape[0]
    tiles = width // LANES
    count = lax.axis_size("seq")
    to_left = [(i + 1, i) for i in range(count - 1)]
    to_right = [(i, i + 1) for i in range(count - 1)]
    qkv = jnp.concatenate([queries[0], keys[0], values[0]], 0)
    qkv_next = lax.ppermute(qkv, "seq", to_left).reshape(3, frames, width)
    qkv = qkv.reshape(3, frames, width)
    cot_next = lax.ppermute(cot, "seq", to_left)

    def sds(shape, dtype):
        return jax.ShapeDtypeStruct(shape, dtype)

    rows16 = sds((frames, width), BF16)
    rows32 = sds((frames, width), F32)
    three = sds((3, frames, width), BF16)
    probs = sds((tiles, frames, 2 * frames), BF16)
    half_sums = sds((taps + 1, width // 2), BF16)
    row = sds((1, width), F32)
    square = sds((frames, frames), F32)
    padded = pltpu.VMEM((frames + 2 * PAD, width), F32)
    plain = pltpu.VMEM((frames, width), F32)

    same, keep, masks = call(
        functools.partial(mask_kernel, taps),
        [square, square, sds((taps * frames, LANES), F32)],
        [pltpu.VMEM((frames + 2 * PAD, LANES), F32)],
        10**10,
        segment_ids,
    )
    out_own, pre_own, prob_own, context_own, sums_own, gain, bias = call(
        own_kernel,
        [rows16, sds((frames + 2 * PAD, width), F32), probs, rows16, sds((taps + 1, width), F32), row, row],
        [padded, pltpu.VMEM((taps, frames, LANES), F32)],
        10**10,
        qkv, cot, norm_gain, conv_kernel, conv_bias, same, keep, masks,
    )
    (half_own,) = call(
        own_half_kernel,
        [sds((frames, width // 2), F32)],
        [],
        2 * 10**9,
        pre_own, masks, conv_kernel,
    )
    out_cross, got, prob_cross, context_cross, slope_cross, in_cross = call(
        cross_forward_kernel,
        [rows16, three, probs, rows16, rows32, rows32],
        [],
        4 * 10**9,
        after(qkv, half_own), qkv_next, segment_ids, gain, conv_kernel, bias,
    )
    grad_pre, mine, other = call(
        cross_sums_kernel,
        [rows32, half_sums, half_sums],
        [pltpu.VMEM((taps + 1, width), F32)],
        3 * 10**9,
        cot, cot_next, segment_ids, slope_cross, in_cross, sums_own,
    )
    steps = sum_steps()
    came = exchange(other, *steps[0])
    out_both, out_next = call(
        cross_place_kernel, [rows16, rows16], [], 10**9, after(out_cross, mine), out_own, segment_ids,
    )
    sent = added(mine, after(came, out_next))
    came = exchange(sent, *steps[1])
    out_came = lax.ppermute(after(out_next, sent), "seq", to_right)
    per_group = tiles // GROUPS
    piece = sds((3, frames, per_group * LANES), BF16)
    parts = []
    grad_pre = after(grad_pre, sent)
    for group in range(GROUPS):
        if group == 1:
            sent = added(sent, after(came, out_came))
            came = exchange(sent, *steps[3])
        extra = [gain, conv_kernel, grad_pre] if group == 0 else [after(grad_cross, sent)]
        own_part, next_part, *rest = call(
            functools.partial(cross_back_kernel, group, per_group),
            [piece, piece] + [rows16] * (group == 0),
            [pltpu.VMEM(piece.shape, BF16)] + [plain] * (group == 0),
            2 * 10**9 + 3 * 10**9 * (group == 0),
            got, prob_cross, context_cross, segment_ids, *extra,
        )
        if group == 0:
            (grad_cross,) = rest
            sent = added(sent, after(came, own_part))
            came = exchange(sent, *steps[2])
        parts += [own_part, lax.ppermute(after(next_part, sent), "seq", to_right)]
    for step in steps[GROUPS + 2 :]:
        sent = added(sent, came)
        came = exchange(sent, *step)
    (grad_own,) = call(
        own_grad_kernel,
        [rows16],
        [plain],
        3 * 10**9,
        after(pre_own, sent), context_own, masks, keep, gain, conv_kernel, half_own,
    )
    (grads_own,) = call(
        own_back_kernel,
        [three],
        [],
        4 * 10**9,
        qkv, prob_own, context_own, after(grad_own, sent),
    )
    sent = added(sent, after(came, grads_own))
    came = exchange(sent, *steps[0])
    scale = (lax.axis_size("dp") * count * frames) ** (-0.5)
    gain_grad, kernel_grad, bias_grad, query_grad, key_grad, value_grad, conv_out = call(
        functools.partial(last_kernel, scale),
        [sds((width,), F32), sds(conv_kernel.shape, F32), sds((width,), F32)] + [rows16] * 4,
        [],
        10**9,
        sent, came, conv_kernel, gain, grads_own, out_both, out_came, *parts,
    )
    return (
        conv_out[None],
        query_grad[None],
        key_grad[None],
        value_grad[None],
        gain_grad,
        kernel_grad,
        bias_grad,
    )


def solution(mesh):
    rows = P("dp", "seq", None)
    return jax.shard_map(
        per_device,
        mesh=mesh,
        in_specs=(rows, rows, rows, P("dp", None), P(), P(), P(), rows),
        out_specs=(rows, rows, rows, rows, P(), P(), P()),
        check_vma=False,
    )
```
